1024 devices in a mesh: lon: 128 (over x, z), lat: 8 (over y, core).
Axes of the slice: x: 4, y: 4, z: 32, core: 2. Of those that a mesh axis runs over, the one named last changes fastest.
Arguments:
- velocity_u: float32 [48, 1024, 1024], P(None, 'lon', 'lat'), may hold values from -4 to 4
- velocity_v: float32 [48, 1024, 1024], P(None, 'lon', 'lat'), may hold values from -4 to 4
- buoyancy: float32 [48, 1024, 1024], P(None, 'lon', 'lat'), may hold values from -6 to 6
- wind_x: float32 [1024, 1024], P('lon', 'lat'), may hold values from -0.02 to 0.02
- wind_y: float32 [1024, 1024], P('lon', 'lat'), may hold values from -0.02 to 0.02
- free_surface: float32 [1024, 1024], P('lon', 'lat'), may hold values from -0.8 to 0.8
- land_sea: int32 [1024, 1024], P('lon', 'lat'), may hold values 0 or 1
- bottom_level: int32 [1024, 1024], P('lon', 'lat'), may hold values from 4 to 48
Outputs:
- new_u: float32 [48, 1024, 1024], P(None, 'lon', 'lat')
- new_v: float32 [48, 1024, 1024], P(None, 'lon', 'lat')
- new_surface: float32 [1024, 1024], P('lon', 'lat')
The draws below stay inside these ranges and needn't reach their ends.
All inputs are finite; a program needn't handle non-finite values. No bound on the sum of `land_sea` on one device may be relied on, other than what follows from the above.
Results may differ from the reference program's by a relative error of at most 0.00002.
Values sent between devices are 32-bit elements; how exact they have to be, the bound alone decides.
No kernel may reach another device: no remote copies, remote signals or barrier semaphores. Data moves between devices by JAX's collectives and lax.ppermute only.
A program may use at most 32 MiB of HBM per device.

```python
import jax
import jax.numpy as jnp

NZ = 48
SUBSTEPS = 30
NX = 1024
NY = 1024


def set_ends(values, key, least, largest):
    index_at = [jax.random.randint(jax.random.fold_in(key, axis), (), 0, length) for axis, length in enumerate(values.shape)]
    longest = values.shape.index(max(values.shape))
    beside = index_at[:longest] + [(index_at[longest] + 1) % values.shape[longest]] + index_at[longest + 1:]
    return values.at[tuple(index_at)].set(least).at[tuple(beside)].set(largest)


def shard_levels(key, dims, cuts, least, top_value):
    loudness = 1.0
    for dim, blocks in cuts:
        steps = jax.random.uniform(jax.random.fold_in(jax.random.fold_in(key, 6), dim), (blocks,), jnp.float32, least / len(cuts), top_value / len(cuts))
        loudness = loudness * jnp.repeat(jnp.exp(steps), dims[dim] // blocks).reshape((-1,) + (1,) * (len(dims) - 1 - dim))
    return loudness


def normal_values(rng, extent, deviation, bound, pieces=(), kind=jnp.bfloat16):
    gain = shard_levels(rng, extent, pieces, -0.22, 0.18) if pieces else 1.0
    array = jax.random.normal(rng, extent, jnp.float32) * deviation * gain
    return jnp.minimum(jnp.maximum(array, -bound), bound).astype(kind)


def setup_inputs(seed: int = 0) -> dict:
    splits = jax.random.split(jax.random.key(seed), 9)
    velocity_u = normal_values(splits[0], (NZ, NX, NY), 0.5, 4.0, ((1, 128), (2, 8)), jnp.float32)
    velocity_v = normal_values(splits[1], (NZ, NX, NY), 0.5, 4.0, ((1, 128), (2, 8)), jnp.float32)
    buoyancy = normal_values(splits[2], (NZ, NX, NY), 1.0, 6.0, ((1, 128), (2, 8)), jnp.float32)
    wind_x = normal_values(splits[3], (NX, NY), 0.003, 0.02, ((0, 128), (1, 8)), jnp.float32)
    wind_y = normal_values(splits[4], (NX, NY), 0.003, 0.02, ((0, 128), (1, 8)), jnp.float32)
    free_surface = normal_values(splits[5], (NX, NY), 0.1, 0.8, ((0, 128), (1, 8)), jnp.float32)
    land_sea = set_ends((jax.random.randint(splits[6], (NX, NY), 0, 4) < 3).astype(jnp.int32), jax.random.fold_in(splits[6], 1), 0, 1)
    bottom_level = set_ends(jax.random.randint(splits[7], (NX, NY), 4, NZ + 1), jax.random.fold_in(splits[7], 1), 4, NZ).astype(jnp.int32)
    return dict(velocity_u=velocity_u, velocity_v=velocity_v, buoyancy=buoyancy, wind_x=wind_x, wind_y=wind_y, free_surface=free_surface, land_sea=land_sea, bottom_level=bottom_level)


def ahead(a, axis):
    size = a.shape[axis]
    lead = jax.lax.slice_in_dim(a, 1, size, axis=axis)
    blank = jnp.zeros_like(jax.lax.slice_in_dim(a, 0, 1, axis=axis))
    return jnp.concatenate([lead, blank], axis)


def behind(a, axis):
    size = a.shape[axis]
    lead = jax.lax.slice_in_dim(a, 0, size - 1, axis=axis)
    blank = jnp.zeros_like(jax.lax.slice_in_dim(a, 0, 1, axis=axis))
    return jnp.concatenate([blank, lead], axis)


def reference(velocity_u, velocity_v, buoyancy, wind_x, wind_y, free_surface, land_sea, bottom_level):
    levels = jnp.arange(NZ, dtype=jnp.float32)
    thick = ((1.0 + 2.0 * levels / NZ) / NZ)[:, None, None]
    water = (land_sea * bottom_level).astype(jnp.float32)
    wet = (levels[:, None, None] < water[None]).astype(jnp.float32)

    def east(a):
        return jnp.roll(a, -1, axis=a.ndim - 2)

    def west(a):
        return jnp.roll(a, 1, axis=a.ndim - 2)

    def north(a):
        return ahead(a, a.ndim - 1)

    def south(a):
        return behind(a, a.ndim - 1)

    face_u = wet * east(wet)
    face_v = wet * north(wet)
    pressure = jnp.cumsum(thick * buoyancy, axis=0)
    top = (levels == 0.0).astype(jnp.float32)[:, None, None]
    lap_u = east(velocity_u) + west(velocity_u) + north(velocity_u) + south(velocity_u) - 4.0 * velocity_u
    lap_v = east(velocity_v) + west(velocity_v) + north(velocity_v) + south(velocity_v) - 4.0 * velocity_v
    force_u = 0.05 * lap_u - (east(pressure) - pressure) + top * (wind_x[None] / thick[0])
    force_v = 0.05 * lap_v - (north(pressure) - pressure) + top * (wind_y[None] / thick[0])
    star_u = (velocity_u + 6.0 * force_u) * face_u
    star_v = (velocity_v + 6.0 * force_v) * face_v
    depth_u = jnp.sum(thick * face_u, axis=0)
    depth_v = jnp.sum(thick * face_v, axis=0)
    forcing_u = jnp.sum(thick * face_u * force_u, axis=0)
    forcing_v = jnp.sum(thick * face_v * force_v, axis=0)
    flow_u = jnp.sum(thick * face_u * velocity_u, axis=0)
    flow_v = jnp.sum(thick * face_v * velocity_v, axis=0)
    rows = jnp.arange(NY, dtype=jnp.float32)[None, :]
    coriolis_u = 0.4 * (2.0 * (rows + 0.5) / NY - 1.0)
    coriolis_v = 0.4 * (2.0 * (rows + 1.0) / NY - 1.0)
    wet_two = land_sea.astype(jnp.float32)
    open_u = face_u[0]
    open_v = face_v[0]
    tau = 6.0 / SUBSTEPS
    surface = free_surface
    total_u = jnp.zeros_like(flow_u)
    total_v = jnp.zeros_like(flow_v)
    for step in range(SUBSTEPS):
        spread = flow_u - west(flow_u) + flow_v - south(flow_v)
        surface_new = surface - tau * wet_two * spread
        vbar = 0.25 * (flow_v + east(flow_v) + south(flow_v) + east(south(flow_v)))
        ubar = 0.25 * (flow_u + west(flow_u) + north(flow_u) + west(north(flow_u)))
        next_u = open_u * (flow_u + tau * (forcing_u - depth_u * (east(surface_new) - surface_new) + coriolis_u * vbar))
        next_v = open_v * (flow_v + tau * (forcing_v - depth_v * (north(surface_new) - surface_new) - coriolis_v * ubar))
        surface, flow_u, flow_v = surface_new, next_u, next_v
        total_u = total_u + next_u
        total_v = total_v + next_v
    mean_u = total_u / SUBSTEPS
    mean_v = total_v / SUBSTEPS
    new_u = star_u + face_u * ((mean_u - jnp.sum(thick * star_u, axis=0)) / jnp.maximum(depth_u, 0.25))[None]
    new_v = star_v + face_v * ((mean_v - jnp.sum(thick * star_v, axis=0)) / jnp.maximum(depth_v, 0.25))[None]
    return new_u, new_v, surface
```

```python
import jax
import jax.numpy as jnp
import numpy as np
from jax import lax
from jax.experimental import pallas as pl
from jax.experimental.pallas import tpu as pltpu
from jax.sharding import PartitionSpec as P

SUBSTEPS = 30
LANES = 128
COLS = 8
RIM = 32
REACH = 4
FIELDS = 9 * COLS
STEP = 6.0
VMEM_BYTES = 32 * 1024 * 1024


def thickness(levels):
    index = np.arange(levels, dtype=np.float32)
    return (np.float32(1.0) + np.float32(2.0) * index / np.float32(levels)) / np.float32(levels)


def lane_index():
    return lax.broadcasted_iota(jnp.int32, (COLS, LANES), 1)


def col_index():
    return lax.broadcasted_iota(jnp.int32, (COLS, LANES), 0)


def is_even(axis):
    return lax.rem(lax.axis_index(axis), 2) == 0


def level(k):
    return pl.ds(COLS * k, COLS)


def north(own, rim):
    last = lane_index() == LANES - 1
    a, b = pltpu.roll(own, LANES - 1, 1), pltpu.roll(rim, LANES - 1, 1)
    return jnp.where(last, b, a), jnp.where(last, a, b)


def south(own, rim):
    first = lane_index() == 0
    a, b = pltpu.roll(own, 1, 1), pltpu.roll(rim, 1, 1)
    return jnp.where(first, b, a), jnp.where(first, a, b)


def pair_rims(first, second):
    lane = lax.broadcasted_iota(jnp.int32, first.shape, 1)
    return jnp.where((lane >= RIM) & (lane < LANES - RIM), pltpu.roll(second, LANES // 2, 1), first)


def pack_rows(u_ref, v_ref, b_ref, plane_refs, a_ref, z_ref):
    even = is_even("lat")
    lane = lane_index()
    slot = lane // RIM

    def strips(parts, shifts):
        moved = [pltpu.roll(p, s, 1) if s else p for p, s in zip(parts, shifts)]
        return jnp.where(
            slot < 2, jnp.where(slot == 0, moved[0], moved[1]), jnp.where(slot == 2, moved[2], moved[3])
        )

    for k in range(u_ref.shape[0] // COLS):
        u, v, b = u_ref[level(k), :], v_ref[level(k), :], b_ref[level(k), :]
        parts = (u, v, b, plane_refs[k][...] if k < len(plane_refs) else b)
        upper = strips(parts, (32, 64, 96, 0))
        lower = strips(parts, (0, 32, 64, 96))
        a_ref[level(k), :] = jnp.where(even, upper, lower)
        z_ref[level(k), :] = jnp.where(even, lower, upper)


def pack_rows_kernel(u_ref, v_ref, b_ref, water_ref, eta_ref, wx_ref, wy_ref, a_ref, z_ref):
    pack_rows(u_ref, v_ref, b_ref, (water_ref, eta_ref, wx_ref, wy_ref), a_ref, z_ref)


def pack_cols_kernel(u_ref, v_ref, b_ref, water_ref, a_in, z_in, a_ref, z_ref, hu_ref, hv_ref, hb_ref, hp_ref):
    even = is_even("lat")
    lane = lane_index()
    upper = lane < LANES // 2
    levels = u_ref.shape[0] // COLS
    for k in range(levels):
        a, z = a_in[level(k), :], z_in[level(k), :]
        n, s = jnp.where(even, a, z), jnp.where(even, z, a)
        hu_ref[level(k), :] = jnp.where(upper, n, pltpu.roll(s, 96, 1))
        hv_ref[level(k), :] = jnp.where(upper, pltpu.roll(n, 96, 1), pltpu.roll(s, 64, 1))
        hb_ref[level(k), :] = jnp.where(upper, pltpu.roll(n, 64, 1), pltpu.roll(s, 32, 1))
        if k < 4:
            hp_ref[level(k), :] = jnp.where(upper, pltpu.roll(n, 32, 1), s)
    even_col = is_even("lon")

    def edge(ref, rows, col):
        return ref[pl.ds(col, rows, stride=COLS), :]

    def store(col, out_ref):
        out_ref[pl.ds(0, levels), :] = edge(u_ref, levels, col)
        out_ref[pl.ds(levels, levels), :] = edge(v_ref, levels, col)
        out_ref[pl.ds(2 * levels, levels), :] = edge(b_ref, levels, col)
        out_ref[pl.ds(3 * levels, levels), :] = pair_rims(edge(hu_ref, levels, col), edge(hv_ref, levels, col))
        out_ref[pl.ds(4 * levels, levels), :] = edge(hb_ref, levels, col)
        out_ref[pl.ds(5 * levels, 1), :] = water_ref[pl.ds(col, 1), :]
        out_ref[pl.ds(5 * levels + 1, 1), :] = hp_ref[pl.ds(col, 1), :]
        out_ref[pl.ds(5 * levels + 2, 6), :] = jnp.zeros((6, LANES), jnp.float32)

    @pl.when(even_col)
    def _():
        store(COLS - 1, a_ref)
        store(0, z_ref)

    @pl.when(jnp.logical_not(even_col))
    def _():
        store(0, a_ref)
        store(COLS - 1, z_ref)


def levels_kernel(
    u_ref, v_ref, b_ref, hu_ref, hv_ref, hb_ref, hp_ref, water_ref, eta_ref, wx_ref, wy_ref, a_in, z_in,
    x_ref, su_ref, sv_ref, east_ref, west_ref,
):
    levels = u_ref.shape[0] // COLS
    thick = thickness(levels)
    even = is_even("lon")
    a, z = a_in[...], z_in[...]
    east_ref[pl.ds(0, a.shape[0]), :] = jnp.where(even, a, z)
    west_ref[pl.ds(0, a.shape[0]), :] = jnp.where(even, z, a)
    for ref in (east_ref, west_ref):
        ref[pl.ds(a.shape[0], levels), :] = pltpu.roll(ref[pl.ds(3 * levels, levels), :], LANES // 2, 1)
    own_at = {"u": 0, "v": levels, "b": 2 * levels, "w": 5 * levels}
    rim_at = {"u": 3 * levels, "v": a.shape[0], "b": 4 * levels, "w": 5 * levels + 1}
    col = col_index()
    top_col, bottom_col = col == COLS - 1, col == 0

    def row(ref, at):
        return jnp.broadcast_to(ref[pl.ds(at, 1), :], (COLS, LANES))

    def east(pair, name, k):
        own, rim = pair
        return (
            jnp.where(top_col, row(east_ref, own_at[name] + k), pltpu.roll(own, COLS - 1, 0)),
            jnp.where(top_col, row(east_ref, rim_at[name] + k), pltpu.roll(rim, COLS - 1, 0)),
        )

    def west(pair, name, k):
        own, rim = pair
        return (
            jnp.where(bottom_col, row(west_ref, own_at[name] + k), pltpu.roll(own, 1, 0)),
            jnp.where(bottom_col, row(west_ref, rim_at[name] + k), pltpu.roll(rim, 1, 0)),
        )

    water = (water_ref[...], hp_ref[pl.ds(0, COLS), :])
    eta = (eta_ref[...], hp_ref[pl.ds(COLS, COLS), :])
    wx = (wx_ref[...], hp_ref[pl.ds(2 * COLS, COLS), :])
    wy = (wy_ref[...], hp_ref[pl.ds(3 * COLS, COLS), :])
    open_u = [jnp.minimum(w, e) for w, e in zip(water, east(water, "w", 0))]
    open_v = [jnp.minimum(w, n) for w, n in zip(water, north(*water))]
    zero = jnp.zeros((COLS, LANES), jnp.float32)
    slope_u, slope_v = [zero, zero], [zero, zero]
    forcing_u, forcing_v = [zero, zero], [zero, zero]
    flow_u, flow_v = [zero, zero], [zero, zero]
    for k in range(levels):
        dz = float(thick[k])
        u = (u_ref[level(k), :], hu_ref[level(k), :])
        v = (v_ref[level(k), :], hv_ref[level(k), :])
        b = (b_ref[level(k), :], hb_ref[level(k), :])
        around_u = list(zip(east(u, "u", k), west(u, "u", k), north(*u), south(*u)))
        around_v = list(zip(east(v, "v", k), west(v, "v", k), north(*v), south(*v)))
        b_east, b_north = east(b, "b", k), north(*b)
        for t in range(2):
            slope_u[t] = slope_u[t] + dz * (b_east[t] - b[t])
            slope_v[t] = slope_v[t] + dz * (b_north[t] - b[t])
            force_u = 0.05 * (sum(around_u[t][1:], around_u[t][0]) - 4.0 * u[t]) - slope_u[t]
            force_v = 0.05 * (sum(around_v[t][1:], around_v[t][0]) - 4.0 * v[t]) - slope_v[t]
            if k == 0:
                force_u = force_u + wx[t] / dz
                force_v = force_v + wy[t] / dz
            wet_u, wet_v = open_u[t] > float(k), open_v[t] > float(k)
            force_u, vel_u = jnp.where(wet_u, force_u, 0.0), jnp.where(wet_u, u[t], 0.0)
            force_v, vel_v = jnp.where(wet_v, force_v, 0.0), jnp.where(wet_v, v[t], 0.0)
            forcing_u[t] = forcing_u[t] + dz * force_u
            forcing_v[t] = forcing_v[t] + dz * force_v
            flow_u[t] = flow_u[t] + dz * vel_u
            flow_v[t] = flow_v[t] + dz * vel_v
            if t == 0:
                su_ref[level(k), :] = vel_u + STEP * force_u
                sv_ref[level(k), :] = vel_v + STEP * force_v
    fields = (forcing_u, forcing_v, flow_u, flow_v, water, eta)
    for i, f in enumerate(fields):
        x_ref[level(i), :] = f[0]
    for i in range(3):
        x_ref[level(6 + i), :] = pair_rims(fields[2 * i][1], fields[2 * i + 1][1])


def depth_of(count, levels):
    return (count + count * (count - 1.0) * (1.0 / levels)) * (1.0 / levels)


def substeps_kernel(
    y_ref, a_in, z_in, su_ref, sv_ref, out_u, out_v, out_eta,
    eta_ref, u_ref, v_ref, w_ref, fu_ref, fv_ref, du_ref, dv_ref, cu_ref, cv_ref, tw_ref, q_ref, t_ref,
):
    levels = su_ref.shape[0] // COLS
    tau = STEP / SUBSTEPS
    blocks = 2 * REACH + 1
    even = is_even("lon")
    lane = lane_index()

    def at(p, shift=0):
        return pl.ds(COLS * (p + 1) + shift, COLS)

    places = (
        ((z_in, 0), (a_in, 2)), ((z_in, 1), (a_in, 1)), ((z_in, 2), (a_in, 0)),
        ((y_ref, 2), (y_ref, 0)), ((y_ref, 1), (y_ref, 1)), ((y_ref, 0), (y_ref, 2)),
        ((a_in, 0), (z_in, 2)), ((a_in, 1), (z_in, 1)), ((a_in, 2), (z_in, 0)),
    )
    for p, (for_even, for_odd) in enumerate(places):
        def tile(i):
            first = for_even[0][pl.ds(for_even[1] * FIELDS + COLS * i, COLS), :]
            if p == REACH:
                return first
            return jnp.where(even, first, for_odd[0][pl.ds(for_odd[1] * FIELDS + COLS * i, COLS), :])

        targets = (fu_ref, fv_ref, u_ref, v_ref, w_ref, eta_ref)
        for i, ref in enumerate(targets):
            value = tile(i)
            ref[0, at(p), :] = tau * value if i < 2 else value
        for i in range(3):
            value = tile(6 + i)
            other = pltpu.roll(value, LANES // 2, 1)
            if i == 0:
                value, other = tau * value, tau * other
            targets[2 * i][1, at(p), :] = value
            targets[2 * i + 1][1, at(p), :] = other

    total_rows = LANES * lax.axis_size("lat")
    base = (lax.axis_index("lat") * LANES).astype(jnp.float32)
    own_row = lane.astype(jnp.float32) + base
    rim_row = jnp.where(lane < LANES // 2, lane + LANES, lane - LANES).astype(jnp.float32) + base
    spin = [
        [0.25 * tau * 0.4 * (2.0 * (r + half) * (1.0 / total_rows) - 1.0) for half in (0.5, 1.0)]
        for r in (own_row, rim_row)
    ]
    for p in range(blocks):
        water = [w_ref[t, at(p), :] for t in range(2)]
        water_north = north(*water)
        for t in range(2):
            open_u = jnp.minimum(water[t], w_ref[t, at(p, 1), :])
            open_v = jnp.minimum(water[t], water_north[t])
            du_ref[t, at(p), :] = tau * depth_of(open_u, levels)
            dv_ref[t, at(p), :] = tau * depth_of(open_v, levels)
            cu_ref[t, at(p), :] = jnp.where(open_u > 0.0, spin[t][0], 0.0)
            cv_ref[t, at(p), :] = jnp.where(open_v > 0.0, spin[t][1], 0.0)
            tw_ref[t, at(p), :] = jnp.where(water[t] > 0.0, tau, 0.0)

    flow_u, flow_v = u_ref[0, at(REACH), :], v_ref[0, at(REACH), :]
    zero = jnp.zeros((COLS, LANES), jnp.float32)

    def substep(first, last):
        def body(_, carry):
            total_u, total_v = carry
            for p in range(first, last):
                u = [u_ref[t, at(p), :] for t in range(2)]
                u_west = [u_ref[t, at(p, -1), :] for t in range(2)]
                v = [v_ref[t, at(p), :] for t in range(2)]
                v_south = south(*v)
                both = [u[t] + u_west[t] for t in range(2)]
                both_north = north(*both)
                for t in range(2):
                    spread = (u[t] - u_west[t]) + (v[t] - v_south[t])
                    eta_ref[t, at(p), :] = eta_ref[t, at(p), :] - tw_ref[t, at(p), :] * spread
                    q_ref[t, at(p), :] = v[t] + v_south[t]
                    t_ref[t, at(p), :] = both[t] + both_north[t]
            for p in range(first, last):
                eta = [eta_ref[t, at(p), :] for t in range(2)]
                eta_north = north(*eta)
                for t in range(2):
                    vbar = q_ref[t, at(p), :] + q_ref[t, at(p, 1), :]
                    rise_u = eta_ref[t, at(p, 1), :] - eta[t]
                    rise_v = eta_north[t] - eta[t]
                    next_u = (u_ref[t, at(p), :] + fu_ref[t, at(p), :]) + (
                        cu_ref[t, at(p), :] * vbar - du_ref[t, at(p), :] * rise_u
                    )
                    next_v = (v_ref[t, at(p), :] + fv_ref[t, at(p), :]) - (
                        cv_ref[t, at(p), :] * t_ref[t, at(p), :] + dv_ref[t, at(p), :] * rise_v
                    )
                    u_ref[t, at(p), :] = next_u
                    v_ref[t, at(p), :] = next_v
                    if p == REACH and t == 0:
                        total_u, total_v = total_u + next_u, total_v + next_v
            return total_u, total_v

        return body

    carry = (zero, zero)
    done = 0
    for ring in range(REACH):
        until = SUBSTEPS - COLS * (REACH - 1 - ring)
        carry = lax.fori_loop(0, until - done, substep(ring, blocks - ring), carry)
        done = until
    out_eta[...] = eta_ref[0, at(REACH), :]
    water = [w_ref[t, at(REACH), :] for t in range(2)]
    open_u = jnp.minimum(water[0], w_ref[0, at(REACH, 1), :])
    open_v = jnp.minimum(water[0], north(*water)[0])
    star_u = flow_u + (STEP / tau) * fu_ref[0, at(REACH), :]
    star_v = flow_v + (STEP / tau) * fv_ref[0, at(REACH), :]
    lift_u = (carry[0] / SUBSTEPS - star_u) / jnp.maximum(depth_of(open_u, levels), 0.25)
    lift_v = (carry[1] / SUBSTEPS - star_v) / jnp.maximum(depth_of(open_v, levels), 0.25)
    for k in range(levels):
        out_u[level(k), :] = su_ref[level(k), :] + jnp.where(open_u > float(k), lift_u, 0.0)
        out_v[level(k), :] = sv_ref[level(k), :] + jnp.where(open_v > float(k), lift_v, 0.0)


def call(kernel, shapes, scratch, *operands):
    return pl.pallas_call(
        kernel,
        out_shape=[jax.ShapeDtypeStruct(s, jnp.float32) for s in shapes],
        scratch_shapes=[pltpu.VMEM(s, jnp.float32) for s in scratch],
        compiler_params=pltpu.CompilerParams(vmem_limit_bytes=VMEM_BYTES),
    )(*operands)


def swap(x, axis, first, hop, wraps):
    count = lax.axis_size(axis)
    pairs = []
    for i in range(first, count, 2):
        j = i + hop
        if wraps or 0 <= j < count:
            pairs += [(i, j % count), (j % count, i)]
    return lax.ppermute(x, axis, pairs)


def local(velocity_u, velocity_v, buoyancy, wind_x, wind_y, free_surface, land_sea, bottom_level):
    levels = velocity_u.shape[0]
    flat = (levels * COLS, LANES)
    u, v, b = (a.reshape(flat) for a in (velocity_u, velocity_v, buoyancy))
    water = (land_sea * bottom_level).astype(jnp.float32)
    rows_a, rows_z = call(
        pack_rows_kernel, [flat, flat], [], u, v, b, water, free_surface, wind_x, wind_y
    )
    rows_a = swap(rows_a, "lat", 0, 1, False)
    rows_z = swap(rows_z, "lat", 1, 1, False)
    edge = (5 * levels + 8, LANES)
    cols_a, cols_z, hu, hv, hb, hp = call(
        pack_cols_kernel, [edge, edge, flat, flat, flat, (4 * COLS, LANES)], [], u, v, b, water, rows_a, rows_z
    )
    cols_a = swap(cols_a, "lon", 0, 1, True)
    cols_z = swap(cols_z, "lon", 1, 1, True)
    both = (edge[0] + levels, LANES)
    x, star_u, star_v = call(
        levels_kernel, [(FIELDS, LANES), flat, flat], [both, both],
        u, v, b, hu, hv, hb, hp, water, free_surface, wind_x, wind_y, cols_a, cols_z,
    )
    near_a = swap(x, "lon", 0, 1, True)
    near_z = swap(x, "lon", 1, 1, True)
    y = jnp.concatenate([near_a, x, near_z], 0)
    far_a = swap(y, "lon", 0, 3, True)
    far_z = swap(y, "lon", 1, 3, True)
    state = (2, (2 * REACH + 3) * COLS, LANES)
    new_u, new_v, surface = call(
        substeps_kernel, [flat, flat, (COLS, LANES)], [state] * 13, y, far_a, far_z, star_u, star_v
    )
    return new_u.reshape(velocity_u.shape), new_v.reshape(velocity_v.shape), surface


def solution(mesh):
    return jax.shard_map(
        local,
        mesh=mesh,
        in_specs=(P(None, "lon", "lat"),) * 3 + (P("lon", "lat"),) * 5,
        out_specs=(P(None, "lon", "lat"), P(None, "lon", "lat"), P("lon", "lat")),
        check_vma=False,
    )
```

```python
import jax
import jax.numpy as jnp
import numpy as np
from jax import lax
from jax.experimental import pallas as pl
from jax.experimental.pallas import tpu as pltpu
from jax.sharding import PartitionSpec as P

SUBSTEPS = 30
LANES = 128
COLS = 8
RIM = 32
SLOTS = 4
CHUNKS = 4
REACH = 4
FIELDS = 9 * COLS
STEP = 6.0
VMEM_BYTES = 32 * 1024 * 1024


def thickness(levels):
    index = np.arange(levels, dtype=np.float32)
    return (np.float32(1.0) + np.float32(2.0) * index / np.float32(levels)) / np.float32(levels)


def lane_index():
    return lax.broadcasted_iota(jnp.int32, (COLS, LANES), 1)


def col_index():
    return lax.broadcasted_iota(jnp.int32, (COLS, LANES), 0)


def is_even(axis):
    return lax.rem(lax.axis_index(axis), 2) == 0


def level(k):
    return pl.ds(COLS * k, COLS)


def north(own, rim):
    last = lane_index() == LANES - 1
    a, b = pltpu.roll(own, LANES - 1, 1), pltpu.roll(rim, LANES - 1, 1)
    return jnp.where(last, b, a), jnp.where(last, a, b)


def south(own, rim):
    first = lane_index() == 0
    a, b = pltpu.roll(own, 1, 1), pltpu.roll(rim, 1, 1)
    return jnp.where(first, b, a), jnp.where(first, a, b)


def pair_rims(first, second):
    lane = lax.broadcasted_iota(jnp.int32, first.shape, 1)
    return jnp.where((lane >= RIM) & (lane < LANES - RIM), pltpu.roll(second, LANES // 2, 1), first)


def strips(parts, shifts):
    slot = lane_index() // RIM
    moved = [pltpu.roll(p, s, 1) if s else p for p, s in zip(parts, shifts)]
    return jnp.where(
        slot < 2, jnp.where(slot == 0, moved[0], moved[1]), jnp.where(slot == 2, moved[2], moved[3])
    )


def pack_rows_kernel(
    u_in, v_in, b_in, land_in, bottom_in, eta_in, wx_in, wy_in,
    a_ref, z_ref, u_ref, v_ref, b_ref, plane_ref, land_ref, bottom_ref, sems, plane_sem,
):
    levels = u_in.shape[0] // COLS
    groups = levels // SLOTS
    chunks = sems.shape[0]
    fields = ((u_in, u_ref), (v_in, v_ref), (b_in, b_ref))
    part = u_in.shape[0] // chunks
    copies = [
        [
            pltpu.make_async_copy(src.at[pl.ds(c * part, part)], dst.at[pl.ds(c * part, part)], sems.at[c, f])
            for f, (src, dst) in enumerate(fields)
        ]
        for c in range(chunks)
    ]
    planes = [
        pltpu.make_async_copy(src, dst, plane_sem.at[i])
        for i, (src, dst) in enumerate(
            (
                (land_in, land_ref), (bottom_in, bottom_ref), (eta_in, plane_ref.at[level(1)]),
                (wx_in, plane_ref.at[level(2)]), (wy_in, plane_ref.at[level(3)]),
            )
        )
    ]
    for copy in sum(copies, []) + planes:
        copy.start()
    even = is_even("lat")

    def send(at, parts):
        upper, lower = strips(parts, (32, 64, 96, 0)), strips(parts, (0, 32, 64, 96))
        a_ref[level(at), :] = jnp.where(even, upper, lower)
        z_ref[level(at), :] = jnp.where(even, lower, upper)

    for c in range(chunks):
        for f, (_, ref) in enumerate(fields):
            copies[c][f].wait()
            for g in range(c * groups // chunks, (c + 1) * groups // chunks):
                send(f * groups + g, [ref[level(SLOTS * g + s), :] for s in range(SLOTS)])
    for copy in planes:
        copy.wait()
    plane_ref[level(0), :] = (land_ref[...] * bottom_ref[...]).astype(jnp.float32)
    send(3 * groups, [plane_ref[level(s), :] for s in range(SLOTS)])


def pack_cols_kernel(u_ref, v_ref, b_ref, plane_ref, z_in, a_in, a_ref, z_ref, hu_ref, hv_ref, hb_ref, hp_ref):
    even = is_even("lat")
    upper = lane_index() < LANES // 2
    levels = u_ref.shape[0] // COLS
    groups = levels // SLOTS

    def receive(at, s):
        a, z = a_in[level(at), :], z_in[level(at), :]
        n, o = jnp.where(even, a, z), jnp.where(even, z, a)
        to_first, to_last = (LANES - RIM * s) % LANES, (LANES - RIM - RIM * s) % LANES
        n = pltpu.roll(n, to_first, 1) if to_first else n
        o = pltpu.roll(o, to_last, 1) if to_last else o
        return jnp.where(upper, n, o)

    for f, ref in enumerate((hu_ref, hv_ref, hb_ref)):
        for k in range(levels):
            ref[level(k), :] = receive(f * groups + k // SLOTS, k % SLOTS)
    for s in range(SLOTS):
        hp_ref[level(s), :] = receive(3 * groups, s)
    even_col = is_even("lon")

    def edge(ref, rows, col):
        return ref[pl.ds(col, rows, stride=COLS), :]

    def store(col, out_ref):
        out_ref[pl.ds(0, levels), :] = edge(u_ref, levels, col)
        out_ref[pl.ds(levels, levels), :] = edge(v_ref, levels, col)
        out_ref[pl.ds(2 * levels, levels), :] = edge(b_ref, levels, col)
        out_ref[pl.ds(3 * levels, levels), :] = pair_rims(edge(hu_ref, levels, col), edge(hv_ref, levels, col))
        out_ref[pl.ds(4 * levels, levels), :] = edge(hb_ref, levels, col)
        out_ref[pl.ds(5 * levels, 1), :] = plane_ref[pl.ds(col, 1), :]
        out_ref[pl.ds(5 * levels + 1, 1), :] = hp_ref[pl.ds(col, 1), :]
        out_ref[pl.ds(5 * levels + 2, 6), :] = jnp.zeros((6, LANES), jnp.float32)

    @pl.when(even_col)
    def _():
        store(COLS - 1, a_ref)
        store(0, z_ref)

    @pl.when(jnp.logical_not(even_col))
    def _():
        store(0, a_ref)
        store(COLS - 1, z_ref)


def levels_kernel(
    u_ref, v_ref, b_ref, hu_ref, hv_ref, hb_ref, hp_ref, plane_ref, z_in, a_in,
    x_ref, su_ref, sv_ref, east_ref, west_ref,
):
    levels = u_ref.shape[0] // COLS
    thick = thickness(levels)
    even = is_even("lon")
    a, z = a_in[...], z_in[...]
    east_ref[pl.ds(0, a.shape[0]), :] = jnp.where(even, a, z)
    west_ref[pl.ds(0, a.shape[0]), :] = jnp.where(even, z, a)
    for ref in (east_ref, west_ref):
        ref[pl.ds(a.shape[0], levels), :] = pltpu.roll(ref[pl.ds(3 * levels, levels), :], LANES // 2, 1)
    own_at = {"u": 0, "v": levels, "b": 2 * levels, "w": 5 * levels}
    rim_at = {"u": 3 * levels, "v": a.shape[0], "b": 4 * levels, "w": 5 * levels + 1}
    col = col_index()
    top_col, bottom_col = col == COLS - 1, col == 0

    def row(ref, at):
        return jnp.broadcast_to(ref[pl.ds(at, 1), :], (COLS, LANES))

    def east(pair, name, k):
        own, rim = pair
        return (
            jnp.where(top_col, row(east_ref, own_at[name] + k), pltpu.roll(own, COLS - 1, 0)),
            jnp.where(top_col, row(east_ref, rim_at[name] + k), pltpu.roll(rim, COLS - 1, 0)),
        )

    def west(pair, name, k):
        own, rim = pair
        return (
            jnp.where(bottom_col, row(west_ref, own_at[name] + k), pltpu.roll(own, 1, 0)),
            jnp.where(bottom_col, row(west_ref, rim_at[name] + k), pltpu.roll(rim, 1, 0)),
        )

    water, eta, wx, wy = [(plane_ref[level(i), :], hp_ref[level(i), :]) for i in range(SLOTS)]
    open_u = [jnp.minimum(w, e) for w, e in zip(water, east(water, "w", 0))]
    open_v = [jnp.minimum(w, n) for w, n in zip(water, north(*water))]
    zero = jnp.zeros((COLS, LANES), jnp.float32)
    slope_u, slope_v = [zero, zero], [zero, zero]
    forcing_u, forcing_v = [zero, zero], [zero, zero]
    flow_u, flow_v = [zero, zero], [zero, zero]
    for k in range(levels):
        dz = float(thick[k])
        u = (u_ref[level(k), :], hu_ref[level(k), :])
        v = (v_ref[level(k), :], hv_ref[level(k), :])
        b = (b_ref[level(k), :], hb_ref[level(k), :])
        around_u = list(zip(east(u, "u", k), west(u, "u", k), north(*u), south(*u)))
        around_v = list(zip(east(v, "v", k), west(v, "v", k), north(*v), south(*v)))
        b_east, b_north = east(b, "b", k), north(*b)
        for t in range(2):
            slope_u[t] = slope_u[t] + dz * (b_east[t] - b[t])
            slope_v[t] = slope_v[t] + dz * (b_north[t] - b[t])
            force_u = 0.05 * (sum(around_u[t][1:], around_u[t][0]) - 4.0 * u[t]) - slope_u[t]
            force_v = 0.05 * (sum(around_v[t][1:], around_v[t][0]) - 4.0 * v[t]) - slope_v[t]
            if k == 0:
                force_u = force_u + wx[t] / dz
                force_v = force_v + wy[t] / dz
            wet_u, wet_v = open_u[t] > float(k), open_v[t] > float(k)
            force_u, vel_u = jnp.where(wet_u, force_u, 0.0), jnp.where(wet_u, u[t], 0.0)
            force_v, vel_v = jnp.where(wet_v, force_v, 0.0), jnp.where(wet_v, v[t], 0.0)
            forcing_u[t] = forcing_u[t] + dz * force_u
            forcing_v[t] = forcing_v[t] + dz * force_v
            flow_u[t] = flow_u[t] + dz * vel_u
            flow_v[t] = flow_v[t] + dz * vel_v
            if t == 0:
                su_ref[level(k), :] = vel_u + STEP * force_u
                sv_ref[level(k), :] = vel_v + STEP * force_v
    fields = (forcing_u, forcing_v, flow_u, flow_v, water, eta)
    for i, f in enumerate(fields):
        x_ref[level(i), :] = f[0]
    for i in range(3):
        x_ref[level(6 + i), :] = pair_rims(fields[2 * i][1], fields[2 * i + 1][1])


def depth_of(count, levels):
    return (count + count * (count - 1.0) * (1.0 / levels)) * (1.0 / levels)


def substeps_kernel(
    y_ref, a_in, z_in, su_ref, sv_ref, out_u, out_v, out_eta,
    eta_ref, u_ref, v_ref, w_ref, fu_ref, fv_ref, du_ref, dv_ref, cu_ref, cv_ref, tw_ref, q_ref, t_ref,
    eta_north_ref, u_north_ref, tw_north_ref,
):
    levels = su_ref.shape[0] // COLS
    tau = STEP / SUBSTEPS
    blocks = 2 * REACH + 1
    even = is_even("lon")
    lane = lane_index()

    def at(p, shift=0):
        return pl.ds(COLS * (p + 1) + shift, COLS)

    places = (
        ((z_in, 2), (a_in, 0)), ((z_in, 1), (a_in, 1)), ((z_in, 0), (a_in, 2)),
        ((y_ref, 0), (y_ref, 2)), ((y_ref, 1), (y_ref, 1)), ((y_ref, 2), (y_ref, 0)),
        ((a_in, 2), (z_in, 0)), ((a_in, 1), (z_in, 1)), ((a_in, 0), (z_in, 2)),
    )
    for p, (for_even, for_odd) in enumerate(places):
        def tile(i):
            first = for_even[0][pl.ds(for_even[1] * FIELDS + COLS * i, COLS), :]
            if p == REACH:
                return first
            return jnp.where(even, first, for_odd[0][pl.ds(for_odd[1] * FIELDS + COLS * i, COLS), :])

        targets = (fu_ref, fv_ref, u_ref, v_ref, w_ref, eta_ref)
        for i, ref in enumerate(targets):
            value = tile(i)
            ref[0, at(p), :] = tau * value if i < 2 else value
        for i in range(3):
            value = tile(6 + i)
            other = pltpu.roll(value, LANES // 2, 1)
            if i == 0:
                value, other = tau * value, tau * other
            targets[2 * i][1, at(p), :] = value
            targets[2 * i + 1][1, at(p), :] = other

    total_rows = LANES * lax.axis_size("lat")
    base = (lax.axis_index("lat") * LANES).astype(jnp.float32)
    own_row = lane.astype(jnp.float32) + base
    rim_row = jnp.where(lane < LANES // 2, lane + LANES, lane - LANES).astype(jnp.float32) + base
    spin = [
        [0.25 * tau * 0.4 * (2.0 * (r + half) * (1.0 / total_rows) - 1.0) for half in (0.5, 1.0)]
        for r in (own_row, rim_row)
    ]
    for p in range(blocks):
        water = [w_ref[t, at(p), :] for t in range(2)]
        water_north = north(*water)
        eta_north = north(eta_ref[0, at(p), :], eta_ref[1, at(p), :])
        for t in range(2):
            eta_north_ref[t, at(p), :] = eta_north[t]
            tw_north_ref[t, at(p), :] = jnp.where(water_north[t] > 0.0, tau, 0.0)
            open_u = jnp.minimum(water[t], w_ref[t, at(p, 1), :])
            open_v = jnp.minimum(water[t], water_north[t])
            du_ref[t, at(p), :] = tau * depth_of(open_u, levels)
            dv_ref[t, at(p), :] = tau * depth_of(open_v, levels)
            cu_ref[t, at(p), :] = jnp.where(open_u > 0.0, spin[t][0], 0.0)
            cv_ref[t, at(p), :] = jnp.where(open_v > 0.0, spin[t][1], 0.0)
            tw_ref[t, at(p), :] = jnp.where(water[t] > 0.0, tau, 0.0)

    flow_u, flow_v = u_ref[0, at(REACH), :], v_ref[0, at(REACH), :]
    zero = jnp.zeros((COLS, LANES), jnp.float32)

    def substep(first, last):
        def body(_, carry):
            total_u, total_v = carry
            for p in range(first, last):
                u = [u_ref[t, at(p), :] for t in range(2)]
                u_west = [u_ref[t, at(p, -1), :] for t in range(2)]
                v = [v_ref[t, at(p), :] for t in range(2)]
                v_south, v_north, u_north = south(*v), north(*v), north(*u)
                for t in range(2):
                    u_north_ref[t, at(p), :] = u_north[t]
                for t in range(2):
                    u_north_west = u_north_ref[t, at(p, -1), :]
                    spread = (u[t] - u_west[t]) + (v[t] - v_south[t])
                    spread_north = (u_north[t] - u_north_west) + (v_north[t] - v[t])
                    eta_ref[t, at(p), :] = eta_ref[t, at(p), :] - tw_ref[t, at(p), :] * spread
                    eta_north_ref[t, at(p), :] = (
                        eta_north_ref[t, at(p), :] - tw_north_ref[t, at(p), :] * spread_north
                    )
                    q_ref[t, at(p), :] = v[t] + v_south[t]
                    t_ref[t, at(p), :] = (u[t] + u_west[t]) + (u_north[t] + u_north_west)
            for p in range(first, last):
                eta = [eta_ref[t, at(p), :] for t in range(2)]
                eta_north = [eta_north_ref[t, at(p), :] for t in range(2)]
                for t in range(2):
                    vbar = q_ref[t, at(p), :] + q_ref[t, at(p, 1), :]
                    rise_u = eta_ref[t, at(p, 1), :] - eta[t]
                    rise_v = eta_north[t] - eta[t]
                    next_u = (u_ref[t, at(p), :] + fu_ref[t, at(p), :]) + (
                        cu_ref[t, at(p), :] * vbar - du_ref[t, at(p), :] * rise_u
                    )
                    next_v = (v_ref[t, at(p), :] + fv_ref[t, at(p), :]) - (
                        cv_ref[t, at(p), :] * t_ref[t, at(p), :] + dv_ref[t, at(p), :] * rise_v
                    )
                    u_ref[t, at(p), :] = next_u
                    v_ref[t, at(p), :] = next_v
                    if p == REACH and t == 0:
                        total_u, total_v = total_u + next_u, total_v + next_v
            return total_u, total_v

        return body

    carry = (zero, zero)
    done = 0
    for ring in range(REACH):
        until = SUBSTEPS - COLS * (REACH - 1 - ring)
        carry = lax.fori_loop(0, until - done, substep(ring, blocks - ring), carry, unroll=2)
        done = until
    out_eta[...] = eta_ref[0, at(REACH), :]
    water = [w_ref[t, at(REACH), :] for t in range(2)]
    open_u = jnp.minimum(water[0], w_ref[0, at(REACH, 1), :])
    open_v = jnp.minimum(water[0], north(*water)[0])
    star_u = flow_u + (STEP / tau) * fu_ref[0, at(REACH), :]
    star_v = flow_v + (STEP / tau) * fv_ref[0, at(REACH), :]
    lift_u = (carry[0] / SUBSTEPS - star_u) / jnp.maximum(depth_of(open_u, levels), 0.25)
    lift_v = (carry[1] / SUBSTEPS - star_v) / jnp.maximum(depth_of(open_v, levels), 0.25)
    for k in range(levels):
        out_u[level(k), :] = su_ref[level(k), :] + jnp.where(open_u > float(k), lift_u, 0.0)
        out_v[level(k), :] = sv_ref[level(k), :] + jnp.where(open_v > float(k), lift_v, 0.0)


def call(kernel, shapes, scratch, *operands, **specs):
    return pl.pallas_call(
        kernel,
        out_shape=[jax.ShapeDtypeStruct(s, jnp.float32) for s in shapes],
        scratch_shapes=[pltpu.VMEM(s, jnp.float32) if isinstance(s, tuple) else s for s in scratch],
        compiler_params=pltpu.CompilerParams(vmem_limit_bytes=VMEM_BYTES),
        **specs,
    )(*operands)


def swap(x, axis, first, hop, wraps):
    count = lax.axis_size(axis)
    pairs = []
    for i in range(first, count, 2):
        j = i + hop
        if wraps or 0 <= j < count:
            pairs += [(i, j % count), (j % count, i)]
    return lax.ppermute(x, axis, pairs)


def local(velocity_u, velocity_v, buoyancy, wind_x, wind_y, free_surface, land_sea, bottom_level):
    levels = velocity_u.shape[0]
    flat = (levels * COLS, LANES)
    u, v, b = (a.reshape(flat) for a in (velocity_u, velocity_v, buoyancy))
    send = (3 * levels // SLOTS * COLS + COLS, LANES)
    inputs = (u, v, b, land_sea, bottom_level, free_surface, wind_x, wind_y)
    whole = pltpu.VMEM((COLS, LANES), jnp.int32)
    rows_a, rows_z, u, v, b, planes = call(
        pack_rows_kernel,
        [send, send, flat, flat, flat, (SLOTS * COLS, LANES)],
        [whole, whole, pltpu.SemaphoreType.DMA((CHUNKS, 3)), pltpu.SemaphoreType.DMA((5,))],
        *[pltpu.with_memory_space_constraint(a, pltpu.HBM) for a in inputs],
        in_specs=[pl.BlockSpec(memory_space=pltpu.HBM)] * 8,
    )
    rows_z = swap(rows_z, "lat", 1, 1, False)
    rows_a = swap(rows_a, "lat", 0, 1, False)
    edge = (5 * levels + 8, LANES)
    cols_a, cols_z, hu, hv, hb, hp = call(
        pack_cols_kernel, [edge, edge, flat, flat, flat, (SLOTS * COLS, LANES)], [], u, v, b, planes, rows_z, rows_a
    )
    cols_z = swap(cols_z, "lon", 1, 1, True)
    cols_a = swap(cols_a, "lon", 0, 1, True)
    both = (edge[0] + levels, LANES)
    x, star_u, star_v = call(
        levels_kernel, [(FIELDS, LANES), flat, flat], [both, both],
        u, v, b, hu, hv, hb, hp, planes, cols_z, cols_a,
    )
    near_z = swap(x, "lon", 1, 1, True)
    near_a = swap(x, "lon", 0, 1, True)
    y = jnp.concatenate([near_z, x, near_a], 0)
    far_z = swap(y, "lon", 1, 3, True)
    far_a = swap(y, "lon", 0, 3, True)
    state = (2, (2 * REACH + 3) * COLS, LANES)
    new_u, new_v, surface = call(
        substeps_kernel, [flat, flat, (COLS, LANES)], [state] * 16, y, far_a, far_z, star_u, star_v
    )
    return new_u.reshape(velocity_u.shape), new_v.reshape(velocity_v.shape), surface


def solution(mesh):
    return jax.shard_map(
        local,
        mesh=mesh,
        in_specs=(P(None, "lon", "lat"),) * 3 + (P("lon", "lat"),) * 5,
        out_specs=(P(None, "lon", "lat"), P(None, "lon", "lat"), P("lon", "lat")),
        check_vma=False,
    )
```

```python
import jax
import jax.numpy as jnp
import numpy as np
from jax import lax
from jax.experimental import pallas as pl
from jax.experimental.pallas import tpu as pltpu
from jax.sharding import PartitionSpec as P

SUBSTEPS = 30
LANES = 128
COLS = 8
RIM = 32
SLOTS = 4
CHUNKS = 4
REACH = 4
FIELDS = 9 * COLS
STEP = 6.0
VMEM_BYTES = 32 * 1024 * 1024


def thickness(levels):
    index = np.arange(levels, dtype=np.float32)
    return (np.float32(1.0) + np.float32(2.0) * index / np.float32(levels)) / np.float32(levels)


def lane_index():
    return lax.broadcasted_iota(jnp.int32, (COLS, LANES), 1)


def col_index():
    return lax.broadcasted_iota(jnp.int32, (COLS, LANES), 0)


def is_even(axis):
    return lax.rem(lax.axis_index(axis), 2) == 0


def level(k):
    return pl.ds(COLS * k, COLS)


def north(own, rim):
    last = lane_index() == LANES - 1
    a, b = pltpu.roll(own, LANES - 1, 1), pltpu.roll(rim, LANES - 1, 1)
    return jnp.where(last, b, a), jnp.where(last, a, b)


def south(own, rim):
    first = lane_index() == 0
    a, b = pltpu.roll(own, 1, 1), pltpu.roll(rim, 1, 1)
    return jnp.where(first, b, a), jnp.where(first, a, b)


def pair_rims(first, second):
    lane = lax.broadcasted_iota(jnp.int32, first.shape, 1)
    return jnp.where((lane >= RIM) & (lane < LANES - RIM), pltpu.roll(second, LANES // 2, 1), first)


def strips(parts, shifts):
    slot = lane_index() // RIM
    moved = [pltpu.roll(p, s, 1) if s else p for p, s in zip(parts, shifts)]
    return jnp.where(
        slot < 2, jnp.where(slot == 0, moved[0], moved[1]), jnp.where(slot == 2, moved[2], moved[3])
    )


def pack_rows_kernel(
    u_in, v_in, b_in, land_in, bottom_in, eta_in, wx_in, wy_in,
    a_ref, z_ref, u_ref, v_ref, b_ref, plane_ref, land_ref, bottom_ref, sems, plane_sem,
):
    levels = u_in.shape[0] // COLS
    groups = levels // SLOTS
    chunks = sems.shape[0]
    fields = ((u_in, u_ref), (v_in, v_ref), (b_in, b_ref))
    part = u_in.shape[0] // chunks
    copies = [
        [
            pltpu.make_async_copy(src.at[pl.ds(c * part, part)], dst.at[pl.ds(c * part, part)], sems.at[c, f])
            for f, (src, dst) in enumerate(fields)
        ]
        for c in range(chunks)
    ]
    planes = [
        pltpu.make_async_copy(src, dst, plane_sem.at[i])
        for i, (src, dst) in enumerate(
            (
                (land_in, land_ref), (bottom_in, bottom_ref), (eta_in, plane_ref.at[level(1)]),
                (wx_in, plane_ref.at[level(2)]), (wy_in, plane_ref.at[level(3)]),
            )
        )
    ]
    for copy in sum(copies, []) + planes:
        copy.start()
    even = is_even("lat")

    def send(at, parts):
        upper, lower = strips(parts, (32, 64, 96, 0)), strips(parts, (0, 32, 64, 96))
        a_ref[level(at), :] = jnp.where(even, upper, lower)
        z_ref[level(at), :] = jnp.where(even, lower, upper)

    for c in range(chunks):
        for f, (_, ref) in enumerate(fields):
            copies[c][f].wait()
            for g in range(c * groups // chunks, (c + 1) * groups // chunks):
                send(f * groups + g, [ref[level(SLOTS * g + s), :] for s in range(SLOTS)])
    for copy in planes:
        copy.wait()
    plane_ref[level(0), :] = (land_ref[...] * bottom_ref[...]).astype(jnp.float32)
    send(3 * groups, [plane_ref[level(s), :] for s in range(SLOTS)])


def pack_cols_kernel(u_ref, v_ref, b_ref, plane_ref, z_in, a_in, a_ref, z_ref, hu_ref, hv_ref, hb_ref, hp_ref):
    even = is_even("lat")
    upper = lane_index() < LANES // 2
    levels = u_ref.shape[0] // COLS
    groups = levels // SLOTS

    def receive(at, s):
        a, z = a_in[level(at), :], z_in[level(at), :]
        n, o = jnp.where(even, a, z), jnp.where(even, z, a)
        to_first, to_last = (LANES - RIM * s) % LANES, (LANES - RIM - RIM * s) % LANES
        n = pltpu.roll(n, to_first, 1) if to_first else n
        o = pltpu.roll(o, to_last, 1) if to_last else o
        return jnp.where(upper, n, o)

    for f, ref in enumerate((hu_ref, hv_ref, hb_ref)):
        for k in range(levels):
            ref[level(k), :] = receive(f * groups + k // SLOTS, k % SLOTS)
    for s in range(SLOTS):
        hp_ref[level(s), :] = receive(3 * groups, s)
    even_col = is_even("lon")

    def edge(ref, rows, col):
        return ref[pl.ds(col, rows, stride=COLS), :]

    def store(col, out_ref):
        out_ref[pl.ds(0, levels), :] = edge(u_ref, levels, col)
        out_ref[pl.ds(levels, levels), :] = edge(v_ref, levels, col)
        out_ref[pl.ds(2 * levels, levels), :] = edge(b_ref, levels, col)
        out_ref[pl.ds(3 * levels, levels), :] = pair_rims(edge(hu_ref, levels, col), edge(hv_ref, levels, col))
        out_ref[pl.ds(4 * levels, levels), :] = edge(hb_ref, levels, col)
        out_ref[pl.ds(5 * levels, 1), :] = plane_ref[pl.ds(col, 1), :]
        out_ref[pl.ds(5 * levels + 1, 1), :] = hp_ref[pl.ds(col, 1), :]
        out_ref[pl.ds(5 * levels + 2, 6), :] = jnp.zeros((6, LANES), jnp.float32)

    @pl.when(even_col)
    def _():
        store(COLS - 1, a_ref)
        store(0, z_ref)

    @pl.when(jnp.logical_not(even_col))
    def _():
        store(0, a_ref)
        store(COLS - 1, z_ref)


def levels_kernel(
    u_ref, v_ref, b_ref, hu_ref, hv_ref, hb_ref, hp_ref, plane_ref, z_in, a_in,
    x_ref, su_ref, sv_ref, east_ref, west_ref,
):
    levels = u_ref.shape[0] // COLS
    thick = thickness(levels)
    even = is_even("lon")
    a, z = a_in[...], z_in[...]
    east_ref[pl.ds(0, a.shape[0]), :] = jnp.where(even, a, z)
    west_ref[pl.ds(0, a.shape[0]), :] = jnp.where(even, z, a)
    for ref in (east_ref, west_ref):
        ref[pl.ds(a.shape[0], levels), :] = pltpu.roll(ref[pl.ds(3 * levels, levels), :], LANES // 2, 1)
    own_at = {"u": 0, "v": levels, "b": 2 * levels, "w": 5 * levels}
    rim_at = {"u": 3 * levels, "v": a.shape[0], "b": 4 * levels, "w": 5 * levels + 1}
    col = col_index()
    top_col, bottom_col = col == COLS - 1, col == 0

    def row(ref, at):
        return jnp.broadcast_to(ref[pl.ds(at, 1), :], (COLS, LANES))

    def east(pair, name, k):
        own, rim = pair
        return (
            jnp.where(top_col, row(east_ref, own_at[name] + k), pltpu.roll(own, COLS - 1, 0)),
            jnp.where(top_col, row(east_ref, rim_at[name] + k), pltpu.roll(rim, COLS - 1, 0)),
        )

    def west(pair, name, k):
        own, rim = pair
        return (
            jnp.where(bottom_col, row(west_ref, own_at[name] + k), pltpu.roll(own, 1, 0)),
            jnp.where(bottom_col, row(west_ref, rim_at[name] + k), pltpu.roll(rim, 1, 0)),
        )

    water, eta, wx, wy = [(plane_ref[level(i), :], hp_ref[level(i), :]) for i in range(SLOTS)]
    open_u = [jnp.minimum(w, e) for w, e in zip(water, east(water, "w", 0))]
    open_v = [jnp.minimum(w, n) for w, n in zip(water, north(*water))]
    zero = jnp.zeros((COLS, LANES), jnp.float32)
    slope_u, slope_v = [zero, zero], [zero, zero]
    forcing_u, forcing_v = [zero, zero], [zero, zero]
    flow_u, flow_v = [zero, zero], [zero, zero]
    for k in range(levels):
        dz = float(thick[k])
        u = (u_ref[level(k), :], hu_ref[level(k), :])
        v = (v_ref[level(k), :], hv_ref[level(k), :])
        b = (b_ref[level(k), :], hb_ref[level(k), :])
        around_u = list(zip(east(u, "u", k), west(u, "u", k), north(*u), south(*u)))
        around_v = list(zip(east(v, "v", k), west(v, "v", k), north(*v), south(*v)))
        b_east, b_north = east(b, "b", k), north(*b)
        for t in range(2):
            slope_u[t] = slope_u[t] + dz * (b_east[t] - b[t])
            slope_v[t] = slope_v[t] + dz * (b_north[t] - b[t])
            force_u = 0.05 * (sum(around_u[t][1:], around_u[t][0]) - 4.0 * u[t]) - slope_u[t]
            force_v = 0.05 * (sum(around_v[t][1:], around_v[t][0]) - 4.0 * v[t]) - slope_v[t]
            if k == 0:
                force_u = force_u + wx[t] / dz
                force_v = force_v + wy[t] / dz
            wet_u, wet_v = open_u[t] > float(k), open_v[t] > float(k)
            force_u, vel_u = jnp.where(wet_u, force_u, 0.0), jnp.where(wet_u, u[t], 0.0)
            force_v, vel_v = jnp.where(wet_v, force_v, 0.0), jnp.where(wet_v, v[t], 0.0)
            forcing_u[t] = forcing_u[t] + dz * force_u
            forcing_v[t] = forcing_v[t] + dz * force_v
            flow_u[t] = flow_u[t] + dz * vel_u
            flow_v[t] = flow_v[t] + dz * vel_v
            if t == 0:
                su_ref[level(k), :] = vel_u + STEP * force_u
                sv_ref[level(k), :] = vel_v + STEP * force_v
    fields = (forcing_u, forcing_v, flow_u, flow_v, water, eta)
    for i, f in enumerate(fields):
        x_ref[level(i), :] = f[0]
    for i in range(3):
        x_ref[level(6 + i), :] = pair_rims(fields[2 * i][1], fields[2 * i + 1][1])


def depth_of(count, levels):
    return (count + count * (count - 1.0) * (1.0 / levels)) * (1.0 / levels)


def substeps_kernel(
    y_ref, z_in, a_in, su_ref, sv_ref, out_u, out_v, out_eta,
    eta_ref, u_ref, v_ref, w_ref, fu_ref, fv_ref, du_ref, dv_ref, cu_ref, cv_ref, tw_ref, q_ref, t_ref,
    eta_north_ref, u_north_ref, tw_north_ref,
):
    levels = su_ref.shape[0] // COLS
    tau = STEP / SUBSTEPS
    blocks = 2 * REACH + 1
    even = is_even("lon")
    lane = lane_index()

    def at(p, shift=0):
        return pl.ds(COLS * (p + 1) + shift, COLS)

    places = (
        ((z_in, 2), (a_in, 0)), ((y_ref, 0), (y_ref, 2)), ((a_in, 2), (z_in, 0)),
        ((z_in, 1), (a_in, 1)), ((y_ref, 1), (y_ref, 1)), ((a_in, 1), (z_in, 1)),
        ((z_in, 0), (a_in, 2)), ((y_ref, 2), (y_ref, 0)), ((a_in, 0), (z_in, 2)),
    )
    for p, (for_even, for_odd) in enumerate(places):
        def tile(i):
            first = for_even[0][pl.ds(for_even[1] * FIELDS + COLS * i, COLS), :]
            if p == REACH:
                return first
            return jnp.where(even, first, for_odd[0][pl.ds(for_odd[1] * FIELDS + COLS * i, COLS), :])

        targets = (fu_ref, fv_ref, u_ref, v_ref, w_ref, eta_ref)
        for i, ref in enumerate(targets):
            value = tile(i)
            ref[0, at(p), :] = tau * value if i < 2 else value
        for i in range(3):
            value = tile(6 + i)
            other = pltpu.roll(value, LANES // 2, 1)
            if i == 0:
                value, other = tau * value, tau * other
            targets[2 * i][1, at(p), :] = value
            targets[2 * i + 1][1, at(p), :] = other

    total_rows = LANES * lax.axis_size("lat")
    base = (lax.axis_index("lat") * LANES).astype(jnp.float32)
    own_row = lane.astype(jnp.float32) + base
    rim_row = jnp.where(lane < LANES // 2, lane + LANES, lane - LANES).astype(jnp.float32) + base
    spin = [
        [0.25 * tau * 0.4 * (2.0 * (r + half) * (1.0 / total_rows) - 1.0) for half in (0.5, 1.0)]
        for r in (own_row, rim_row)
    ]
    for p in range(blocks):
        water = [w_ref[t, at(p), :] for t in range(2)]
        water_north = north(*water)
        eta_north = north(eta_ref[0, at(p), :], eta_ref[1, at(p), :])
        for t in range(2):
            eta_north_ref[t, at(p), :] = eta_north[t]
            tw_north_ref[t, at(p), :] = jnp.where(water_north[t] > 0.0, tau, 0.0)
            open_u = jnp.minimum(water[t], w_ref[t, at(p, 1), :])
            open_v = jnp.minimum(water[t], water_north[t])
            du_ref[t, at(p), :] = tau * depth_of(open_u, levels)
            dv_ref[t, at(p), :] = tau * depth_of(open_v, levels)
            cu_ref[t, at(p), :] = jnp.where(open_u > 0.0, spin[t][0], 0.0)
            cv_ref[t, at(p), :] = jnp.where(open_v > 0.0, spin[t][1], 0.0)
            tw_ref[t, at(p), :] = jnp.where(water[t] > 0.0, tau, 0.0)

    flow_u, flow_v = u_ref[0, at(REACH), :], v_ref[0, at(REACH), :]
    zero = jnp.zeros((COLS, LANES), jnp.float32)

    def substep(first, last):
        def body(_, carry):
            total_u, total_v = carry
            for p in range(first, last):
                u = [u_ref[t, at(p), :] for t in range(2)]
                u_west = [u_ref[t, at(p, -1), :] for t in range(2)]
                v = [v_ref[t, at(p), :] for t in range(2)]
                v_south, v_north, u_north = south(*v), north(*v), north(*u)
                for t in range(2):
                    u_north_ref[t, at(p), :] = u_north[t]
                for t in range(2):
                    u_north_west = u_north_ref[t, at(p, -1), :]
                    spread = (u[t] - u_west[t]) + (v[t] - v_south[t])
                    spread_north = (u_north[t] - u_north_west) + (v_north[t] - v[t])
                    eta_ref[t, at(p), :] = eta_ref[t, at(p), :] - tw_ref[t, at(p), :] * spread
                    eta_north_ref[t, at(p), :] = (
                        eta_north_ref[t, at(p), :] - tw_north_ref[t, at(p), :] * spread_north
                    )
                    q_ref[t, at(p), :] = v[t] + v_south[t]
                    t_ref[t, at(p), :] = (u[t] + u_west[t]) + (u_north[t] + u_north_west)
            for p in range(first, last):
                eta = [eta_ref[t, at(p), :] for t in range(2)]
                eta_north = [eta_north_ref[t, at(p), :] for t in range(2)]
                for t in range(2):
                    vbar = q_ref[t, at(p), :] + q_ref[t, at(p, 1), :]
                    rise_u = eta_ref[t, at(p, 1), :] - eta[t]
                    rise_v = eta_north[t] - eta[t]
                    next_u = (u_ref[t, at(p), :] + fu_ref[t, at(p), :]) + (
                        cu_ref[t, at(p), :] * vbar - du_ref[t, at(p), :] * rise_u
                    )
                    next_v = (v_ref[t, at(p), :] + fv_ref[t, at(p), :]) - (
                        cv_ref[t, at(p), :] * t_ref[t, at(p), :] + dv_ref[t, at(p), :] * rise_v
                    )
                    u_ref[t, at(p), :] = next_u
                    v_ref[t, at(p), :] = next_v
                    if p == REACH and t == 0:
                        total_u, total_v = total_u + next_u, total_v + next_v
            return total_u, total_v

        return body

    carry = (zero, zero)
    done = 0
    for ring in range(REACH):
        until = SUBSTEPS - COLS * (REACH - 1 - ring)
        carry = lax.fori_loop(0, until - done, substep(ring, blocks - ring), carry, unroll=2)
        done = until
    out_eta[...] = eta_ref[0, at(REACH), :]
    water = [w_ref[t, at(REACH), :] for t in range(2)]
    open_u = jnp.minimum(water[0], w_ref[0, at(REACH, 1), :])
    open_v = jnp.minimum(water[0], north(*water)[0])
    star_u = flow_u + (STEP / tau) * fu_ref[0, at(REACH), :]
    star_v = flow_v + (STEP / tau) * fv_ref[0, at(REACH), :]
    lift_u = (carry[0] / SUBSTEPS - star_u) / jnp.maximum(depth_of(open_u, levels), 0.25)
    lift_v = (carry[1] / SUBSTEPS - star_v) / jnp.maximum(depth_of(open_v, levels), 0.25)
    for k in range(levels):
        out_u[level(k), :] = su_ref[level(k), :] + jnp.where(open_u > float(k), lift_u, 0.0)
        out_v[level(k), :] = sv_ref[level(k), :] + jnp.where(open_v > float(k), lift_v, 0.0)


def call(kernel, shapes, scratch, *operands, **specs):
    return pl.pallas_call(
        kernel,
        out_shape=[jax.ShapeDtypeStruct(s, jnp.float32) for s in shapes],
        scratch_shapes=[pltpu.VMEM(s, jnp.float32) if isinstance(s, tuple) else s for s in scratch],
        compiler_params=pltpu.CompilerParams(vmem_limit_bytes=VMEM_BYTES),
        **specs,
    )(*operands)


def swap(x, axis, first, hop, wraps):
    count = lax.axis_size(axis)
    pairs = []
    for i in range(first, count, 2):
        j = i + hop
        if wraps or 0 <= j < count:
            pairs += [(i, j % count), (j % count, i)]
    return lax.ppermute(x, axis, pairs)


def local(velocity_u, velocity_v, buoyancy, wind_x, wind_y, free_surface, land_sea, bottom_level):
    levels = velocity_u.shape[0]
    flat = (levels * COLS, LANES)
    u, v, b = (a.reshape(flat) for a in (velocity_u, velocity_v, buoyancy))
    send = (3 * levels // SLOTS * COLS + COLS, LANES)
    inputs = (u, v, b, land_sea, bottom_level, free_surface, wind_x, wind_y)
    whole = pltpu.VMEM((COLS, LANES), jnp.int32)
    rows_a, rows_z, u, v, b, planes = call(
        pack_rows_kernel,
        [send, send, flat, flat, flat, (SLOTS * COLS, LANES)],
        [whole, whole, pltpu.SemaphoreType.DMA((CHUNKS, 3)), pltpu.SemaphoreType.DMA((5,))],
        *[pltpu.with_memory_space_constraint(a, pltpu.HBM) for a in inputs],
        in_specs=[pl.BlockSpec(memory_space=pltpu.HBM)] * 8,
    )
    rows_z = swap(rows_z, "lat", 1, 1, False)
    rows_a = swap(rows_a, "lat", 0, 1, False)
    edge = (5 * levels + 8, LANES)
    cols_a, cols_z, hu, hv, hb, hp = call(
        pack_cols_kernel, [edge, edge, flat, flat, flat, (SLOTS * COLS, LANES)], [], u, v, b, planes, rows_z, rows_a
    )
    cols_z = swap(cols_z, "lon", 1, 1, True)
    cols_a = swap(cols_a, "lon", 0, 1, True)
    both = (edge[0] + levels, LANES)
    x, star_u, star_v = call(
        levels_kernel, [(FIELDS, LANES), flat, flat], [both, both],
        u, v, b, hu, hv, hb, hp, planes, cols_z, cols_a,
    )
    far_z = swap(x, "lon", 1, 3, True)
    far_a = swap(x, "lon", 0, 3, True)
    y = jnp.concatenate([far_z, x, far_a], 0)
    near_z = swap(y, "lon", 1, 1, True)
    near_a = swap(y, "lon", 0, 1, True)
    state = (2, (2 * REACH + 3) * COLS, LANES)
    new_u, new_v, surface = call(
        substeps_kernel, [flat, flat, (COLS, LANES)], [state] * 16, y, near_z, near_a, star_u, star_v
    )
    return new_u.reshape(velocity_u.shape), new_v.reshape(velocity_v.shape), surface


def solution(mesh):
    return jax.shard_map(
        local,
        mesh=mesh,
        in_specs=(P(None, "lon", "lat"),) * 3 + (P("lon", "lat"),) * 5,
        out_specs=(P(None, "lon", "lat"), P(None, "lon", "lat"), P("lon", "lat")),
        check_vma=False,
    )
```

```python
import jax
import jax.numpy as jnp
import numpy as np
from jax import lax
from jax.experimental import pallas as pl
from jax.experimental.pallas import tpu as pltpu
from jax.sharding import PartitionSpec as P

SUBSTEPS = 30
LANES = 128
COLS = 8
RIM = 32
SLOTS = 4
CHUNKS = 4
REACH = 4
FIELDS = 9 * COLS
STEP = 6.0
VMEM_BYTES = 32 * 1024 * 1024


def thickness(levels):
    index = np.arange(levels, dtype=np.float32)
    return (np.float32(1.0) + np.float32(2.0) * index / np.float32(levels)) / np.float32(levels)


def lane_index():
    return lax.broadcasted_iota(jnp.int32, (COLS, LANES), 1)


def col_index():
    return lax.broadcasted_iota(jnp.int32, (COLS, LANES), 0)


def is_even(axis):
    return lax.rem(lax.axis_index(axis), 2) == 0


def level(k):
    return pl.ds(COLS * k, COLS)


def north(own, rim):
    last = lane_index() == LANES - 1
    a, b = pltpu.roll(own, LANES - 1, 1), pltpu.roll(rim, LANES - 1, 1)
    return jnp.where(last, b, a), jnp.where(last, a, b)


def south(own, rim):
    first = lane_index() == 0
    a, b = pltpu.roll(own, 1, 1), pltpu.roll(rim, 1, 1)
    return jnp.where(first, b, a), jnp.where(first, a, b)


def pair_rims(first, second):
    lane = lax.broadcasted_iota(jnp.int32, first.shape, 1)
    return jnp.where((lane >= RIM) & (lane < LANES - RIM), pltpu.roll(second, LANES // 2, 1), first)


def strips(parts, shifts):
    slot = lane_index() // RIM
    moved = [pltpu.roll(p, s, 1) if s else p for p, s in zip(parts, shifts)]
    return jnp.where(
        slot < 2, jnp.where(slot == 0, moved[0], moved[1]), jnp.where(slot == 2, moved[2], moved[3])
    )


def pack_rows_kernel(
    u_in, v_in, b_in, land_in, bottom_in, eta_in, wx_in, wy_in,
    a_ref, z_ref, u_ref, v_ref, b_ref, plane_ref, land_ref, bottom_ref, sems, plane_sem,
):
    levels = u_in.shape[0] // COLS
    groups = levels // SLOTS
    chunks = sems.shape[0]
    fields = ((u_in, u_ref), (v_in, v_ref), (b_in, b_ref))
    part = u_in.shape[0] // chunks
    copies = [
        [
            pltpu.make_async_copy(src.at[pl.ds(c * part, part)], dst.at[pl.ds(c * part, part)], sems.at[c, f])
            for f, (src, dst) in enumerate(fields)
        ]
        for c in range(chunks)
    ]
    planes = [
        pltpu.make_async_copy(src, dst, plane_sem.at[i])
        for i, (src, dst) in enumerate(
            (
                (land_in, land_ref), (bottom_in, bottom_ref), (eta_in, plane_ref.at[level(1)]),
                (wx_in, plane_ref.at[level(2)]), (wy_in, plane_ref.at[level(3)]),
            )
        )
    ]
    for copy in sum(copies, []) + planes:
        copy.start()
    even = is_even("lat")

    def send(at, parts):
        upper, lower = strips(parts, (32, 64, 96, 0)), strips(parts, (0, 32, 64, 96))
        a_ref[level(at), :] = jnp.where(even, upper, lower)
        z_ref[level(at), :] = jnp.where(even, lower, upper)

    for c in range(chunks):
        for f, (_, ref) in enumerate(fields):
            copies[c][f].wait()
            for g in range(c * groups // chunks, (c + 1) * groups // chunks):
                send(f * groups + g, [ref[level(SLOTS * g + s), :] for s in range(SLOTS)])
    for copy in planes:
        copy.wait()
    plane_ref[level(0), :] = (land_ref[...] * bottom_ref[...]).astype(jnp.float32)
    send(3 * groups, [plane_ref[level(s), :] for s in range(SLOTS)])


def pack_cols_kernel(u_ref, v_ref, b_ref, plane_ref, z_in, a_in, a_ref, z_ref, hu_ref, hv_ref, hb_ref, hp_ref):
    even = is_even("lat")
    upper = lane_index() < LANES // 2
    levels = u_ref.shape[0] // COLS
    groups = levels // SLOTS

    def receive(at, s):
        a, z = a_in[level(at), :], z_in[level(at), :]
        n, o = jnp.where(even, a, z), jnp.where(even, z, a)
        to_first, to_last = (LANES - RIM * s) % LANES, (LANES - RIM - RIM * s) % LANES
        n = pltpu.roll(n, to_first, 1) if to_first else n
        o = pltpu.roll(o, to_last, 1) if to_last else o
        return jnp.where(upper, n, o)

    for f, ref in enumerate((hu_ref, hv_ref, hb_ref)):
        for k in range(levels):
            ref[level(k), :] = receive(f * groups + k // SLOTS, k % SLOTS)
    for s in range(SLOTS):
        hp_ref[level(s), :] = receive(3 * groups, s)
    even_col = is_even("lon")

    def edge(ref, rows, col):
        return ref[pl.ds(col, rows, stride=COLS), :]

    def store(col, out_ref):
        out_ref[pl.ds(0, levels), :] = edge(u_ref, levels, col)
        out_ref[pl.ds(levels, levels), :] = edge(v_ref, levels, col)
        out_ref[pl.ds(2 * levels, levels), :] = edge(b_ref, levels, col)
        out_ref[pl.ds(3 * levels, levels), :] = pair_rims(edge(hu_ref, levels, col), edge(hv_ref, levels, col))
        out_ref[pl.ds(4 * levels, levels), :] = edge(hb_ref, levels, col)
        out_ref[pl.ds(5 * levels, 1), :] = plane_ref[pl.ds(col, 1), :]
        out_ref[pl.ds(5 * levels + 1, 1), :] = hp_ref[pl.ds(col, 1), :]
        out_ref[pl.ds(5 * levels + 2, 6), :] = jnp.zeros((6, LANES), jnp.float32)

    @pl.when(even_col)
    def _():
        store(COLS - 1, a_ref)
        store(0, z_ref)

    @pl.when(jnp.logical_not(even_col))
    def _():
        store(0, a_ref)
        store(COLS - 1, z_ref)


def levels_kernel(
    u_ref, v_ref, b_ref, hu_ref, hv_ref, hb_ref, hp_ref, plane_ref, z_in, a_in,
    x_ref, su_ref, sv_ref, east_ref, west_ref,
):
    levels = u_ref.shape[0] // COLS
    thick = thickness(levels)
    even = is_even("lon")
    a, z = a_in[...], z_in[...]
    east_ref[pl.ds(0, a.shape[0]), :] = jnp.where(even, a, z)
    west_ref[pl.ds(0, a.shape[0]), :] = jnp.where(even, z, a)
    for ref in (east_ref, west_ref):
        ref[pl.ds(a.shape[0], levels), :] = pltpu.roll(ref[pl.ds(3 * levels, levels), :], LANES // 2, 1)
    own_at = {"u": 0, "v": levels, "b": 2 * levels, "w": 5 * levels}
    rim_at = {"u": 3 * levels, "v": a.shape[0], "b": 4 * levels, "w": 5 * levels + 1}
    col = col_index()
    top_col, bottom_col = col == COLS - 1, col == 0

    def row(ref, at):
        return jnp.broadcast_to(ref[pl.ds(at, 1), :], (COLS, LANES))

    def east(pair, name, k):
        own, rim = pair
        return (
            jnp.where(top_col, row(east_ref, own_at[name] + k), pltpu.roll(own, COLS - 1, 0)),
            jnp.where(top_col, row(east_ref, rim_at[name] + k), pltpu.roll(rim, COLS - 1, 0)),
        )

    def west(pair, name, k):
        own, rim = pair
        return (
            jnp.where(bottom_col, row(west_ref, own_at[name] + k), pltpu.roll(own, 1, 0)),
            jnp.where(bottom_col, row(west_ref, rim_at[name] + k), pltpu.roll(rim, 1, 0)),
        )

    water, eta, wx, wy = [(plane_ref[level(i), :], hp_ref[level(i), :]) for i in range(SLOTS)]
    open_u = [jnp.minimum(w, e) for w, e in zip(water, east(water, "w", 0))]
    open_v = [jnp.minimum(w, n) for w, n in zip(water, north(*water))]
    zero = jnp.zeros((COLS, LANES), jnp.float32)
    slope_u, slope_v = [zero, zero], [zero, zero]
    forcing_u, forcing_v = [zero, zero], [zero, zero]
    flow_u, flow_v = [zero, zero], [zero, zero]
    for k in range(levels):
        dz = float(thick[k])
        u = (u_ref[level(k), :], hu_ref[level(k), :])
        v = (v_ref[level(k), :], hv_ref[level(k), :])
        b = (b_ref[level(k), :], hb_ref[level(k), :])
        around_u = list(zip(east(u, "u", k), west(u, "u", k), north(*u), south(*u)))
        around_v = list(zip(east(v, "v", k), west(v, "v", k), north(*v), south(*v)))
        b_east, b_north = east(b, "b", k), north(*b)
        for t in range(2):
            slope_u[t] = slope_u[t] + dz * (b_east[t] - b[t])
            slope_v[t] = slope_v[t] + dz * (b_north[t] - b[t])
            force_u = 0.05 * (sum(around_u[t][1:], around_u[t][0]) - 4.0 * u[t]) - slope_u[t]
            force_v = 0.05 * (sum(around_v[t][1:], around_v[t][0]) - 4.0 * v[t]) - slope_v[t]
            if k == 0:
                force_u = force_u + wx[t] / dz
                force_v = force_v + wy[t] / dz
            wet_u, wet_v = open_u[t] > float(k), open_v[t] > float(k)
            force_u, vel_u = jnp.where(wet_u, force_u, 0.0), jnp.where(wet_u, u[t], 0.0)
            force_v, vel_v = jnp.where(wet_v, force_v, 0.0), jnp.where(wet_v, v[t], 0.0)
            forcing_u[t] = forcing_u[t] + dz * force_u
            forcing_v[t] = forcing_v[t] + dz * force_v
            flow_u[t] = flow_u[t] + dz * vel_u
            flow_v[t] = flow_v[t] + dz * vel_v
            if t == 0:
                su_ref[level(k), :] = vel_u + STEP * force_u
                sv_ref[level(k), :] = vel_v + STEP * force_v
    fields = (forcing_u, forcing_v, flow_u, flow_v, water, eta)
    for i, f in enumerate(fields):
        x_ref[level(i), :] = f[0]
    for i in range(3):
        x_ref[level(6 + i), :] = pair_rims(fields[2 * i][1], fields[2 * i + 1][1])


def depth_of(count, levels):
    return (count + count * (count - 1.0) * (1.0 / levels)) * (1.0 / levels)


def substeps_kernel(
    y_ref, a_in, z_in, su_ref, sv_ref, out_u, out_v, out_eta,
    eta_ref, u_ref, v_ref, w_ref, fu_ref, fv_ref, du_ref, dv_ref, cu_ref, cv_ref, tw_ref, q_ref, t_ref,
    eta_north_ref, u_north_ref, tw_north_ref,
):
    levels = su_ref.shape[0] // COLS
    tau = STEP / SUBSTEPS
    blocks = 2 * REACH + 1
    even = is_even("lon")
    lane = lane_index()

    def at(p, shift=0):
        return pl.ds(COLS * (p + 1) + shift, COLS)

    places = (
        ((z_in, 2), (a_in, 0)), ((y_ref, 0), (y_ref, 2)), ((a_in, 2), (z_in, 0)),
        ((z_in, 1), (a_in, 1)), ((y_ref, 1), (y_ref, 1)), ((a_in, 1), (z_in, 1)),
        ((z_in, 0), (a_in, 2)), ((y_ref, 2), (y_ref, 0)), ((a_in, 0), (z_in, 2)),
    )
    for p, (for_even, for_odd) in enumerate(places):
        def tile(i):
            first = for_even[0][pl.ds(for_even[1] * FIELDS + COLS * i, COLS), :]
            if p == REACH:
                return first
            return jnp.where(even, first, for_odd[0][pl.ds(for_odd[1] * FIELDS + COLS * i, COLS), :])

        targets = (fu_ref, fv_ref, u_ref, v_ref, w_ref, eta_ref)
        for i, ref in enumerate(targets):
            value = tile(i)
            ref[0, at(p), :] = tau * value if i < 2 else value
        for i in range(3):
            value = tile(6 + i)
            other = pltpu.roll(value, LANES // 2, 1)
            if i == 0:
                value, other = tau * value, tau * other
            targets[2 * i][1, at(p), :] = value
            targets[2 * i + 1][1, at(p), :] = other

    total_rows = LANES * lax.axis_size("lat")
    base = (lax.axis_index("lat") * LANES).astype(jnp.float32)
    own_row = lane.astype(jnp.float32) + base
    rim_row = jnp.where(lane < LANES // 2, lane + LANES, lane - LANES).astype(jnp.float32) + base
    spin = [
        [0.25 * tau * 0.4 * (2.0 * (r + half) * (1.0 / total_rows) - 1.0) for half in (0.5, 1.0)]
        for r in (own_row, rim_row)
    ]
    for p in range(blocks):
        water = [w_ref[t, at(p), :] for t in range(2)]
        water_north = north(*water)
        eta_north = north(eta_ref[0, at(p), :], eta_ref[1, at(p), :])
        for t in range(2):
            eta_north_ref[t, at(p), :] = eta_north[t]
            tw_north_ref[t, at(p), :] = jnp.where(water_north[t] > 0.0, tau, 0.0)
            open_u = jnp.minimum(water[t], w_ref[t, at(p, 1), :])
            open_v = jnp.minimum(water[t], water_north[t])
            du_ref[t, at(p), :] = tau * depth_of(open_u, levels)
            dv_ref[t, at(p), :] = tau * depth_of(open_v, levels)
            cu_ref[t, at(p), :] = jnp.where(open_u > 0.0, spin[t][0], 0.0)
            cv_ref[t, at(p), :] = jnp.where(open_v > 0.0, spin[t][1], 0.0)
            tw_ref[t, at(p), :] = jnp.where(water[t] > 0.0, tau, 0.0)

    flow_u, flow_v = u_ref[0, at(REACH), :], v_ref[0, at(REACH), :]
    zero = jnp.zeros((COLS, LANES), jnp.float32)

    def substep(first, last):
        def body(_, carry):
            total_u, total_v = carry
            for p in range(first, last):
                u = [u_ref[t, at(p), :] for t in range(2)]
                u_west = [u_ref[t, at(p, -1), :] for t in range(2)]
                v = [v_ref[t, at(p), :] for t in range(2)]
                v_south, v_north, u_north = south(*v), north(*v), north(*u)
                for t in range(2):
                    u_north_ref[t, at(p), :] = u_north[t]
                for t in range(2):
                    u_north_west = u_north_ref[t, at(p, -1), :]
                    spread = (u[t] - u_west[t]) + (v[t] - v_south[t])
                    spread_north = (u_north[t] - u_north_west) + (v_north[t] - v[t])
                    eta_ref[t, at(p), :] = eta_ref[t, at(p), :] - tw_ref[t, at(p), :] * spread
                    eta_north_ref[t, at(p), :] = (
                        eta_north_ref[t, at(p), :] - tw_north_ref[t, at(p), :] * spread_north
                    )
                    q_ref[t, at(p), :] = v[t] + v_south[t]
                    t_ref[t, at(p), :] = (u[t] + u_west[t]) + (u_north[t] + u_north_west)
            for p in range(first, last):
                eta = [eta_ref[t, at(p), :] for t in range(2)]
                eta_north = [eta_north_ref[t, at(p), :] for t in range(2)]
                for t in range(2):
                    vbar = q_ref[t, at(p), :] + q_ref[t, at(p, 1), :]
                    rise_u = eta_ref[t, at(p, 1), :] - eta[t]
                    rise_v = eta_north[t] - eta[t]
                    next_u = (u_ref[t, at(p), :] + fu_ref[t, at(p), :]) + (
                        cu_ref[t, at(p), :] * vbar - du_ref[t, at(p), :] * rise_u
                    )
                    next_v = (v_ref[t, at(p), :] + fv_ref[t, at(p), :]) - (
                        cv_ref[t, at(p), :] * t_ref[t, at(p), :] + dv_ref[t, at(p), :] * rise_v
                    )
                    u_ref[t, at(p), :] = next_u
                    v_ref[t, at(p), :] = next_v
                    if p == REACH and t == 0:
                        total_u, total_v = total_u + next_u, total_v + next_v
            return total_u, total_v

        return body

    carry = (zero, zero)
    done = 0
    for ring in range(REACH):
        until = SUBSTEPS - COLS * (REACH - 1 - ring)
        carry = lax.fori_loop(0, until - done, substep(ring, blocks - ring), carry, unroll=2)
        done = until
    out_eta[...] = eta_ref[0, at(REACH), :]
    water = [w_ref[t, at(REACH), :] for t in range(2)]
    open_u = jnp.minimum(water[0], w_ref[0, at(REACH, 1), :])
    open_v = jnp.minimum(water[0], north(*water)[0])
    star_u = flow_u + (STEP / tau) * fu_ref[0, at(REACH), :]
    star_v = flow_v + (STEP / tau) * fv_ref[0, at(REACH), :]
    lift_u = (carry[0] / SUBSTEPS - star_u) / jnp.maximum(depth_of(open_u, levels), 0.25)
    lift_v = (carry[1] / SUBSTEPS - star_v) / jnp.maximum(depth_of(open_v, levels), 0.25)
    for k in range(levels):
        out_u[level(k), :] = su_ref[level(k), :] + jnp.where(open_u > float(k), lift_u, 0.0)
        out_v[level(k), :] = sv_ref[level(k), :] + jnp.where(open_v > float(k), lift_v, 0.0)


def call(kernel, shapes, scratch, *operands, **specs):
    return pl.pallas_call(
        kernel,
        out_shape=[jax.ShapeDtypeStruct(s, jnp.float32) for s in shapes],
        scratch_shapes=[pltpu.VMEM(s, jnp.float32) if isinstance(s, tuple) else s for s in scratch],
        compiler_params=pltpu.CompilerParams(vmem_limit_bytes=VMEM_BYTES),
        **specs,
    )(*operands)


def swap(x, axis, first, hop, wraps):
    count = lax.axis_size(axis)
    pairs = []
    for i in range(first, count, 2):
        j = i + hop
        if wraps or 0 <= j < count:
            pairs += [(i, j % count), (j % count, i)]
    return lax.ppermute(x, axis, pairs)


def local(velocity_u, velocity_v, buoyancy, wind_x, wind_y, free_surface, land_sea, bottom_level):
    levels = velocity_u.shape[0]
    flat = (levels * COLS, LANES)
    u, v, b = (a.reshape(flat) for a in (velocity_u, velocity_v, buoyancy))
    send = (3 * levels // SLOTS * COLS + COLS, LANES)
    inputs = (u, v, b, land_sea, bottom_level, free_surface, wind_x, wind_y)
    whole = pltpu.VMEM((COLS, LANES), jnp.int32)
    rows_a, rows_z, u, v, b, planes = call(
        pack_rows_kernel,
        [send, send, flat, flat, flat, (SLOTS * COLS, LANES)],
        [whole, whole, pltpu.SemaphoreType.DMA((CHUNKS, 3)), pltpu.SemaphoreType.DMA((5,))],
        *[pltpu.with_memory_space_constraint(a, pltpu.HBM) for a in inputs],
        in_specs=[pl.BlockSpec(memory_space=pltpu.HBM)] * 8,
    )
    rows_z = swap(rows_z, "lat", 1, 1, False)
    rows_a = swap(rows_a, "lat", 0, 1, False)
    edge = (5 * levels + 8, LANES)
    cols_a, cols_z, hu, hv, hb, hp = call(
        pack_cols_kernel, [edge, edge, flat, flat, flat, (SLOTS * COLS, LANES)], [], u, v, b, planes, rows_z, rows_a
    )
    cols_z = swap(cols_z, "lon", 1, 1, True)
    cols_a = swap(cols_a, "lon", 0, 1, True)
    both = (edge[0] + levels, LANES)
    x, star_u, star_v = call(
        levels_kernel, [(FIELDS, LANES), flat, flat], [both, both],
        u, v, b, hu, hv, hb, hp, planes, cols_z, cols_a,
    )
    far_z = swap(x, "lon", 1, 3, True)
    far_a = swap(x, "lon", 0, 3, True)
    y = jnp.concatenate([far_z, x, far_a], 0)
    near_z = swap(y, "lon", 1, 1, True)
    near_a = swap(y, "lon", 0, 1, True)
    state = (2, (2 * REACH + 3) * COLS, LANES)
    new_u, new_v, surface = call(
        substeps_kernel, [flat, flat, (COLS, LANES)], [state] * 16, y, near_a, near_z, star_u, star_v
    )
    return new_u.reshape(velocity_u.shape), new_v.reshape(velocity_v.shape), surface


def solution(mesh):
    return jax.shard_map(
        local,
        mesh=mesh,
        in_specs=(P(None, "lon", "lat"),) * 3 + (P("lon", "lat"),) * 5,
        out_specs=(P(None, "lon", "lat"), P(None, "lon", "lat"), P("lon", "lat")),
        check_vma=False,
    )
```

```python
import jax
import jax.numpy as jnp
import numpy as np
from jax import lax
from jax.experimental import pallas as pl
from jax.experimental.pallas import tpu as pltpu
from jax.sharding import PartitionSpec as P

SUBSTEPS = 30
LANES = 128
COLS = 8
RIM = 32
SLOTS = 4
CHUNKS = 4
REACH = 4
NEAR_ROWS = 9 * COLS
FAR_ROWS = 8 * COLS
TRIOS = (((2, 0, 21), (3, 43, 22), (0, 86, 21)), ((1, 0, 21), (4, 42, 21), (5, 84, 21)))
STEP = 6.0
VMEM_BYTES = 32 * 1024 * 1024


def thickness(levels):
    index = np.arange(levels, dtype=np.float32)
    return (np.float32(1.0) + np.float32(2.0) * index / np.float32(levels)) / np.float32(levels)


def lane_index():
    return lax.broadcasted_iota(jnp.int32, (COLS, LANES), 1)


def col_index():
    return lax.broadcasted_iota(jnp.int32, (COLS, LANES), 0)


def is_even(axis):
    return lax.rem(lax.axis_index(axis), 2) == 0


def level(k):
    return pl.ds(COLS * k, COLS)


def north(own, rim):
    last = lane_index() == LANES - 1
    a, b = pltpu.roll(own, LANES - 1, 1), pltpu.roll(rim, LANES - 1, 1)
    return jnp.where(last, b, a), jnp.where(last, a, b)


def south(own, rim):
    first = lane_index() == 0
    a, b = pltpu.roll(own, 1, 1), pltpu.roll(rim, 1, 1)
    return jnp.where(first, b, a), jnp.where(first, a, b)


def pair_rims(first, second):
    lane = lax.broadcasted_iota(jnp.int32, first.shape, 1)
    return jnp.where((lane >= RIM) & (lane < LANES - RIM), pltpu.roll(second, LANES // 2, 1), first)


def strips(parts, shifts):
    slot = lane_index() // RIM
    moved = [pltpu.roll(p, s, 1) if s else p for p, s in zip(parts, shifts)]
    return jnp.where(
        slot < 2, jnp.where(slot == 0, moved[0], moved[1]), jnp.where(slot == 2, moved[2], moved[3])
    )


def pack_rows_kernel(
    u_in, v_in, b_in, land_in, bottom_in, eta_in, wx_in, wy_in,
    a_ref, z_ref, u_ref, v_ref, b_ref, plane_ref, land_ref, bottom_ref, sems, plane_sem,
):
    levels = u_in.shape[0] // COLS
    groups = levels // SLOTS
    chunks = sems.shape[0]
    fields = ((u_in, u_ref), (v_in, v_ref), (b_in, b_ref))
    part = u_in.shape[0] // chunks
    copies = [
        [
            pltpu.make_async_copy(src.at[pl.ds(c * part, part)], dst.at[pl.ds(c * part, part)], sems.at[c, f])
            for f, (src, dst) in enumerate(fields)
        ]
        for c in range(chunks)
    ]
    planes = [
        pltpu.make_async_copy(src, dst, plane_sem.at[i])
        for i, (src, dst) in enumerate(
            (
                (land_in, land_ref), (bottom_in, bottom_ref), (eta_in, plane_ref.at[level(1)]),
                (wx_in, plane_ref.at[level(2)]), (wy_in, plane_ref.at[level(3)]),
            )
        )
    ]
    for copy in sum(copies, []) + planes:
        copy.start()
    even = is_even("lat")

    def send(at, parts):
        upper, lower = strips(parts, (32, 64, 96, 0)), strips(parts, (0, 32, 64, 96))
        a_ref[level(at), :] = jnp.where(even, upper, lower)
        z_ref[level(at), :] = jnp.where(even, lower, upper)

    for c in range(chunks):
        for f, (_, ref) in enumerate(fields):
            copies[c][f].wait()
            for g in range(c * groups // chunks, (c + 1) * groups // chunks):
                send(f * groups + g, [ref[level(SLOTS * g + s), :] for s in range(SLOTS)])
    for copy in planes:
        copy.wait()
    plane_ref[level(0), :] = (land_ref[...] * bottom_ref[...]).astype(jnp.float32)
    send(3 * groups, [plane_ref[level(s), :] for s in range(SLOTS)])


def pack_cols_kernel(
    u_ref, v_ref, b_ref, plane_ref, z_in, a_in,
    a_ref, z_ref, hu_ref, hv_ref, hplane_ref, p_ref, hp_ref,
):
    even = is_even("lat")
    upper = lane_index() < LANES // 2
    levels = u_ref.shape[0] // COLS
    thick = thickness(levels)
    groups = levels // SLOTS

    def receive(at, s):
        a, z = a_in[level(at), :], z_in[level(at), :]
        n, o = jnp.where(even, a, z), jnp.where(even, z, a)
        to_first, to_last = (LANES - RIM * s) % LANES, (LANES - RIM - RIM * s) % LANES
        n = pltpu.roll(n, to_first, 1) if to_first else n
        o = pltpu.roll(o, to_last, 1) if to_last else o
        return jnp.where(upper, n, o)

    own = rim = jnp.zeros((COLS, LANES), jnp.float32)
    for k in range(levels):
        dz = float(thick[k])
        hu_ref[level(k), :] = receive(k // SLOTS, k % SLOTS)
        hv_ref[level(k), :] = receive(groups + k // SLOTS, k % SLOTS)
        own = own + dz * b_ref[level(k), :]
        rim = rim + dz * receive(2 * groups + k // SLOTS, k % SLOTS)
        p_ref[level(k), :] = own
        hp_ref[level(k), :] = rim
    for s in range(SLOTS):
        hplane_ref[level(s), :] = receive(3 * groups, s)

    def edge(ref, col):
        return ref[pl.ds(col, levels, stride=COLS), :]

    def store(col, out_ref):
        own, rim = edge(u_ref, col), edge(hu_ref, col)
        if col == 0:
            own, rim = 0.05 * own - edge(p_ref, col), 0.05 * rim - edge(hp_ref, col)
        out_ref[pl.ds(0, levels), :] = own
        out_ref[pl.ds(levels, levels), :] = edge(v_ref, col)
        out_ref[pl.ds(2 * levels, levels), :] = pair_rims(rim, edge(hv_ref, col))
        out_ref[pl.ds(3 * levels, 1), :] = plane_ref[pl.ds(col, 1), :]
        out_ref[pl.ds(3 * levels + 1, 1), :] = hplane_ref[pl.ds(col, 1), :]
        out_ref[pl.ds(3 * levels + 2, 6), :] = jnp.zeros((6, LANES), jnp.float32)

    even_col = is_even("lon")

    @pl.when(even_col)
    def _():
        store(COLS - 1, a_ref)
        store(0, z_ref)

    @pl.when(jnp.logical_not(even_col))
    def _():
        store(0, a_ref)
        store(COLS - 1, z_ref)


def levels_kernel(
    u_ref, v_ref, hu_ref, hv_ref, p_ref, hp_ref, plane_ref, hplane_ref, z_in, a_in,
    far_ref, x_ref, su_ref, sv_ref, east_ref, west_ref,
):
    levels = u_ref.shape[0] // COLS
    thick = thickness(levels)
    even = is_even("lon")
    a, z = a_in[...], z_in[...]
    rows = a.shape[0]
    east_ref[pl.ds(0, rows), :] = jnp.where(even, a, z)
    west_ref[pl.ds(0, rows), :] = jnp.where(even, z, a)
    for ref in (east_ref, west_ref):
        ref[pl.ds(rows, levels), :] = pltpu.roll(ref[pl.ds(2 * levels, levels), :], LANES // 2, 1)
    U, V, W = (0, 2 * levels), (levels, rows), (3 * levels, 3 * levels + 1)
    col = col_index()
    top_col, bottom_col = col == COLS - 1, col == 0

    def row(ref, at):
        return jnp.broadcast_to(ref[pl.ds(at, 1), :], (COLS, LANES))

    def east(pair, places, k):
        return [
            jnp.where(top_col, row(east_ref, at + k), pltpu.roll(x, COLS - 1, 0)) for x, at in zip(pair, places)
        ]

    def west(pair, places, k):
        return [
            jnp.where(bottom_col, row(west_ref, at + k), pltpu.roll(x, 1, 0)) for x, at in zip(pair, places)
        ]

    water, eta, wx, wy = [(plane_ref[level(i), :], hplane_ref[level(i), :]) for i in range(SLOTS)]
    open_u = [jnp.minimum(w, e) for w, e in zip(water, east(water, W, 0))]
    open_v = [jnp.minimum(w, n) for w, n in zip(water, north(*water))]
    zero = jnp.zeros((COLS, LANES), jnp.float32)
    forcing_u, forcing_v = [zero, zero], [zero, zero]
    flow_u, flow_v = [zero, zero], [zero, zero]
    for k in range(levels):
        dz = float(thick[k])
        u = (u_ref[level(k), :], hu_ref[level(k), :])
        v = (v_ref[level(k), :], hv_ref[level(k), :])
        p = (p_ref[level(k), :], hp_ref[level(k), :])
        push_east = east([0.05 * u[t] - p[t] for t in range(2)], U, k)
        around_u = list(zip(west(u, U, k), north(*u), south(*u)))
        around_v = list(zip(east(v, V, k), west(v, V, k), north(*v), south(*v)))
        p_north = north(*p)
        for t in range(2):
            force_u = push_east[t] + (0.05 * (sum(around_u[t][1:], around_u[t][0]) - 4.0 * u[t]) + p[t])
            force_v = 0.05 * (sum(around_v[t][1:], around_v[t][0]) - 4.0 * v[t]) - (p_north[t] - p[t])
            if k == 0:
                force_u = force_u + wx[t] / dz
                force_v = force_v + wy[t] / dz
            wet_u, wet_v = open_u[t] > float(k), open_v[t] > float(k)
            force_u, vel_u = jnp.where(wet_u, force_u, 0.0), jnp.where(wet_u, u[t], 0.0)
            force_v, vel_v = jnp.where(wet_v, force_v, 0.0), jnp.where(wet_v, v[t], 0.0)
            forcing_u[t] = forcing_u[t] + dz * force_u
            forcing_v[t] = forcing_v[t] + dz * force_v
            flow_u[t] = flow_u[t] + dz * vel_u
            flow_v[t] = flow_v[t] + dz * vel_v
            if t == 0:
                su_ref[level(k), :] = vel_u + STEP * force_u
                sv_ref[level(k), :] = vel_v + STEP * force_v
    fields = (forcing_u, forcing_v, flow_u, flow_v, water, eta)
    for i, f in enumerate(fields):
        x_ref[level(i), :] = f[0]
        far_ref[level(i), :] = f[0]
    for i in range(3):
        x_ref[level(6 + i), :] = pair_rims(fields[2 * i][1], fields[2 * i + 1][1])
    for i, trio in enumerate(TRIOS):
        parts = [pltpu.roll(fields[f][1], at + count, 1) for f, at, count in trio]
        lane = lane_index()
        far_ref[level(6 + i), :] = jnp.where(
            lane < trio[1][1], parts[0], jnp.where(lane < trio[2][1], parts[1], parts[2])
        )


def depth_of(count, levels):
    return (count + count * (count - 1.0) * (1.0 / levels)) * (1.0 / levels)


def substeps_kernel(
    y_ref, a_in, z_in, x_ref, su_ref, sv_ref, out_u, out_v, out_eta,
    eta_ref, u_ref, v_ref, w_ref, fu_ref, fv_ref, du_ref, dv_ref, cu_ref, cv_ref, tw_ref, q_ref, t_ref,
    eta_north_ref, u_north_ref, tw_north_ref,
):
    levels = su_ref.shape[0] // COLS
    tau = STEP / SUBSTEPS
    blocks = 2 * REACH + 1
    even = is_even("lon")
    lane = lane_index()

    def at(p, shift=0):
        return pl.ds(COLS * (p + 1) + shift, COLS)

    places = (
        ((z_in, 2), (a_in, 0)), ((y_ref, 0), (y_ref, 2)), ((a_in, 2), (z_in, 0)),
        ((z_in, 1), (a_in, 1)), ((x_ref, 0), (x_ref, 0)), ((a_in, 1), (z_in, 1)),
        ((z_in, 0), (a_in, 2)), ((y_ref, 2), (y_ref, 0)), ((a_in, 0), (z_in, 2)),
    )
    for p, (for_even, for_odd) in enumerate(places):
        def tile(i):
            def read(place):
                ref, part = place
                start = 0
                if ref is not x_ref:
                    start = (0, FAR_ROWS, FAR_ROWS + NEAR_ROWS)[part]
                return ref[pl.ds(start + COLS * i, COLS), :]

            first = read(for_even)
            return first if p == REACH else jnp.where(even, first, read(for_odd))

        targets = (fu_ref, fv_ref, u_ref, v_ref, w_ref, eta_ref)
        for i, ref in enumerate(targets):
            value = tile(i)
            ref[0, at(p), :] = tau * value if i < 2 else value
        rims = [None] * 6
        if abs(p - REACH) <= 1:
            for i in range(3):
                rims[2 * i] = tile(6 + i)
                rims[2 * i + 1] = pltpu.roll(rims[2 * i], LANES // 2, 1)
        else:
            for i, trio in enumerate(TRIOS):
                shared = tile(6 + i)
                for f, first_lane, count in trio:
                    rims[f] = pltpu.roll(shared, LANES - first_lane - count, 1)
        for i, ref in enumerate(targets):
            ref[1, at(p), :] = tau * rims[i] if i < 2 else rims[i]

    total_rows = LANES * lax.axis_size("lat")
    base = (lax.axis_index("lat") * LANES).astype(jnp.float32)
    own_row = lane.astype(jnp.float32) + base
    rim_row = jnp.where(lane < LANES // 2, lane + LANES, lane - LANES).astype(jnp.float32) + base
    spin = [
        [0.25 * tau * 0.4 * (2.0 * (r + half) * (1.0 / total_rows) - 1.0) for half in (0.5, 1.0)]
        for r in (own_row, rim_row)
    ]
    for p in range(blocks):
        water = [w_ref[t, at(p), :] for t in range(2)]
        water_north = north(*water)
        eta_north = north(eta_ref[0, at(p), :], eta_ref[1, at(p), :])
        for t in range(2):
            eta_north_ref[t, at(p), :] = eta_north[t]
            tw_north_ref[t, at(p), :] = jnp.where(water_north[t] > 0.0, tau, 0.0)
            open_u = jnp.minimum(water[t], w_ref[t, at(p, 1), :])
            open_v = jnp.minimum(water[t], water_north[t])
            du_ref[t, at(p), :] = tau * depth_of(open_u, levels)
            dv_ref[t, at(p), :] = tau * depth_of(open_v, levels)
            cu_ref[t, at(p), :] = jnp.where(open_u > 0.0, spin[t][0], 0.0)
            cv_ref[t, at(p), :] = jnp.where(open_v > 0.0, spin[t][1], 0.0)
            tw_ref[t, at(p), :] = jnp.where(water[t] > 0.0, tau, 0.0)

    flow_u, flow_v = u_ref[0, at(REACH), :], v_ref[0, at(REACH), :]
    zero = jnp.zeros((COLS, LANES), jnp.float32)

    def substep(first, last):
        def body(_, carry):
            total_u, total_v = carry
            for p in range(first, last):
                u = [u_ref[t, at(p), :] for t in range(2)]
                u_west = [u_ref[t, at(p, -1), :] for t in range(2)]
                v = [v_ref[t, at(p), :] for t in range(2)]
                v_south, v_north, u_north = south(*v), north(*v), north(*u)
                for t in range(2):
                    u_north_ref[t, at(p), :] = u_north[t]
                for t in range(2):
                    u_north_west = u_north_ref[t, at(p, -1), :]
                    spread = (u[t] - u_west[t]) + (v[t] - v_south[t])
                    spread_north = (u_north[t] - u_north_west) + (v_north[t] - v[t])
                    eta_ref[t, at(p), :] = eta_ref[t, at(p), :] - tw_ref[t, at(p), :] * spread
                    eta_north_ref[t, at(p), :] = (
                        eta_north_ref[t, at(p), :] - tw_north_ref[t, at(p), :] * spread_north
                    )
                    q_ref[t, at(p), :] = v[t] + v_south[t]
                    t_ref[t, at(p), :] = (u[t] + u_west[t]) + (u_north[t] + u_north_west)
            for p in range(first, last):
                eta = [eta_ref[t, at(p), :] for t in range(2)]
                eta_north = [eta_north_ref[t, at(p), :] for t in range(2)]
                for t in range(2):
                    vbar = q_ref[t, at(p), :] + q_ref[t, at(p, 1), :]
                    rise_u = eta_ref[t, at(p, 1), :] - eta[t]
                    rise_v = eta_north[t] - eta[t]
                    next_u = (u_ref[t, at(p), :] + fu_ref[t, at(p), :]) + (
                        cu_ref[t, at(p), :] * vbar - du_ref[t, at(p), :] * rise_u
                    )
                    next_v = (v_ref[t, at(p), :] + fv_ref[t, at(p), :]) - (
                        cv_ref[t, at(p), :] * t_ref[t, at(p), :] + dv_ref[t, at(p), :] * rise_v
                    )
                    u_ref[t, at(p), :] = next_u
                    v_ref[t, at(p), :] = next_v
                    if p == REACH and t == 0:
                        total_u, total_v = total_u + next_u, total_v + next_v
            return total_u, total_v

        return body

    carry = (zero, zero)
    done = 0
    for ring in range(REACH):
        until = SUBSTEPS - COLS * (REACH - 1 - ring)
        carry = lax.fori_loop(0, until - done, substep(ring, blocks - ring), carry, unroll=2)
        done = until
    out_eta[...] = eta_ref[0, at(REACH), :]
    water = [w_ref[t, at(REACH), :] for t in range(2)]
    open_u = jnp.minimum(water[0], w_ref[0, at(REACH, 1), :])
    open_v = jnp.minimum(water[0], north(*water)[0])
    star_u = flow_u + (STEP / tau) * fu_ref[0, at(REACH), :]
    star_v = flow_v + (STEP / tau) * fv_ref[0, at(REACH), :]
    lift_u = (carry[0] / SUBSTEPS - star_u) / jnp.maximum(depth_of(open_u, levels), 0.25)
    lift_v = (carry[1] / SUBSTEPS - star_v) / jnp.maximum(depth_of(open_v, levels), 0.25)
    for k in range(levels):
        out_u[level(k), :] = su_ref[level(k), :] + jnp.where(open_u > float(k), lift_u, 0.0)
        out_v[level(k), :] = sv_ref[level(k), :] + jnp.where(open_v > float(k), lift_v, 0.0)


def call(kernel, shapes, scratch, *operands, **specs):
    return pl.pallas_call(
        kernel,
        out_shape=[jax.ShapeDtypeStruct(s, jnp.float32) for s in shapes],
        scratch_shapes=[pltpu.VMEM(s, jnp.float32) if isinstance(s, tuple) else s for s in scratch],
        compiler_params=pltpu.CompilerParams(vmem_limit_bytes=VMEM_BYTES),
        **specs,
    )(*operands)


def swap(x, axis, first, hop, wraps):
    count = lax.axis_size(axis)
    pairs = []
    for i in range(first, count, 2):
        j = i + hop
        if wraps or 0 <= j < count:
            pairs += [(i, j % count), (j % count, i)]
    return lax.ppermute(x, axis, pairs)


def local(velocity_u, velocity_v, buoyancy, wind_x, wind_y, free_surface, land_sea, bottom_level):
    levels = velocity_u.shape[0]
    flat = (levels * COLS, LANES)
    u, v, b = (a.reshape(flat) for a in (velocity_u, velocity_v, buoyancy))
    send = (3 * levels // SLOTS * COLS + COLS, LANES)
    inputs = (u, v, b, land_sea, bottom_level, free_surface, wind_x, wind_y)
    whole = pltpu.VMEM((COLS, LANES), jnp.int32)
    rows_a, rows_z, u, v, b, planes = call(
        pack_rows_kernel,
        [send, send, flat, flat, flat, (SLOTS * COLS, LANES)],
        [whole, whole, pltpu.SemaphoreType.DMA((CHUNKS, 3)), pltpu.SemaphoreType.DMA((5,))],
        *[pltpu.with_memory_space_constraint(a, pltpu.HBM) for a in inputs],
        in_specs=[pl.BlockSpec(memory_space=pltpu.HBM)] * 8,
    )
    rows_z = swap(rows_z, "lat", 1, 1, False)
    rows_a = swap(rows_a, "lat", 0, 1, False)
    edge = (3 * levels + 8, LANES)
    cols_a, cols_z, hu, hv, hplanes, p, hp = call(
        pack_cols_kernel,
        [edge, edge, flat, flat, (SLOTS * COLS, LANES), flat, flat], [],
        u, v, b, planes, rows_z, rows_a,
    )
    cols_z = swap(cols_z, "lon", 1, 1, True)
    cols_a = swap(cols_a, "lon", 0, 1, True)
    both = (edge[0] + levels, LANES)
    far, x, star_u, star_v = call(
        levels_kernel, [(FAR_ROWS, LANES), (NEAR_ROWS, LANES), flat, flat], [both, both],
        u, v, hu, hv, p, hp, planes, hplanes, cols_z, cols_a,
    )
    far_z = swap(far, "lon", 1, 3, True)
    far_a = swap(far, "lon", 0, 3, True)
    y = jnp.concatenate([far_z, x, far_a], 0)
    near_z = swap(y, "lon", 1, 1, True)
    near_a = swap(y, "lon", 0, 1, True)
    state = (2, (2 * REACH + 3) * COLS, LANES)
    new_u, new_v, surface = call(
        substeps_kernel, [flat, flat, (COLS, LANES)], [state] * 16, y, near_a, near_z, x, star_u, star_v
    )
    return new_u.reshape(velocity_u.shape), new_v.reshape(velocity_v.shape), surface


def solution(mesh):
    return jax.shard_map(
        local,
        mesh=mesh,
        in_specs=(P(None, "lon", "lat"),) * 3 + (P("lon", "lat"),) * 5,
        out_specs=(P(None, "lon", "lat"), P(None, "lon", "lat"), P("lon", "lat")),
        check_vma=False,
    )
```

```python
import jax
import jax.numpy as jnp
import numpy as np
from jax import lax
from jax.experimental import pallas as pl
from jax.experimental.pallas import tpu as pltpu
from jax.sharding import PartitionSpec as P

SUBSTEPS = 30
LANES = 128
COLS = 8
RIM = 32
SLOTS = 4
REACH = 4
BLOCKS = 2 * REACH + 1
FIELDS = 6
BLOCK_ROWS = FIELDS * COLS
RIM_TILES = -(-BLOCKS * FIELDS // SLOTS)
STEP = 6.0
VMEM_BYTES = 32 * 1024 * 1024


def thickness(levels):
    index = np.arange(levels, dtype=np.float32)
    return (np.float32(1.0) + np.float32(2.0) * index / np.float32(levels)) / np.float32(levels)


def lane_index():
    return lax.broadcasted_iota(jnp.int32, (COLS, LANES), 1)


def col_index():
    return lax.broadcasted_iota(jnp.int32, (COLS, LANES), 0)


def is_even(axis):
    return lax.rem(lax.axis_index(axis), 2) == 0


def level(k):
    return pl.ds(COLS * k, COLS)


def north(own, rim):
    last = lane_index() == LANES - 1
    a, b = pltpu.roll(own, LANES - 1, 1), pltpu.roll(rim, LANES - 1, 1)
    return jnp.where(last, b, a), jnp.where(last, a, b)


def south(own, rim):
    first = lane_index() == 0
    a, b = pltpu.roll(own, 1, 1), pltpu.roll(rim, 1, 1)
    return jnp.where(first, b, a), jnp.where(first, a, b)


def strips(parts, shifts):
    slot = lane_index() // RIM
    moved = [pltpu.roll(p, s, 1) if s else p for p, s in zip(parts, shifts)]
    return jnp.where(
        slot < 2, jnp.where(slot == 0, moved[0], moved[1]), jnp.where(slot == 2, moved[2], moved[3])
    )


def pack_edges_kernel(
    u_in, v_in, b_in, land_in, bottom_in, eta_in, wx_in, wy_in,
    col_a_ref, col_z_ref, row_a_ref, row_z_ref, u_ref, v_ref, p_ref, plane_ref,
    b_ref, land_ref, bottom_ref, sems,
):
    levels = u_in.shape[0] // COLS
    thick = thickness(levels)
    copies = [
        pltpu.make_async_copy(src, dst, sems.at[i])
        for i, (src, dst) in enumerate(
            (
                (u_in, u_ref), (v_in, v_ref), (b_in, b_ref), (land_in, land_ref), (bottom_in, bottom_ref),
                (eta_in, plane_ref.at[level(1)]), (wx_in, plane_ref.at[level(2)]), (wy_in, plane_ref.at[level(3)]),
            )
        )
    ]
    for copy in copies:
        copy.start()
    for copy in copies:
        copy.wait()
    lane = lane_index()
    water = (land_ref[...] * bottom_ref[...]).astype(jnp.float32)
    plane_ref[level(0), :] = water
    upper = jnp.zeros((COLS, LANES), jnp.float32)
    lower = jnp.where(lane == 2 * levels, pltpu.roll(water, 2 * levels, 1), 0.0)
    p = jnp.zeros((COLS, LANES), jnp.float32)
    for k in range(levels):
        u, v = u_ref[level(k), :], v_ref[level(k), :]
        p = p + float(thick[k]) * b_ref[level(k), :]
        p_ref[level(k), :] = p
        for at, up, low in ((k, u, u), (levels + k, v, 0.05 * v - p)):
            upper = jnp.where(lane == at, pltpu.roll(up, at + 1, 1), upper)
            lower = jnp.where(lane == at, pltpu.roll(low, at, 1) if at else low, lower)
    even_row = is_even("lat")
    row_a_ref[...] = jnp.where(even_row, upper, lower)
    row_z_ref[...] = jnp.where(even_row, lower, upper)

    def edge(ref, col):
        return ref[pl.ds(col, levels, stride=COLS), :]

    def store(col, out_ref):
        first = edge(u_ref, col)
        out_ref[pl.ds(0, levels), :] = first if col else 0.05 * first - edge(p_ref, col)
        out_ref[pl.ds(levels, levels), :] = edge(v_ref, col)
        out_ref[pl.ds(2 * levels, COLS), :] = water

    even_col = is_even("lon")

    @pl.when(even_col)
    def _():
        store(COLS - 1, col_a_ref)
        store(0, col_z_ref)

    @pl.when(jnp.logical_not(even_col))
    def _():
        store(0, col_a_ref)
        store(COLS - 1, col_z_ref)


def levels_kernel(
    u_ref, v_ref, p_ref, plane_ref, col_z, col_a, row_z, row_a, x_ref, su_ref, sv_ref, east_ref, west_ref
):
    levels = u_ref.shape[0] // COLS
    thick = thickness(levels)
    even_col, even_row = is_even("lon"), is_even("lat")
    east_ref[...] = jnp.where(even_col, col_a[...], col_z[...])
    west_ref[...] = jnp.where(even_col, col_z[...], col_a[...])
    from_north = jnp.where(even_row, row_a[...], row_z[...])
    from_south = jnp.where(even_row, row_z[...], row_a[...])
    col, lane = col_index(), lane_index()
    top_col, bottom_col = col == COLS - 1, col == 0
    top_row, bottom_row = lane == LANES - 1, lane == 0

    def row(ref, at):
        return jnp.broadcast_to(ref[pl.ds(at, 1), :], (COLS, LANES))

    def east(x, at):
        return jnp.where(top_col, row(east_ref, at), pltpu.roll(x, COLS - 1, 0))

    def west(x, at):
        return jnp.where(bottom_col, row(west_ref, at), pltpu.roll(x, 1, 0))

    def northern(x, at):
        return jnp.where(top_row, pltpu.roll(from_north, LANES - 1 - at, 1), pltpu.roll(x, LANES - 1, 1))

    def southern(x, at):
        edge = pltpu.roll(from_south, LANES - at, 1) if at else from_south
        return jnp.where(bottom_row, edge, pltpu.roll(x, 1, 1))

    water, eta, wx, wy = [plane_ref[level(i), :] for i in range(4)]
    open_u = jnp.minimum(water, east(water, 2 * levels))
    open_v = jnp.minimum(water, northern(water, 2 * levels))
    zero = jnp.zeros((COLS, LANES), jnp.float32)
    forcing_u = forcing_v = flow_u = flow_v = zero
    for k in range(levels):
        dz = float(thick[k])
        u, v, p = u_ref[level(k), :], v_ref[level(k), :], p_ref[level(k), :]
        force_u = east(0.05 * u - p, k) + (
            0.05 * (west(u, k) + northern(u, k) + southern(u, k) - 4.0 * u) + p
        )
        force_v = northern(0.05 * v - p, levels + k) + (
            0.05 * (east(v, levels + k) + west(v, levels + k) + southern(v, levels + k) - 4.0 * v) + p
        )
        if k == 0:
            force_u = force_u + wx / dz
            force_v = force_v + wy / dz
        wet_u, wet_v = open_u > float(k), open_v > float(k)
        force_u, vel_u = jnp.where(wet_u, force_u, 0.0), jnp.where(wet_u, u, 0.0)
        force_v, vel_v = jnp.where(wet_v, force_v, 0.0), jnp.where(wet_v, v, 0.0)
        forcing_u = forcing_u + dz * force_u
        forcing_v = forcing_v + dz * force_v
        flow_u = flow_u + dz * vel_u
        flow_v = flow_v + dz * vel_v
        su_ref[level(k), :] = vel_u + STEP * force_u
        sv_ref[level(k), :] = vel_v + STEP * force_v
    for i, f in enumerate((forcing_u, forcing_v, flow_u, flow_v, water, eta)):
        x_ref[level(i), :] = f


def pack_rims_kernel(y_ref, a_in, z_in, own_ref, row_a_ref, row_z_ref):
    even_col, even_row = is_even("lon"), is_even("lat")
    places = (
        ((z_in, 2), (a_in, 0)), ((y_ref, 0), (y_ref, 2)), ((a_in, 2), (z_in, 0)),
        ((z_in, 1), (a_in, 1)), ((y_ref, 1), (y_ref, 1)), ((a_in, 1), (z_in, 1)),
        ((z_in, 0), (a_in, 2)), ((y_ref, 2), (y_ref, 0)), ((a_in, 0), (z_in, 2)),
    )
    parts = []
    for p, sources in enumerate(places):
        for f in range(FIELDS):
            even, odd = [ref[pl.ds(part * BLOCK_ROWS + COLS * f, COLS), :] for ref, part in sources]
            value = even if p == REACH else jnp.where(even_col, even, odd)
            own_ref[level(f * BLOCKS + p), :] = value
            parts.append(value)
    parts += parts[: RIM_TILES * SLOTS - len(parts)]
    for t in range(RIM_TILES):
        group = parts[SLOTS * t : SLOTS * (t + 1)]
        upper, lower = strips(group, (32, 64, 96, 0)), strips(group, (0, 32, 64, 96))
        row_a_ref[level(t), :] = jnp.where(even_row, upper, lower)
        row_z_ref[level(t), :] = jnp.where(even_row, lower, upper)


def depth_of(count, levels):
    return (count + count * (count - 1.0) * (1.0 / levels)) * (1.0 / levels)


def substeps_kernel(
    own_ref, z_in, a_in, su_ref, sv_ref, out_u, out_v, out_eta,
    eta_ref, u_ref, v_ref, w_ref, fu_ref, fv_ref, du_ref, dv_ref, cu_ref, cv_ref, tw_ref, q_ref, t_ref,
    eta_north_ref, u_north_ref, tw_north_ref,
):
    levels = su_ref.shape[0] // COLS
    tau = STEP / SUBSTEPS
    even_row = is_even("lat")
    lane = lane_index()
    northern = lane < LANES // 2

    def at(p, shift=0):
        return pl.ds(COLS * (p + 1) + shift, COLS)

    def rim(q):
        a, z, s = a_in[level(q // SLOTS), :], z_in[level(q // SLOTS), :], q % SLOTS
        n, o = jnp.where(even_row, a, z), jnp.where(even_row, z, a)
        n = pltpu.roll(n, LANES - RIM * s, 1) if s else n
        o = pltpu.roll(o, LANES - RIM - RIM * s, 1) if s < SLOTS - 1 else o
        return jnp.where(northern, n, o)

    for p in range(BLOCKS):
        for f, ref in enumerate((fu_ref, fv_ref, u_ref, v_ref, w_ref, eta_ref)):
            pair = own_ref[level(f * BLOCKS + p), :], rim(FIELDS * p + f)
            for t in range(2):
                ref[t, at(p), :] = tau * pair[t] if f < 2 else pair[t]

    total_rows = LANES * lax.axis_size("lat")
    base = (lax.axis_index("lat") * LANES).astype(jnp.float32)
    own_row = lane.astype(jnp.float32) + base
    rim_row = jnp.where(lane < LANES // 2, lane + LANES, lane - LANES).astype(jnp.float32) + base
    spin = [
        [0.25 * tau * 0.4 * (2.0 * (r + half) * (1.0 / total_rows) - 1.0) for half in (0.5, 1.0)]
        for r in (own_row, rim_row)
    ]
    for p in range(BLOCKS):
        water = [w_ref[t, at(p), :] for t in range(2)]
        water_north = north(*water)
        eta_north = north(eta_ref[0, at(p), :], eta_ref[1, at(p), :])
        for t in range(2):
            eta_north_ref[t, at(p), :] = eta_north[t]
            tw_north_ref[t, at(p), :] = jnp.where(water_north[t] > 0.0, tau, 0.0)
            open_u = jnp.minimum(water[t], w_ref[t, at(p, 1), :])
            open_v = jnp.minimum(water[t], water_north[t])
            du_ref[t, at(p), :] = tau * depth_of(open_u, levels)
            dv_ref[t, at(p), :] = tau * depth_of(open_v, levels)
            cu_ref[t, at(p), :] = jnp.where(open_u > 0.0, spin[t][0], 0.0)
            cv_ref[t, at(p), :] = jnp.where(open_v > 0.0, spin[t][1], 0.0)
            tw_ref[t, at(p), :] = jnp.where(water[t] > 0.0, tau, 0.0)

    flow_u, flow_v = u_ref[0, at(REACH), :], v_ref[0, at(REACH), :]
    zero = jnp.zeros((COLS, LANES), jnp.float32)

    def substep(first, last):
        def body(_, carry):
            total_u, total_v = carry
            for p in range(first, last):
                u = [u_ref[t, at(p), :] for t in range(2)]
                u_west = [u_ref[t, at(p, -1), :] for t in range(2)]
                v = [v_ref[t, at(p), :] for t in range(2)]
                v_south, v_north, u_north = south(*v), north(*v), north(*u)
                for t in range(2):
                    u_north_ref[t, at(p), :] = u_north[t]
                for t in range(2):
                    u_north_west = u_north_ref[t, at(p, -1), :]
                    spread = (u[t] - u_west[t]) + (v[t] - v_south[t])
                    spread_north = (u_north[t] - u_north_west) + (v_north[t] - v[t])
                    eta_ref[t, at(p), :] = eta_ref[t, at(p), :] - tw_ref[t, at(p), :] * spread
                    eta_north_ref[t, at(p), :] = (
                        eta_north_ref[t, at(p), :] - tw_north_ref[t, at(p), :] * spread_north
                    )
                    q_ref[t, at(p), :] = v[t] + v_south[t]
                    t_ref[t, at(p), :] = (u[t] + u_west[t]) + (u_north[t] + u_north_west)
            for p in range(first, last):
                eta = [eta_ref[t, at(p), :] for t in range(2)]
                eta_north = [eta_north_ref[t, at(p), :] for t in range(2)]
                for t in range(2):
                    vbar = q_ref[t, at(p), :] + q_ref[t, at(p, 1), :]
                    rise_u = eta_ref[t, at(p, 1), :] - eta[t]
                    rise_v = eta_north[t] - eta[t]
                    next_u = (u_ref[t, at(p), :] + fu_ref[t, at(p), :]) + (
                        cu_ref[t, at(p), :] * vbar - du_ref[t, at(p), :] * rise_u
                    )
                    next_v = (v_ref[t, at(p), :] + fv_ref[t, at(p), :]) - (
                        cv_ref[t, at(p), :] * t_ref[t, at(p), :] + dv_ref[t, at(p), :] * rise_v
                    )
                    u_ref[t, at(p), :] = next_u
                    v_ref[t, at(p), :] = next_v
                    if p == REACH and t == 0:
                        total_u, total_v = total_u + next_u, total_v + next_v
            return total_u, total_v

        return body

    carry = (zero, zero)
    done = 0
    for ring in range(REACH):
        until = SUBSTEPS - COLS * (REACH - 1 - ring)
        carry = lax.fori_loop(0, until - done, substep(ring, BLOCKS - ring), carry, unroll=2)
        done = until
    out_eta[...] = eta_ref[0, at(REACH), :]
    water = [w_ref[t, at(REACH), :] for t in range(2)]
    open_u = jnp.minimum(water[0], w_ref[0, at(REACH, 1), :])
    open_v = jnp.minimum(water[0], north(*water)[0])
    star_u = flow_u + (STEP / tau) * fu_ref[0, at(REACH), :]
    star_v = flow_v + (STEP / tau) * fv_ref[0, at(REACH), :]
    lift_u = (carry[0] / SUBSTEPS - star_u) / jnp.maximum(depth_of(open_u, levels), 0.25)
    lift_v = (carry[1] / SUBSTEPS - star_v) / jnp.maximum(depth_of(open_v, levels), 0.25)
    for k in range(levels):
        out_u[level(k), :] = su_ref[level(k), :] + jnp.where(open_u > float(k), lift_u, 0.0)
        out_v[level(k), :] = sv_ref[level(k), :] + jnp.where(open_v > float(k), lift_v, 0.0)


def call(kernel, shapes, scratch, *operands, **specs):
    return pl.pallas_call(
        kernel,
        out_shape=[jax.ShapeDtypeStruct(s, jnp.float32) for s in shapes],
        scratch_shapes=[pltpu.VMEM(s, jnp.float32) if isinstance(s, tuple) else s for s in scratch],
        compiler_params=pltpu.CompilerParams(vmem_limit_bytes=VMEM_BYTES),
        **specs,
    )(*operands)


def swap(x, axis, first, hop, wraps):
    count = lax.axis_size(axis)
    pairs = []
    for i in range(first, count, 2):
        j = i + hop
        if wraps or 0 <= j < count:
            pairs += [(i, j % count), (j % count, i)]
    return lax.ppermute(x, axis, pairs)


def local(velocity_u, velocity_v, buoyancy, wind_x, wind_y, free_surface, land_sea, bottom_level):
    levels = velocity_u.shape[0]
    flat = (levels * COLS, LANES)
    u, v, b = (a.reshape(flat) for a in (velocity_u, velocity_v, buoyancy))
    inputs = (u, v, b, land_sea, bottom_level, free_surface, wind_x, wind_y)
    edge, tile = (2 * levels + COLS, LANES), (COLS, LANES)
    whole = pltpu.VMEM(tile, jnp.int32)
    col_a, col_z, row_a, row_z, u, v, p, planes = call(
        pack_edges_kernel,
        [edge, edge, tile, tile, flat, flat, flat, (4 * COLS, LANES)],
        [flat, whole, whole, pltpu.SemaphoreType.DMA((len(inputs),))],
        *[pltpu.with_memory_space_constraint(a, pltpu.HBM) for a in inputs],
        in_specs=[pl.BlockSpec(memory_space=pltpu.HBM)] * len(inputs),
    )
    col_z = swap(col_z, "lon", 1, 1, True)
    col_a = swap(col_a, "lon", 0, 1, True)
    row_z = swap(row_z, "lat", 1, 1, False)
    row_a = swap(row_a, "lat", 0, 1, False)
    x, star_u, star_v = call(
        levels_kernel, [(BLOCK_ROWS, LANES), flat, flat], [edge, edge],
        u, v, p, planes, col_z, col_a, row_z, row_a,
    )
    far_z = swap(x, "lon", 1, 3, True)
    far_a = swap(x, "lon", 0, 3, True)
    y = jnp.concatenate([far_z, x, far_a], 0)
    near_z = swap(y, "lon", 1, 1, True)
    near_a = swap(y, "lon", 0, 1, True)
    rims = (RIM_TILES * COLS, LANES)
    own, rim_a, rim_z = call(
        pack_rims_kernel, [(FIELDS * BLOCKS * COLS, LANES), rims, rims], [], y, near_a, near_z
    )
    rim_z = swap(rim_z, "lat", 1, 1, False)
    rim_a = swap(rim_a, "lat", 0, 1, False)
    state = (2, (2 * REACH + 3) * COLS, LANES)
    new_u, new_v, surface = call(
        substeps_kernel, [flat, flat, tile], [state] * 16, own, rim_z, rim_a, star_u, star_v
    )
    return new_u.reshape(velocity_u.shape), new_v.reshape(velocity_v.shape), surface


def solution(mesh):
    return jax.shard_map(
        local,
        mesh=mesh,
        in_specs=(P(None, "lon", "lat"),) * 3 + (P("lon", "lat"),) * 5,
        out_specs=(P(None, "lon", "lat"), P(None, "lon", "lat"), P("lon", "lat")),
        check_vma=False,
    )
```

```python
import jax
import jax.numpy as jnp
import numpy as np
from jax import lax
from jax.experimental import pallas as pl
from jax.experimental.pallas import tpu as pltpu
from jax.sharding import PartitionSpec as P

SUBSTEPS = 30
LANES = 128
COLS = 8
RIM = 32
SLOTS = 4
REACH = 4
NEAR_ROWS = 9 * COLS
FAR_ROWS = 8 * COLS
TRIOS = (((2, 0, 21), (3, 43, 22), (0, 86, 21)), ((1, 0, 21), (4, 42, 21), (5, 84, 21)))
STEP = 6.0
VMEM_BYTES = 32 * 1024 * 1024


def thickness(levels):
    index = np.arange(levels, dtype=np.float32)
    return (np.float32(1.0) + np.float32(2.0) * index / np.float32(levels)) / np.float32(levels)


def lane_index():
    return lax.broadcasted_iota(jnp.int32, (COLS, LANES), 1)


def col_index():
    return lax.broadcasted_iota(jnp.int32, (COLS, LANES), 0)


def is_even(axis):
    return lax.rem(lax.axis_index(axis), 2) == 0


def level(k):
    return pl.ds(COLS * k, COLS)


def north(own, rim):
    last = lane_index() == LANES - 1
    a, b = pltpu.roll(own, LANES - 1, 1), pltpu.roll(rim, LANES - 1, 1)
    return jnp.where(last, b, a), jnp.where(last, a, b)


def south(own, rim):
    first = lane_index() == 0
    a, b = pltpu.roll(own, 1, 1), pltpu.roll(rim, 1, 1)
    return jnp.where(first, b, a), jnp.where(first, a, b)


def pair_rims(first, second):
    lane = lax.broadcasted_iota(jnp.int32, first.shape, 1)
    return jnp.where((lane >= RIM) & (lane < LANES - RIM), pltpu.roll(second, LANES // 2, 1), first)


def strips(parts, shifts):
    slot = lax.broadcasted_iota(jnp.int32, parts[0].shape, 1) // RIM
    moved = [pltpu.roll(p, s, 1) if s else p for p, s in zip(parts, shifts)]
    return jnp.where(
        slot < 2, jnp.where(slot == 0, moved[0], moved[1]), jnp.where(slot == 2, moved[2], moved[3])
    )


def pack_edges_kernel(
    u_in, v_in, b_in, land_in, bottom_in, eta_in, wx_in, wy_in,
    col_a_ref, col_z_ref, u_ref, v_ref, p_ref, plane_ref,
    b_ref, land_ref, bottom_ref, sems,
):
    levels = u_in.shape[0] // COLS
    thick = thickness(levels)
    copies = [
        pltpu.make_async_copy(src, dst, sems.at[i])
        for i, (src, dst) in enumerate(
            (
                (u_in, u_ref), (v_in, v_ref), (b_in, b_ref), (land_in, land_ref), (bottom_in, bottom_ref),
                (eta_in, plane_ref.at[level(1)]), (wx_in, plane_ref.at[level(2)]), (wy_in, plane_ref.at[level(3)]),
            )
        )
    ]
    for copy in copies:
        copy.start()
    for copy in copies:
        copy.wait()
    water = (land_ref[...] * bottom_ref[...]).astype(jnp.float32)
    plane_ref[level(0), :] = water
    p = jnp.zeros((COLS, LANES), jnp.float32)
    for k in range(levels):
        p = p + float(thick[k]) * b_ref[level(k), :]
        p_ref[level(k), :] = p

    def edge(ref, col):
        return ref[pl.ds(col, levels, stride=COLS), :]

    def store(col, out_ref):
        first = edge(u_ref, col)
        out_ref[pl.ds(0, levels), :] = first if col else 0.05 * first - edge(p_ref, col)
        out_ref[pl.ds(levels, levels), :] = edge(v_ref, col)
        out_ref[pl.ds(2 * levels, COLS), :] = water

    even_col = is_even("lon")

    @pl.when(even_col)
    def _():
        store(COLS - 1, col_a_ref)
        store(0, col_z_ref)

    @pl.when(jnp.logical_not(even_col))
    def _():
        store(0, col_a_ref)
        store(COLS - 1, col_z_ref)


def pack_rows_kernel(u_ref, v_ref, p_ref, plane_ref, a_ref, z_ref):
    even = is_even("lat")
    groups = u_ref.shape[0] // COLS // SLOTS

    def send(at, parts):
        upper, lower = strips(parts, (32, 64, 96, 0)), strips(parts, (0, 32, 64, 96))
        a_ref[level(at), :] = jnp.where(even, upper, lower)
        z_ref[level(at), :] = jnp.where(even, lower, upper)

    for f, ref in enumerate((u_ref, v_ref, p_ref)):
        for g in range(groups):
            send(f * groups + g, [ref[level(SLOTS * g + s), :] for s in range(SLOTS)])
    send(3 * groups, [plane_ref[level(s), :] for s in range(SLOTS)])


def pack_corners_kernel(rows_a, rows_z, col_z, col_a, a_ref, z_ref):
    even_row, even_col = is_even("lat"), is_even("lon")
    a, z = col_a[...], col_z[...]
    east, west = jnp.where(even_col, a, z), jnp.where(even_col, z, a)
    levels = (a.shape[0] - COLS) // 2
    done = rows_a.shape[0]
    a_ref[pl.ds(0, done), :] = rows_a[...]
    z_ref[pl.ds(0, done), :] = rows_z[...]

    def send(at, parts):
        upper, lower = strips(parts, (32, 64, 96, 0)), strips(parts, (0, 32, 64, 96))
        a_ref[pl.ds(at, parts[0].shape[0]), :] = jnp.where(even_row, upper, lower)
        z_ref[pl.ds(at, parts[0].shape[0]), :] = jnp.where(even_row, lower, upper)

    send(done, [east[:levels], east[levels : 2 * levels], west[:levels], west[levels : 2 * levels]])
    send(done + levels, [east[2 * levels :]] * SLOTS)


def levels_kernel(
    u_ref, v_ref, p_ref, plane_ref, col_z, col_a, z_in, a_in,
    far_ref, x_ref, su_ref, sv_ref, east_ref, west_ref,
):
    levels = u_ref.shape[0] // COLS
    thick = thickness(levels)
    groups = levels // SLOTS
    even_col, even_row = is_even("lon"), is_even("lat")

    def receive(at, s, rows=COLS):
        a, z = a_in[pl.ds(at, rows), :], z_in[pl.ds(at, rows), :]
        n, o = jnp.where(even_row, a, z), jnp.where(even_row, z, a)
        n = pltpu.roll(n, LANES - RIM * s, 1) if s else n
        o = pltpu.roll(o, LANES - RIM - RIM * s, 1) if s < SLOTS - 1 else o
        return jnp.where(lax.broadcasted_iota(jnp.int32, (rows, LANES), 1) < LANES // 2, n, o)

    a, z = col_a[...], col_z[...]
    rows = a.shape[0]
    corners = (3 * groups + 1) * COLS
    for i, (ref, value) in enumerate(
        ((east_ref, jnp.where(even_col, a, z)), (west_ref, jnp.where(even_col, z, a)))
    ):
        ref[pl.ds(0, rows), :] = value
        ref[pl.ds(rows, levels), :] = receive(corners, 2 * i, levels)
        ref[pl.ds(rows + levels, levels), :] = receive(corners, 2 * i + 1, levels)
        ref[pl.ds(rows + 2 * levels, COLS), :] = receive(corners + levels, 0)
    U, V, W = (0, rows), (levels, rows + levels), (2 * levels, rows + 2 * levels)
    col = col_index()
    top_col, bottom_col = col == COLS - 1, col == 0

    def row(ref, at):
        return jnp.broadcast_to(ref[pl.ds(at, 1), :], (COLS, LANES))

    def east(pair, places, k):
        return [
            jnp.where(top_col, row(east_ref, at + k), pltpu.roll(x, COLS - 1, 0)) for x, at in zip(pair, places)
        ]

    def west(pair, places, k):
        return [
            jnp.where(bottom_col, row(west_ref, at + k), pltpu.roll(x, 1, 0)) for x, at in zip(pair, places)
        ]

    water, eta, wx, wy = [(plane_ref[level(i), :], receive(3 * groups * COLS, i)) for i in range(SLOTS)]
    open_u = [jnp.minimum(w, e) for w, e in zip(water, east(water, W, 0))]
    open_v = [jnp.minimum(w, n) for w, n in zip(water, north(*water))]
    zero = jnp.zeros((COLS, LANES), jnp.float32)
    forcing_u, forcing_v = [zero, zero], [zero, zero]
    flow_u, flow_v = [zero, zero], [zero, zero]
    for k in range(levels):
        dz = float(thick[k])
        u, v, p = [
            (ref[level(k), :], receive((f * groups + k // SLOTS) * COLS, k % SLOTS))
            for f, ref in enumerate((u_ref, v_ref, p_ref))
        ]
        push_east = east([0.05 * u[t] - p[t] for t in range(2)], U, k)
        around_u = list(zip(west(u, U, k), north(*u), south(*u)))
        around_v = list(zip(east(v, V, k), west(v, V, k), north(*v), south(*v)))
        p_north = north(*p)
        for t in range(2):
            force_u = push_east[t] + (0.05 * (sum(around_u[t][1:], around_u[t][0]) - 4.0 * u[t]) + p[t])
            force_v = 0.05 * (sum(around_v[t][1:], around_v[t][0]) - 4.0 * v[t]) - (p_north[t] - p[t])
            if k == 0:
                force_u = force_u + wx[t] / dz
                force_v = force_v + wy[t] / dz
            wet_u, wet_v = open_u[t] > float(k), open_v[t] > float(k)
            force_u, vel_u = jnp.where(wet_u, force_u, 0.0), jnp.where(wet_u, u[t], 0.0)
            force_v, vel_v = jnp.where(wet_v, force_v, 0.0), jnp.where(wet_v, v[t], 0.0)
            forcing_u[t] = forcing_u[t] + dz * force_u
            forcing_v[t] = forcing_v[t] + dz * force_v
            flow_u[t] = flow_u[t] + dz * vel_u
            flow_v[t] = flow_v[t] + dz * vel_v
            if t == 0:
                su_ref[level(k), :] = vel_u + STEP * force_u
                sv_ref[level(k), :] = vel_v + STEP * force_v
    fields = (forcing_u, forcing_v, flow_u, flow_v, water, eta)
    for i, f in enumerate(fields):
        x_ref[level(i), :] = f[0]
        far_ref[level(i), :] = f[0]
    for i in range(3):
        x_ref[level(6 + i), :] = pair_rims(fields[2 * i][1], fields[2 * i + 1][1])
    for i, trio in enumerate(TRIOS):
        parts = [pltpu.roll(fields[f][1], at + count, 1) for f, at, count in trio]
        lane = lane_index()
        far_ref[level(6 + i), :] = jnp.where(
            lane < trio[1][1], parts[0], jnp.where(lane < trio[2][1], parts[1], parts[2])
        )


def depth_of(count, levels):
    return (count + count * (count - 1.0) * (1.0 / levels)) * (1.0 / levels)


def substeps_kernel(
    y_ref, a_in, z_in, x_ref, su_ref, sv_ref, out_u, out_v, out_eta,
    eta_ref, u_ref, v_ref, w_ref, fu_ref, fv_ref, du_ref, dv_ref, cu_ref, cv_ref, tw_ref, q_ref, t_ref,
    eta_north_ref, u_north_ref, tw_north_ref,
):
    levels = su_ref.shape[0] // COLS
    tau = STEP / SUBSTEPS
    blocks = 2 * REACH + 1
    even = is_even("lon")
    lane = lane_index()

    def at(p, shift=0):
        return pl.ds(COLS * (p + 1) + shift, COLS)

    places = (
        ((z_in, 2), (a_in, 0)), ((y_ref, 0), (y_ref, 2)), ((a_in, 2), (z_in, 0)),
        ((z_in, 1), (a_in, 1)), ((x_ref, 0), (x_ref, 0)), ((a_in, 1), (z_in, 1)),
        ((z_in, 0), (a_in, 2)), ((y_ref, 2), (y_ref, 0)), ((a_in, 0), (z_in, 2)),
    )
    for p, (for_even, for_odd) in enumerate(places):
        def tile(i):
            def read(place):
                ref, part = place
                start = 0
                if ref is not x_ref:
                    start = (0, FAR_ROWS, FAR_ROWS + NEAR_ROWS)[part]
                return ref[pl.ds(start + COLS * i, COLS), :]

            first = read(for_even)
            return first if p == REACH else jnp.where(even, first, read(for_odd))

        targets = (fu_ref, fv_ref, u_ref, v_ref, w_ref, eta_ref)
        for i, ref in enumerate(targets):
            value = tile(i)
            ref[0, at(p), :] = tau * value if i < 2 else value
        rims = [None] * 6
        if abs(p - REACH) <= 1:
            for i in range(3):
                rims[2 * i] = tile(6 + i)
                rims[2 * i + 1] = pltpu.roll(rims[2 * i], LANES // 2, 1)
        else:
            for i, trio in enumerate(TRIOS):
                shared = tile(6 + i)
                for f, first_lane, count in trio:
                    rims[f] = pltpu.roll(shared, LANES - first_lane - count, 1)
        for i, ref in enumerate(targets):
            ref[1, at(p), :] = tau * rims[i] if i < 2 else rims[i]

    total_rows = LANES * lax.axis_size("lat")
    base = (lax.axis_index("lat") * LANES).astype(jnp.float32)
    own_row = lane.astype(jnp.float32) + base
    rim_row = jnp.where(lane < LANES // 2, lane + LANES, lane - LANES).astype(jnp.float32) + base
    spin = [
        [0.25 * tau * 0.4 * (2.0 * (r + half) * (1.0 / total_rows) - 1.0) for half in (0.5, 1.0)]
        for r in (own_row, rim_row)
    ]
    for p in range(blocks):
        water = [w_ref[t, at(p), :] for t in range(2)]
        water_north = north(*water)
        eta_north = north(eta_ref[0, at(p), :], eta_ref[1, at(p), :])
        for t in range(2):
            eta_north_ref[t, at(p), :] = eta_north[t]
            tw_north_ref[t, at(p), :] = jnp.where(water_north[t] > 0.0, tau, 0.0)
            open_u = jnp.minimum(water[t], w_ref[t, at(p, 1), :])
            open_v = jnp.minimum(water[t], water_north[t])
            du_ref[t, at(p), :] = tau * depth_of(open_u, levels)
            dv_ref[t, at(p), :] = tau * depth_of(open_v, levels)
            cu_ref[t, at(p), :] = jnp.where(open_u > 0.0, spin[t][0], 0.0)
            cv_ref[t, at(p), :] = jnp.where(open_v > 0.0, spin[t][1], 0.0)
            tw_ref[t, at(p), :] = jnp.where(water[t] > 0.0, tau, 0.0)

    flow_u, flow_v = u_ref[0, at(REACH), :], v_ref[0, at(REACH), :]
    zero = jnp.zeros((COLS, LANES), jnp.float32)

    def substep(first, last):
        def body(_, carry):
            total_u, total_v = carry
            for p in range(first, last):
                u = [u_ref[t, at(p), :] for t in range(2)]
                u_west = [u_ref[t, at(p, -1), :] for t in range(2)]
                v = [v_ref[t, at(p), :] for t in range(2)]
                v_south, v_north, u_north = south(*v), north(*v), north(*u)
                for t in range(2):
                    u_north_ref[t, at(p), :] = u_north[t]
                for t in range(2):
                    u_north_west = u_north_ref[t, at(p, -1), :]
                    spread = (u[t] - u_west[t]) + (v[t] - v_south[t])
                    spread_north = (u_north[t] - u_north_west) + (v_north[t] - v[t])
                    eta_ref[t, at(p), :] = eta_ref[t, at(p), :] - tw_ref[t, at(p), :] * spread
                    eta_north_ref[t, at(p), :] = (
                        eta_north_ref[t, at(p), :] - tw_north_ref[t, at(p), :] * spread_north
                    )
                    q_ref[t, at(p), :] = v[t] + v_south[t]
                    t_ref[t, at(p), :] = (u[t] + u_west[t]) + (u_north[t] + u_north_west)
            for p in range(first, last):
                eta = [eta_ref[t, at(p), :] for t in range(2)]
                eta_north = [eta_north_ref[t, at(p), :] for t in range(2)]
                for t in range(2):
                    vbar = q_ref[t, at(p), :] + q_ref[t, at(p, 1), :]
                    rise_u = eta_ref[t, at(p, 1), :] - eta[t]
                    rise_v = eta_north[t] - eta[t]
                    next_u = (u_ref[t, at(p), :] + fu_ref[t, at(p), :]) + (
                        cu_ref[t, at(p), :] * vbar - du_ref[t, at(p), :] * rise_u
                    )
                    next_v = (v_ref[t, at(p), :] + fv_ref[t, at(p), :]) - (
                        cv_ref[t, at(p), :] * t_ref[t, at(p), :] + dv_ref[t, at(p), :] * rise_v
                    )
                    u_ref[t, at(p), :] = next_u
                    v_ref[t, at(p), :] = next_v
                    if p == REACH and t == 0:
                        total_u, total_v = total_u + next_u, total_v + next_v
            return total_u, total_v

        return body

    carry = (zero, zero)
    done = 0
    for ring in range(REACH):
        until = SUBSTEPS - COLS * (REACH - 1 - ring)
        carry = lax.fori_loop(0, until - done, substep(ring, blocks - ring), carry, unroll=2)
        done = until
    out_eta[...] = eta_ref[0, at(REACH), :]
    water = [w_ref[t, at(REACH), :] for t in range(2)]
    open_u = jnp.minimum(water[0], w_ref[0, at(REACH, 1), :])
    open_v = jnp.minimum(water[0], north(*water)[0])
    star_u = flow_u + (STEP / tau) * fu_ref[0, at(REACH), :]
    star_v = flow_v + (STEP / tau) * fv_ref[0, at(REACH), :]
    lift_u = (carry[0] / SUBSTEPS - star_u) / jnp.maximum(depth_of(open_u, levels), 0.25)
    lift_v = (carry[1] / SUBSTEPS - star_v) / jnp.maximum(depth_of(open_v, levels), 0.25)
    for k in range(levels):
        out_u[level(k), :] = su_ref[level(k), :] + jnp.where(open_u > float(k), lift_u, 0.0)
        out_v[level(k), :] = sv_ref[level(k), :] + jnp.where(open_v > float(k), lift_v, 0.0)


def call(kernel, shapes, scratch, *operands, **specs):
    return pl.pallas_call(
        kernel,
        out_shape=[jax.ShapeDtypeStruct(s, jnp.float32) for s in shapes],
        scratch_shapes=[pltpu.VMEM(s, jnp.float32) if isinstance(s, tuple) else s for s in scratch],
        compiler_params=pltpu.CompilerParams(vmem_limit_bytes=VMEM_BYTES),
        **specs,
    )(*operands)


def swap(x, axis, first, hop, wraps):
    count = lax.axis_size(axis)
    pairs = []
    for i in range(first, count, 2):
        j = i + hop
        if wraps or 0 <= j < count:
            pairs += [(i, j % count), (j % count, i)]
    return lax.ppermute(x, axis, pairs)


def local(velocity_u, velocity_v, buoyancy, wind_x, wind_y, free_surface, land_sea, bottom_level):
    levels = velocity_u.shape[0]
    flat = (levels * COLS, LANES)
    u, v, b = (a.reshape(flat) for a in (velocity_u, velocity_v, buoyancy))
    inputs = (u, v, b, land_sea, bottom_level, free_surface, wind_x, wind_y)
    edge, tile = (2 * levels + COLS, LANES), (COLS, LANES)
    whole = pltpu.VMEM(tile, jnp.int32)
    col_a, col_z, u, v, p, planes = call(
        pack_edges_kernel,
        [edge, edge, flat, flat, flat, (SLOTS * COLS, LANES)],
        [flat, whole, whole, pltpu.SemaphoreType.DMA((len(inputs),))],
        *[pltpu.with_memory_space_constraint(a, pltpu.HBM) for a in inputs],
        in_specs=[pl.BlockSpec(memory_space=pltpu.HBM)] * len(inputs),
    )
    col_z = swap(col_z, "lon", 1, 1, True)
    col_a = swap(col_a, "lon", 0, 1, True)
    rims = (3 * levels // SLOTS + 1) * COLS
    rows_a, rows_z = call(pack_rows_kernel, [(rims, LANES)] * 2, [], u, v, p, planes)
    rows_a, rows_z = call(
        pack_corners_kernel, [(rims + levels + COLS, LANES)] * 2, [], rows_a, rows_z, col_z, col_a
    )
    rows_z = swap(rows_z, "lat", 1, 1, False)
    rows_a = swap(rows_a, "lat", 0, 1, False)
    both = (2 * edge[0], LANES)
    far, x, star_u, star_v = call(
        levels_kernel, [(FAR_ROWS, LANES), (NEAR_ROWS, LANES), flat, flat], [both, both],
        u, v, p, planes, col_z, col_a, rows_z, rows_a,
    )
    far_z = swap(far, "lon", 1, 3, True)
    far_a = swap(far, "lon", 0, 3, True)
    y = jnp.concatenate([far_z, x, far_a], 0)
    near_z = swap(y, "lon", 1, 1, True)
    near_a = swap(y, "lon", 0, 1, True)
    state = (2, (2 * REACH + 3) * COLS, LANES)
    new_u, new_v, surface = call(
        substeps_kernel, [flat, flat, (COLS, LANES)], [state] * 16, y, near_a, near_z, x, star_u, star_v
    )
    return new_u.reshape(velocity_u.shape), new_v.reshape(velocity_v.shape), surface


def solution(mesh):
    return jax.shard_map(
        local,
        mesh=mesh,
        in_specs=(P(None, "lon", "lat"),) * 3 + (P("lon", "lat"),) * 5,
        out_specs=(P(None, "lon", "lat"), P(None, "lon", "lat"), P("lon", "lat")),
        check_vma=False,
    )
```

```python
import jax
import jax.numpy as jnp
import numpy as np
from jax import lax
from jax.experimental import pallas as pl
from jax.experimental.pallas import tpu as pltpu
from jax.sharding import PartitionSpec as P

SUBSTEPS = 30
LANES = 128
COLS = 8
RIM = 32
SLOTS = 4
REACH = 4
NEAR_ROWS = 9 * COLS
FAR_ROWS = 8 * COLS
TRIOS = (((2, 0, 21), (3, 43, 22), (0, 86, 21)), ((1, 0, 21), (4, 42, 21), (5, 84, 21)))
STEP = 6.0
VMEM_BYTES = 32 * 1024 * 1024


def thickness(levels):
    index = np.arange(levels, dtype=np.float32)
    return (np.float32(1.0) + np.float32(2.0) * index / np.float32(levels)) / np.float32(levels)


def lane_index():
    return lax.broadcasted_iota(jnp.int32, (COLS, LANES), 1)


def col_index():
    return lax.broadcasted_iota(jnp.int32, (COLS, LANES), 0)


def is_even(axis):
    return lax.rem(lax.axis_index(axis), 2) == 0


def level(k):
    return pl.ds(COLS * k, COLS)


def north(own, rim):
    last = lane_index() == LANES - 1
    a, b = pltpu.roll(own, LANES - 1, 1), pltpu.roll(rim, LANES - 1, 1)
    return jnp.where(last, b, a), jnp.where(last, a, b)


def south(own, rim):
    first = lane_index() == 0
    a, b = pltpu.roll(own, 1, 1), pltpu.roll(rim, 1, 1)
    return jnp.where(first, b, a), jnp.where(first, a, b)


def pair_rims(first, second):
    lane = lax.broadcasted_iota(jnp.int32, first.shape, 1)
    return jnp.where((lane >= RIM) & (lane < LANES - RIM), pltpu.roll(second, LANES // 2, 1), first)


def strips(parts, shifts):
    slot = lax.broadcasted_iota(jnp.int32, parts[0].shape, 1) // RIM
    moved = [pltpu.roll(p, s, 1) if s else p for p, s in zip(parts, shifts)]
    return jnp.where(
        slot < 2, jnp.where(slot == 0, moved[0], moved[1]), jnp.where(slot == 2, moved[2], moved[3])
    )


def pack_edges_kernel(
    u_in, v_in, b_in, land_in, bottom_in, eta_in, wx_in, wy_in,
    col_a_ref, col_z_ref, u_ref, v_ref, p_ref, plane_ref,
    b_ref, land_ref, bottom_ref, sems,
):
    levels = u_in.shape[0] // COLS
    thick = thickness(levels)
    copies = [
        pltpu.make_async_copy(src, dst, sems.at[i])
        for i, (src, dst) in enumerate(
            (
                (u_in, u_ref), (v_in, v_ref), (b_in, b_ref), (land_in, land_ref), (bottom_in, bottom_ref),
                (eta_in, plane_ref.at[level(1)]), (wx_in, plane_ref.at[level(2)]), (wy_in, plane_ref.at[level(3)]),
            )
        )
    ]
    for copy in copies:
        copy.start()
    for copy in copies:
        copy.wait()
    water = (land_ref[...] * bottom_ref[...]).astype(jnp.float32)
    plane_ref[level(0), :] = water
    p = jnp.zeros((COLS, LANES), jnp.float32)
    for k in range(levels):
        p = p + float(thick[k]) * b_ref[level(k), :]
        p_ref[level(k), :] = p

    def edge(ref, col):
        return ref[pl.ds(col, levels, stride=COLS), :]

    def store(col, out_ref):
        first = edge(u_ref, col)
        out_ref[pl.ds(0, levels), :] = first if col else 0.05 * first - edge(p_ref, col)
        out_ref[pl.ds(levels, levels), :] = edge(v_ref, col)
        out_ref[pl.ds(2 * levels, COLS), :] = water

    even_col = is_even("lon")

    @pl.when(even_col)
    def _():
        store(COLS - 1, col_a_ref)
        store(0, col_z_ref)

    @pl.when(jnp.logical_not(even_col))
    def _():
        store(0, col_a_ref)
        store(COLS - 1, col_z_ref)


def pack_rows_kernel(u_ref, v_ref, p_ref, plane_ref, a_ref, z_ref):
    even = is_even("lat")
    groups = u_ref.shape[0] // COLS // SLOTS

    def send(at, parts):
        upper, lower = strips(parts, (32, 64, 96, 0)), strips(parts, (0, 32, 64, 96))
        a_ref[level(at), :] = jnp.where(even, upper, lower)
        z_ref[level(at), :] = jnp.where(even, lower, upper)

    for f, ref in enumerate((u_ref, v_ref, p_ref)):
        for g in range(groups):
            send(f * groups + g, [ref[level(SLOTS * g + s), :] for s in range(SLOTS)])
    send(3 * groups, [plane_ref[level(s), :] for s in range(SLOTS)])


def pack_corners_kernel(rows_a, rows_z, col_z, col_a, a_ref, z_ref):
    even_row, even_col = is_even("lat"), is_even("lon")
    a, z = col_a[...], col_z[...]
    east, west = jnp.where(even_col, a, z), jnp.where(even_col, z, a)
    levels = (a.shape[0] - COLS) // 2
    done = rows_a.shape[0]
    a_ref[pl.ds(0, done), :] = rows_a[...]
    z_ref[pl.ds(0, done), :] = rows_z[...]

    def send(at, parts):
        upper, lower = strips(parts, (32, 64, 96, 0)), strips(parts, (0, 32, 64, 96))
        a_ref[pl.ds(at, parts[0].shape[0]), :] = jnp.where(even_row, upper, lower)
        z_ref[pl.ds(at, parts[0].shape[0]), :] = jnp.where(even_row, lower, upper)

    send(done, [east[:levels], east[levels : 2 * levels], west[:levels], west[levels : 2 * levels]])
    send(done + levels, [east[2 * levels :]] * SLOTS)


def levels_kernel(
    u_ref, v_ref, p_ref, plane_ref, col_z, col_a, z_in, a_in,
    far_ref, x_ref, su_ref, sv_ref, east_ref, west_ref, hu_ref, hv_ref, hp_ref,
):
    levels = u_ref.shape[0] // COLS
    thick = thickness(levels)
    groups = levels // SLOTS
    even_col, even_row = is_even("lon"), is_even("lat")

    def receive(at, s, rows=COLS):
        a, z = a_in[pl.ds(at, rows), :], z_in[pl.ds(at, rows), :]
        n, o = jnp.where(even_row, a, z), jnp.where(even_row, z, a)
        n = pltpu.roll(n, LANES - RIM * s, 1) if s else n
        o = pltpu.roll(o, LANES - RIM - RIM * s, 1) if s < SLOTS - 1 else o
        return jnp.where(lax.broadcasted_iota(jnp.int32, (rows, LANES), 1) < LANES // 2, n, o)

    a, z = col_a[...], col_z[...]
    rows = a.shape[0]
    corners = (3 * groups + 1) * COLS
    for i, (ref, value) in enumerate(
        ((east_ref, jnp.where(even_col, a, z)), (west_ref, jnp.where(even_col, z, a)))
    ):
        ref[pl.ds(0, rows), :] = value
        ref[pl.ds(rows, levels), :] = receive(corners, 2 * i, levels)
        ref[pl.ds(rows + levels, levels), :] = receive(corners, 2 * i + 1, levels)
        ref[pl.ds(rows + 2 * levels, COLS), :] = receive(corners + levels, 0)
    for f, ref in enumerate((hu_ref, hv_ref, hp_ref)):
        for k in range(levels):
            ref[level(k), :] = receive((f * groups + k // SLOTS) * COLS, k % SLOTS)
    U, V, W = (0, rows), (levels, rows + levels), (2 * levels, rows + 2 * levels)
    col = col_index()
    top_col, bottom_col = col == COLS - 1, col == 0

    def row(ref, at):
        return jnp.broadcast_to(ref[pl.ds(at, 1), :], (COLS, LANES))

    def east(pair, places, k):
        return [
            jnp.where(top_col, row(east_ref, at + k), pltpu.roll(x, COLS - 1, 0)) for x, at in zip(pair, places)
        ]

    def west(pair, places, k):
        return [
            jnp.where(bottom_col, row(west_ref, at + k), pltpu.roll(x, 1, 0)) for x, at in zip(pair, places)
        ]

    water, eta, wx, wy = [(plane_ref[level(i), :], receive(3 * groups * COLS, i)) for i in range(SLOTS)]
    open_u = [jnp.minimum(w, e) for w, e in zip(water, east(water, W, 0))]
    open_v = [jnp.minimum(w, n) for w, n in zip(water, north(*water))]
    zero = jnp.zeros((COLS, LANES), jnp.float32)
    forcing_u, forcing_v = [zero, zero], [zero, zero]
    flow_u, flow_v = [zero, zero], [zero, zero]
    for k in range(levels):
        dz = float(thick[k])
        u, v, p = [
            (own[level(k), :], rim[level(k), :])
            for own, rim in ((u_ref, hu_ref), (v_ref, hv_ref), (p_ref, hp_ref))
        ]
        push_east = east([0.05 * u[t] - p[t] for t in range(2)], U, k)
        around_u = list(zip(west(u, U, k), north(*u), south(*u)))
        around_v = list(zip(east(v, V, k), west(v, V, k), north(*v), south(*v)))
        p_north = north(*p)
        for t in range(2):
            force_u = push_east[t] + (0.05 * (sum(around_u[t][1:], around_u[t][0]) - 4.0 * u[t]) + p[t])
            force_v = 0.05 * (sum(around_v[t][1:], around_v[t][0]) - 4.0 * v[t]) - (p_north[t] - p[t])
            if k == 0:
                force_u = force_u + wx[t] / dz
                force_v = force_v + wy[t] / dz
            wet_u, wet_v = open_u[t] > float(k), open_v[t] > float(k)
            force_u, vel_u = jnp.where(wet_u, force_u, 0.0), jnp.where(wet_u, u[t], 0.0)
            force_v, vel_v = jnp.where(wet_v, force_v, 0.0), jnp.where(wet_v, v[t], 0.0)
            forcing_u[t] = forcing_u[t] + dz * force_u
            forcing_v[t] = forcing_v[t] + dz * force_v
            flow_u[t] = flow_u[t] + dz * vel_u
            flow_v[t] = flow_v[t] + dz * vel_v
            if t == 0:
                su_ref[level(k), :] = vel_u + STEP * force_u
                sv_ref[level(k), :] = vel_v + STEP * force_v
    fields = (forcing_u, forcing_v, flow_u, flow_v, water, eta)
    for i, f in enumerate(fields):
        x_ref[level(i), :] = f[0]
        far_ref[level(i), :] = f[0]
    for i in range(3):
        x_ref[level(6 + i), :] = pair_rims(fields[2 * i][1], fields[2 * i + 1][1])
    for i, trio in enumerate(TRIOS):
        parts = [pltpu.roll(fields[f][1], at + count, 1) for f, at, count in trio]
        lane = lane_index()
        far_ref[level(6 + i), :] = jnp.where(
            lane < trio[1][1], parts[0], jnp.where(lane < trio[2][1], parts[1], parts[2])
        )


def depth_of(count, levels):
    return (count + count * (count - 1.0) * (1.0 / levels)) * (1.0 / levels)


def substeps_kernel(
    y_ref, a_in, z_in, x_ref, su_ref, sv_ref, out_u, out_v, out_eta,
    eta_ref, u_ref, v_ref, w_ref, fu_ref, fv_ref, du_ref, dv_ref, cu_ref, cv_ref, tw_ref, q_ref, t_ref,
    eta_north_ref, u_north_ref, tw_north_ref,
):
    levels = su_ref.shape[0] // COLS
    tau = STEP / SUBSTEPS
    blocks = 2 * REACH + 1
    even = is_even("lon")
    lane = lane_index()

    def at(p, shift=0):
        return pl.ds(COLS * (p + 1) + shift, COLS)

    places = (
        ((z_in, 2), (a_in, 0)), ((y_ref, 0), (y_ref, 2)), ((a_in, 2), (z_in, 0)),
        ((z_in, 1), (a_in, 1)), ((x_ref, 0), (x_ref, 0)), ((a_in, 1), (z_in, 1)),
        ((z_in, 0), (a_in, 2)), ((y_ref, 2), (y_ref, 0)), ((a_in, 0), (z_in, 2)),
    )
    for p, (for_even, for_odd) in enumerate(places):
        def tile(i):
            def read(place):
                ref, part = place
                start = 0
                if ref is not x_ref:
                    start = (0, FAR_ROWS, FAR_ROWS + NEAR_ROWS)[part]
                return ref[pl.ds(start + COLS * i, COLS), :]

            first = read(for_even)
            return first if p == REACH else jnp.where(even, first, read(for_odd))

        targets = (fu_ref, fv_ref, u_ref, v_ref, w_ref, eta_ref)
        for i, ref in enumerate(targets):
            value = tile(i)
            ref[0, at(p), :] = tau * value if i < 2 else value
        rims = [None] * 6
        if abs(p - REACH) <= 1:
            for i in range(3):
                rims[2 * i] = tile(6 + i)
                rims[2 * i + 1] = pltpu.roll(rims[2 * i], LANES // 2, 1)
        else:
            for i, trio in enumerate(TRIOS):
                shared = tile(6 + i)
                for f, first_lane, count in trio:
                    rims[f] = pltpu.roll(shared, LANES - first_lane - count, 1)
        for i, ref in enumerate(targets):
            ref[1, at(p), :] = tau * rims[i] if i < 2 else rims[i]

    total_rows = LANES * lax.axis_size("lat")
    base = (lax.axis_index("lat") * LANES).astype(jnp.float32)
    own_row = lane.astype(jnp.float32) + base
    rim_row = jnp.where(lane < LANES // 2, lane + LANES, lane - LANES).astype(jnp.float32) + base
    spin = [
        [0.25 * tau * 0.4 * (2.0 * (r + half) * (1.0 / total_rows) - 1.0) for half in (0.5, 1.0)]
        for r in (own_row, rim_row)
    ]
    for p in range(blocks):
        water = [w_ref[t, at(p), :] for t in range(2)]
        water_north = north(*water)
        eta_north = north(eta_ref[0, at(p), :], eta_ref[1, at(p), :])
        for t in range(2):
            eta_north_ref[t, at(p), :] = eta_north[t]
            tw_north_ref[t, at(p), :] = jnp.where(water_north[t] > 0.0, tau, 0.0)
            open_u = jnp.minimum(water[t], w_ref[t, at(p, 1), :])
            open_v = jnp.minimum(water[t], water_north[t])
            du_ref[t, at(p), :] = tau * depth_of(open_u, levels)
            dv_ref[t, at(p), :] = tau * depth_of(open_v, levels)
            cu_ref[t, at(p), :] = jnp.where(open_u > 0.0, spin[t][0], 0.0)
            cv_ref[t, at(p), :] = jnp.where(open_v > 0.0, spin[t][1], 0.0)
            tw_ref[t, at(p), :] = jnp.where(water[t] > 0.0, tau, 0.0)

    flow_u, flow_v = u_ref[0, at(REACH), :], v_ref[0, at(REACH), :]
    zero = jnp.zeros((COLS, LANES), jnp.float32)

    def substep(first, last):
        def body(_, carry):
            total_u, total_v = carry
            for p in range(first, last):
                u = [u_ref[t, at(p), :] for t in range(2)]
                u_west = [u_ref[t, at(p, -1), :] for t in range(2)]
                v = [v_ref[t, at(p), :] for t in range(2)]
                v_south, v_north, u_north = south(*v), north(*v), north(*u)
                for t in range(2):
                    u_north_ref[t, at(p), :] = u_north[t]
                for t in range(2):
                    u_north_west = u_north_ref[t, at(p, -1), :]
                    spread = (u[t] - u_west[t]) + (v[t] - v_south[t])
                    spread_north = (u_north[t] - u_north_west) + (v_north[t] - v[t])
                    eta_ref[t, at(p), :] = eta_ref[t, at(p), :] - tw_ref[t, at(p), :] * spread
                    eta_north_ref[t, at(p), :] = (
                        eta_north_ref[t, at(p), :] - tw_north_ref[t, at(p), :] * spread_north
                    )
                    q_ref[t, at(p), :] = v[t] + v_south[t]
                    t_ref[t, at(p), :] = (u[t] + u_west[t]) + (u_north[t] + u_north_west)
            for p in range(first, last):
                eta = [eta_ref[t, at(p), :] for t in range(2)]
                eta_north = [eta_north_ref[t, at(p), :] for t in range(2)]
                for t in range(2):
                    vbar = q_ref[t, at(p), :] + q_ref[t, at(p, 1), :]
                    rise_u = eta_ref[t, at(p, 1), :] - eta[t]
                    rise_v = eta_north[t] - eta[t]
                    next_u = (u_ref[t, at(p), :] + fu_ref[t, at(p), :]) + (
                        cu_ref[t, at(p), :] * vbar - du_ref[t, at(p), :] * rise_u
                    )
                    next_v = (v_ref[t, at(p), :] + fv_ref[t, at(p), :]) - (
                        cv_ref[t, at(p), :] * t_ref[t, at(p), :] + dv_ref[t, at(p), :] * rise_v
                    )
                    u_ref[t, at(p), :] = next_u
                    v_ref[t, at(p), :] = next_v
                    if p == REACH and t == 0:
                        total_u, total_v = total_u + next_u, total_v + next_v
            return total_u, total_v

        return body

    carry = (zero, zero)
    done = 0
    for ring in range(REACH):
        until = SUBSTEPS - COLS * (REACH - 1 - ring)
        carry = lax.fori_loop(0, until - done, substep(ring, blocks - ring), carry, unroll=2)
        done = until
    out_eta[...] = eta_ref[0, at(REACH), :]
    water = [w_ref[t, at(REACH), :] for t in range(2)]
    open_u = jnp.minimum(water[0], w_ref[0, at(REACH, 1), :])
    open_v = jnp.minimum(water[0], north(*water)[0])
    star_u = flow_u + (STEP / tau) * fu_ref[0, at(REACH), :]
    star_v = flow_v + (STEP / tau) * fv_ref[0, at(REACH), :]
    lift_u = (carry[0] / SUBSTEPS - star_u) / jnp.maximum(depth_of(open_u, levels), 0.25)
    lift_v = (carry[1] / SUBSTEPS - star_v) / jnp.maximum(depth_of(open_v, levels), 0.25)
    for k in range(levels):
        out_u[level(k), :] = su_ref[level(k), :] + jnp.where(open_u > float(k), lift_u, 0.0)
        out_v[level(k), :] = sv_ref[level(k), :] + jnp.where(open_v > float(k), lift_v, 0.0)


def call(kernel, shapes, scratch, *operands, **specs):
    return pl.pallas_call(
        kernel,
        out_shape=[jax.ShapeDtypeStruct(s, jnp.float32) for s in shapes],
        scratch_shapes=[pltpu.VMEM(s, jnp.float32) if isinstance(s, tuple) else s for s in scratch],
        compiler_params=pltpu.CompilerParams(vmem_limit_bytes=VMEM_BYTES),
        **specs,
    )(*operands)


def swap(x, axis, first, hop, wraps):
    count = lax.axis_size(axis)
    pairs = []
    for i in range(first, count, 2):
        j = i + hop
        if wraps or 0 <= j < count:
            pairs += [(i, j % count), (j % count, i)]
    return lax.ppermute(x, axis, pairs)


def local(velocity_u, velocity_v, buoyancy, wind_x, wind_y, free_surface, land_sea, bottom_level):
    levels = velocity_u.shape[0]
    flat = (levels * COLS, LANES)
    u, v, b = (a.reshape(flat) for a in (velocity_u, velocity_v, buoyancy))
    inputs = (u, v, b, land_sea, bottom_level, free_surface, wind_x, wind_y)
    edge, tile = (2 * levels + COLS, LANES), (COLS, LANES)
    whole = pltpu.VMEM(tile, jnp.int32)
    col_a, col_z, u, v, p, planes = call(
        pack_edges_kernel,
        [edge, edge, flat, flat, flat, (SLOTS * COLS, LANES)],
        [flat, whole, whole, pltpu.SemaphoreType.DMA((len(inputs),))],
        *[pltpu.with_memory_space_constraint(a, pltpu.HBM) for a in inputs],
        in_specs=[pl.BlockSpec(memory_space=pltpu.HBM)] * len(inputs),
    )
    col_z = swap(col_z, "lon", 1, 1, True)
    col_a = swap(col_a, "lon", 0, 1, True)
    rims = (3 * levels // SLOTS + 1) * COLS
    rows_a, rows_z = call(pack_rows_kernel, [(rims, LANES)] * 2, [], u, v, p, planes)
    rows_a, rows_z = call(
        pack_corners_kernel, [(rims + levels + COLS, LANES)] * 2, [], rows_a, rows_z, col_z, col_a
    )
    rows_z = swap(rows_z, "lat", 1, 1, False)
    rows_a = swap(rows_a, "lat", 0, 1, False)
    both = (2 * edge[0], LANES)
    far, x, star_u, star_v = call(
        levels_kernel, [(FAR_ROWS, LANES), (NEAR_ROWS, LANES), flat, flat], [both, both, flat, flat, flat],
        u, v, p, planes, col_z, col_a, rows_z, rows_a,
    )
    far_z = swap(far, "lon", 1, 3, True)
    far_a = swap(far, "lon", 0, 3, True)
    y = jnp.concatenate([far_z, x, far_a], 0)
    near_z = swap(y, "lon", 1, 1, True)
    near_a = swap(y, "lon", 0, 1, True)
    state = (2, (2 * REACH + 3) * COLS, LANES)
    new_u, new_v, surface = call(
        substeps_kernel, [flat, flat, (COLS, LANES)], [state] * 16, y, near_a, near_z, x, star_u, star_v
    )
    return new_u.reshape(velocity_u.shape), new_v.reshape(velocity_v.shape), surface


def solution(mesh):
    return jax.shard_map(
        local,
        mesh=mesh,
        in_specs=(P(None, "lon", "lat"),) * 3 + (P("lon", "lat"),) * 5,
        out_specs=(P(None, "lon", "lat"), P(None, "lon", "lat"), P("lon", "lat")),
        check_vma=False,
    )
```

```python
import jax
import jax.numpy as jnp
import numpy as np
from jax import lax
from jax.experimental import pallas as pl
from jax.experimental.pallas import tpu as pltpu
from jax.sharding import PartitionSpec as P

SUBSTEPS = 30
LANES = 128
COLS = 8
RIM = 32
SLOTS = 4
REACH = 4
NEAR_ROWS = 9 * COLS
FAR_ROWS = 8 * COLS
TRIOS = (((2, 0, 21), (3, 43, 22), (0, 86, 21)), ((1, 0, 21), (4, 42, 21), (5, 84, 21)))
STEP = 6.0
VMEM_BYTES = 32 * 1024 * 1024


def thickness(levels):
    index = np.arange(levels, dtype=np.float32)
    return (np.float32(1.0) + np.float32(2.0) * index / np.float32(levels)) / np.float32(levels)


def lane_index():
    return lax.broadcasted_iota(jnp.int32, (COLS, LANES), 1)


def col_index():
    return lax.broadcasted_iota(jnp.int32, (COLS, LANES), 0)


def is_even(axis):
    return lax.rem(lax.axis_index(axis), 2) == 0


def level(k):
    return pl.ds(COLS * k, COLS)


def north(own, rim):
    last = lane_index() == LANES - 1
    a, b = pltpu.roll(own, LANES - 1, 1), pltpu.roll(rim, LANES - 1, 1)
    return jnp.where(last, b, a), jnp.where(last, a, b)


def south(own, rim):
    first = lane_index() == 0
    a, b = pltpu.roll(own, 1, 1), pltpu.roll(rim, 1, 1)
    return jnp.where(first, b, a), jnp.where(first, a, b)


def pair_rims(first, second):
    lane = lax.broadcasted_iota(jnp.int32, first.shape, 1)
    return jnp.where((lane >= RIM) & (lane < LANES - RIM), pltpu.roll(second, LANES // 2, 1), first)


def strips(parts):
    slot = lax.broadcasted_iota(jnp.int32, parts[0].shape, 1) // RIM
    moved = [pltpu.roll(p, RIM * s, 1) if s else p for s, p in enumerate(parts)]

    def choose(order):
        first, second, third, fourth = [moved[s] for s in order]
        return jnp.where(slot < 2, jnp.where(slot == 0, first, second), jnp.where(slot == 2, third, fourth))

    return choose((1, 2, 3, 0)), choose((0, 1, 2, 3))


def pack_edges_kernel(
    u_in, v_in, b_in, land_in, bottom_in, eta_in, wx_in, wy_in,
    col_a_ref, col_z_ref, u_ref, v_ref, p_ref, plane_ref,
    b_ref, land_ref, bottom_ref, sems,
):
    levels = u_in.shape[0] // COLS
    thick = thickness(levels)
    copies = [
        pltpu.make_async_copy(src, dst, sems.at[i])
        for i, (src, dst) in enumerate(
            (
                (u_in, u_ref), (v_in, v_ref), (b_in, b_ref), (land_in, land_ref), (bottom_in, bottom_ref),
                (eta_in, plane_ref.at[level(1)]), (wx_in, plane_ref.at[level(2)]), (wy_in, plane_ref.at[level(3)]),
            )
        )
    ]
    for copy in copies:
        copy.start()
    for copy in copies:
        copy.wait()
    water = (land_ref[...] * bottom_ref[...]).astype(jnp.float32)
    plane_ref[level(0), :] = water
    p = jnp.zeros((COLS, LANES), jnp.float32)
    for k in range(levels):
        p = p + float(thick[k]) * b_ref[level(k), :]
        p_ref[level(k), :] = p

    def edge(ref, col):
        return ref[pl.ds(col, levels, stride=COLS), :]

    def store(col, out_ref):
        first = edge(u_ref, col)
        out_ref[pl.ds(0, levels), :] = first if col else 0.05 * first - edge(p_ref, col)
        out_ref[pl.ds(levels, levels), :] = edge(v_ref, col)
        out_ref[pl.ds(2 * levels, COLS), :] = water

    even_col = is_even("lon")

    @pl.when(even_col)
    def _():
        store(COLS - 1, col_a_ref)
        store(0, col_z_ref)

    @pl.when(jnp.logical_not(even_col))
    def _():
        store(0, col_a_ref)
        store(COLS - 1, col_z_ref)


def pack_rows_kernel(u_ref, v_ref, p_ref, plane_ref, a_ref, z_ref):
    even = is_even("lat")
    groups = u_ref.shape[0] // COLS // SLOTS

    def send(at, parts):
        upper, lower = strips(parts)
        a_ref[level(at), :] = jnp.where(even, upper, lower)
        z_ref[level(at), :] = jnp.where(even, lower, upper)

    for f, ref in enumerate((u_ref, v_ref, p_ref)):
        for g in range(groups):
            send(f * groups + g, [ref[level(SLOTS * g + s), :] for s in range(SLOTS)])
    send(3 * groups, [plane_ref[level(s), :] for s in range(SLOTS)])


def pack_corners_kernel(rows_a, rows_z, col_z, col_a, a_ref, z_ref):
    even_row, even_col = is_even("lat"), is_even("lon")
    a, z = col_a[...], col_z[...]
    east, west = jnp.where(even_col, a, z), jnp.where(even_col, z, a)
    levels = (a.shape[0] - COLS) // 2
    done = rows_a.shape[0]
    a_ref[pl.ds(0, done), :] = rows_a[...]
    z_ref[pl.ds(0, done), :] = rows_z[...]

    def send(at, parts):
        upper, lower = strips(parts)
        a_ref[pl.ds(at, parts[0].shape[0]), :] = jnp.where(even_row, upper, lower)
        z_ref[pl.ds(at, parts[0].shape[0]), :] = jnp.where(even_row, lower, upper)

    send(done, [east[:levels], east[levels : 2 * levels], west[:levels], west[levels : 2 * levels]])
    send(done + levels, [east[2 * levels :]] * SLOTS)


def levels_kernel(
    u_ref, v_ref, p_ref, plane_ref, col_z, col_a, z_in, a_in,
    far_ref, x_ref, su_ref, sv_ref, east_ref, west_ref, hu_ref, hv_ref, hp_ref,
):
    levels = u_ref.shape[0] // COLS
    thick = thickness(levels)
    groups = levels // SLOTS
    even_col = is_even("lon")
    even_number = 1 - lax.rem(lax.axis_index("lat"), 2)

    def from_a(s, rows):
        slot = lax.broadcasted_iota(jnp.int32, (rows, LANES), 1) // RIM
        return jnp.where(slot == s, even_number, 1 - even_number) == 1

    masks = [from_a(s, COLS) for s in range(SLOTS)]

    def receive(at, s, rows=COLS):
        mask = masks[s] if rows == COLS else from_a(s, rows)
        both = jnp.where(mask, a_in[pl.ds(at, rows), :], z_in[pl.ds(at, rows), :])
        return pltpu.roll(both, LANES - RIM * s, 1) if s else both

    a, z = col_a[...], col_z[...]
    rows = a.shape[0]
    corners = (3 * groups + 1) * COLS
    for i, (ref, value) in enumerate(
        ((east_ref, jnp.where(even_col, a, z)), (west_ref, jnp.where(even_col, z, a)))
    ):
        ref[pl.ds(0, rows), :] = value
        ref[pl.ds(rows, levels), :] = receive(corners, 2 * i, levels)
        ref[pl.ds(rows + levels, levels), :] = receive(corners, 2 * i + 1, levels)
        ref[pl.ds(rows + 2 * levels, COLS), :] = receive(corners + levels, 0)
    for f, ref in enumerate((hu_ref, hv_ref, hp_ref)):
        for k in range(levels):
            ref[level(k), :] = receive((f * groups + k // SLOTS) * COLS, k % SLOTS)
    U, V, W = (0, rows), (levels, rows + levels), (2 * levels, rows + 2 * levels)
    col = col_index()
    top_col, bottom_col = col == COLS - 1, col == 0

    def row(ref, at):
        return jnp.broadcast_to(ref[pl.ds(at, 1), :], (COLS, LANES))

    def east(pair, places, k):
        return [
            jnp.where(top_col, row(east_ref, at + k), pltpu.roll(x, COLS - 1, 0)) for x, at in zip(pair, places)
        ]

    def west(pair, places, k):
        return [
            jnp.where(bottom_col, row(west_ref, at + k), pltpu.roll(x, 1, 0)) for x, at in zip(pair, places)
        ]

    water, eta, wx, wy = [(plane_ref[level(i), :], receive(3 * groups * COLS, i)) for i in range(SLOTS)]
    open_u = [jnp.minimum(w, e) for w, e in zip(water, east(water, W, 0))]
    open_v = [jnp.minimum(w, n) for w, n in zip(water, north(*water))]
    zero = jnp.zeros((COLS, LANES), jnp.float32)
    forcing_u, forcing_v = [zero, zero], [zero, zero]
    flow_u, flow_v = [zero, zero], [zero, zero]
    for k in range(levels):
        dz = float(thick[k])
        u, v, p = [
            (own[level(k), :], rim[level(k), :])
            for own, rim in ((u_ref, hu_ref), (v_ref, hv_ref), (p_ref, hp_ref))
        ]
        push_east = east([0.05 * u[t] - p[t] for t in range(2)], U, k)
        around_u = list(zip(west(u, U, k), north(*u), south(*u)))
        around_v = list(zip(east(v, V, k), west(v, V, k), north(*v), south(*v)))
        p_north = north(*p)
        for t in range(2):
            force_u = push_east[t] + (0.05 * (sum(around_u[t][1:], around_u[t][0]) - 4.0 * u[t]) + p[t])
            force_v = 0.05 * (sum(around_v[t][1:], around_v[t][0]) - 4.0 * v[t]) - (p_north[t] - p[t])
            if k == 0:
                force_u = force_u + wx[t] / dz
                force_v = force_v + wy[t] / dz
            wet_u, wet_v = open_u[t] > float(k), open_v[t] > float(k)
            force_u, vel_u = jnp.where(wet_u, force_u, 0.0), jnp.where(wet_u, u[t], 0.0)
            force_v, vel_v = jnp.where(wet_v, force_v, 0.0), jnp.where(wet_v, v[t], 0.0)
            forcing_u[t] = forcing_u[t] + dz * force_u
            forcing_v[t] = forcing_v[t] + dz * force_v
            flow_u[t] = flow_u[t] + dz * vel_u
            flow_v[t] = flow_v[t] + dz * vel_v
            if t == 0:
                su_ref[level(k), :] = vel_u + STEP * force_u
                sv_ref[level(k), :] = vel_v + STEP * force_v
    fields = (forcing_u, forcing_v, flow_u, flow_v, water, eta)
    for i, f in enumerate(fields):
        x_ref[level(i), :] = f[0]
        far_ref[level(i), :] = f[0]
    for i in range(3):
        x_ref[level(6 + i), :] = pair_rims(fields[2 * i][1], fields[2 * i + 1][1])
    for i, trio in enumerate(TRIOS):
        parts = [pltpu.roll(fields[f][1], at + count, 1) for f, at, count in trio]
        lane = lane_index()
        far_ref[level(6 + i), :] = jnp.where(
            lane < trio[1][1], parts[0], jnp.where(lane < trio[2][1], parts[1], parts[2])
        )


def depth_of(count, levels):
    return (count + count * (count - 1.0) * (1.0 / levels)) * (1.0 / levels)


def substeps_kernel(
    y_ref, a_in, z_in, x_ref, su_ref, sv_ref, out_u, out_v, out_eta,
    eta_ref, u_ref, v_ref, w_ref, fu_ref, fv_ref, du_ref, dv_ref, cu_ref, cv_ref, tw_ref, q_ref, t_ref,
    eta_north_ref, u_north_ref, tw_north_ref,
):
    levels = su_ref.shape[0] // COLS
    tau = STEP / SUBSTEPS
    blocks = 2 * REACH + 1
    even = is_even("lon")
    lane = lane_index()

    def at(p, shift=0):
        return pl.ds(COLS * (p + 1) + shift, COLS)

    places = (
        ((z_in, 2), (a_in, 0)), ((y_ref, 0), (y_ref, 2)), ((a_in, 2), (z_in, 0)),
        ((z_in, 1), (a_in, 1)), ((x_ref, 0), (x_ref, 0)), ((a_in, 1), (z_in, 1)),
        ((z_in, 0), (a_in, 2)), ((y_ref, 2), (y_ref, 0)), ((a_in, 0), (z_in, 2)),
    )
    for p, (for_even, for_odd) in enumerate(places):
        def tile(i):
            def read(place):
                ref, part = place
                start = 0
                if ref is not x_ref:
                    start = (0, FAR_ROWS, FAR_ROWS + NEAR_ROWS)[part]
                return ref[pl.ds(start + COLS * i, COLS), :]

            first = read(for_even)
            return first if p == REACH else jnp.where(even, first, read(for_odd))

        targets = (fu_ref, fv_ref, u_ref, v_ref, w_ref, eta_ref)
        for i, ref in enumerate(targets):
            value = tile(i)
            ref[0, at(p), :] = tau * value if i < 2 else value
        rims = [None] * 6
        if abs(p - REACH) <= 1:
            for i in range(3):
                rims[2 * i] = tile(6 + i)
                rims[2 * i + 1] = pltpu.roll(rims[2 * i], LANES // 2, 1)
        else:
            for i, trio in enumerate(TRIOS):
                shared = tile(6 + i)
                for f, first_lane, count in trio:
                    rims[f] = pltpu.roll(shared, LANES - first_lane - count, 1)
        for i, ref in enumerate(targets):
            ref[1, at(p), :] = tau * rims[i] if i < 2 else rims[i]

    total_rows = LANES * lax.axis_size("lat")
    base = (lax.axis_index("lat") * LANES).astype(jnp.float32)
    own_row = lane.astype(jnp.float32) + base
    rim_row = jnp.where(lane < LANES // 2, lane + LANES, lane - LANES).astype(jnp.float32) + base
    spin = [
        [0.25 * tau * 0.4 * (2.0 * (r + half) * (1.0 / total_rows) - 1.0) for half in (0.5, 1.0)]
        for r in (own_row, rim_row)
    ]
    for p in range(blocks):
        water = [w_ref[t, at(p), :] for t in range(2)]
        water_north = north(*water)
        eta_north = north(eta_ref[0, at(p), :], eta_ref[1, at(p), :])
        for t in range(2):
            eta_north_ref[t, at(p), :] = eta_north[t]
            tw_north_ref[t, at(p), :] = jnp.where(water_north[t] > 0.0, tau, 0.0)
            open_u = jnp.minimum(water[t], w_ref[t, at(p, 1), :])
            open_v = jnp.minimum(water[t], water_north[t])
            du_ref[t, at(p), :] = tau * depth_of(open_u, levels)
            dv_ref[t, at(p), :] = tau * depth_of(open_v, levels)
            cu_ref[t, at(p), :] = jnp.where(open_u > 0.0, spin[t][0], 0.0)
            cv_ref[t, at(p), :] = jnp.where(open_v > 0.0, spin[t][1], 0.0)
            tw_ref[t, at(p), :] = jnp.where(water[t] > 0.0, tau, 0.0)

    flow_u, flow_v = u_ref[0, at(REACH), :], v_ref[0, at(REACH), :]
    zero = jnp.zeros((COLS, LANES), jnp.float32)

    def substep(first, last):
        def body(_, carry):
            total_u, total_v = carry
            for p in range(first, last):
                u = [u_ref[t, at(p), :] for t in range(2)]
                u_west = [u_ref[t, at(p, -1), :] for t in range(2)]
                v = [v_ref[t, at(p), :] for t in range(2)]
                v_south, v_north, u_north = south(*v), north(*v), north(*u)
                for t in range(2):
                    u_north_ref[t, at(p), :] = u_north[t]
                for t in range(2):
                    u_north_west = u_north_ref[t, at(p, -1), :]
                    spread = (u[t] - u_west[t]) + (v[t] - v_south[t])
                    spread_north = (u_north[t] - u_north_west) + (v_north[t] - v[t])
                    eta_ref[t, at(p), :] = eta_ref[t, at(p), :] - tw_ref[t, at(p), :] * spread
                    eta_north_ref[t, at(p), :] = (
                        eta_north_ref[t, at(p), :] - tw_north_ref[t, at(p), :] * spread_north
                    )
                    q_ref[t, at(p), :] = v[t] + v_south[t]
                    t_ref[t, at(p), :] = (u[t] + u_west[t]) + (u_north[t] + u_north_west)
            for p in range(first, last):
                eta = [eta_ref[t, at(p), :] for t in range(2)]
                eta_north = [eta_north_ref[t, at(p), :] for t in range(2)]
                for t in range(2):
                    vbar = q_ref[t, at(p), :] + q_ref[t, at(p, 1), :]
                    rise_u = eta_ref[t, at(p, 1), :] - eta[t]
                    rise_v = eta_north[t] - eta[t]
                    next_u = (u_ref[t, at(p), :] + fu_ref[t, at(p), :]) + (
                        cu_ref[t, at(p), :] * vbar - du_ref[t, at(p), :] * rise_u
                    )
                    next_v = (v_ref[t, at(p), :] + fv_ref[t, at(p), :]) - (
                        cv_ref[t, at(p), :] * t_ref[t, at(p), :] + dv_ref[t, at(p), :] * rise_v
                    )
                    u_ref[t, at(p), :] = next_u
                    v_ref[t, at(p), :] = next_v
                    if p == REACH and t == 0:
                        total_u, total_v = total_u + next_u, total_v + next_v
            return total_u, total_v

        return body

    carry = (zero, zero)
    done = 0
    for ring in range(REACH):
        until = SUBSTEPS - COLS * (REACH - 1 - ring)
        carry = lax.fori_loop(0, until - done, substep(ring, blocks - ring), carry, unroll=until - done)
        done = until
    out_eta[...] = eta_ref[0, at(REACH), :]
    water = [w_ref[t, at(REACH), :] for t in range(2)]
    open_u = jnp.minimum(water[0], w_ref[0, at(REACH, 1), :])
    open_v = jnp.minimum(water[0], north(*water)[0])
    star_u = flow_u + (STEP / tau) * fu_ref[0, at(REACH), :]
    star_v = flow_v + (STEP / tau) * fv_ref[0, at(REACH), :]
    lift_u = (carry[0] / SUBSTEPS - star_u) / jnp.maximum(depth_of(open_u, levels), 0.25)
    lift_v = (carry[1] / SUBSTEPS - star_v) / jnp.maximum(depth_of(open_v, levels), 0.25)
    for k in range(levels):
        out_u[level(k), :] = su_ref[level(k), :] + jnp.where(open_u > float(k), lift_u, 0.0)
        out_v[level(k), :] = sv_ref[level(k), :] + jnp.where(open_v > float(k), lift_v, 0.0)


def call(kernel, shapes, scratch, *operands, **specs):
    return pl.pallas_call(
        kernel,
        out_shape=[jax.ShapeDtypeStruct(s, jnp.float32) for s in shapes],
        scratch_shapes=[pltpu.VMEM(s, jnp.float32) if isinstance(s, tuple) else s for s in scratch],
        compiler_params=pltpu.CompilerParams(vmem_limit_bytes=VMEM_BYTES),
        **specs,
    )(*operands)


def swap(x, axis, first, hop, wraps):
    count = lax.axis_size(axis)
    pairs = []
    for i in range(first, count, 2):
        j = i + hop
        if wraps or 0 <= j < count:
            pairs += [(i, j % count), (j % count, i)]
    return lax.ppermute(x, axis, pairs)


def local(velocity_u, velocity_v, buoyancy, wind_x, wind_y, free_surface, land_sea, bottom_level):
    levels = velocity_u.shape[0]
    flat = (levels * COLS, LANES)
    u, v, b = (a.reshape(flat) for a in (velocity_u, velocity_v, buoyancy))
    inputs = (u, v, b, land_sea, bottom_level, free_surface, wind_x, wind_y)
    edge, tile = (2 * levels + COLS, LANES), (COLS, LANES)
    whole = pltpu.VMEM(tile, jnp.int32)
    col_a, col_z, u, v, p, planes = call(
        pack_edges_kernel,
        [edge, edge, flat, flat, flat, (SLOTS * COLS, LANES)],
        [flat, whole, whole, pltpu.SemaphoreType.DMA((len(inputs),))],
        *[pltpu.with_memory_space_constraint(a, pltpu.HBM) for a in inputs],
        in_specs=[pl.BlockSpec(memory_space=pltpu.HBM)] * len(inputs),
    )
    col_z = swap(col_z, "lon", 1, 1, True)
    col_a = swap(col_a, "lon", 0, 1, True)
    rims = (3 * levels // SLOTS + 1) * COLS
    rows_a, rows_z = call(pack_rows_kernel, [(rims, LANES)] * 2, [], u, v, p, planes)
    rows_a, rows_z = call(
        pack_corners_kernel, [(rims + levels + COLS, LANES)] * 2, [], rows_a, rows_z, col_z, col_a
    )
    rows_z = swap(rows_z, "lat", 1, 1, False)
    rows_a = swap(rows_a, "lat", 0, 1, False)
    both = (2 * edge[0], LANES)
    far, x, star_u, star_v = call(
        levels_kernel, [(FAR_ROWS, LANES), (NEAR_ROWS, LANES), flat, flat], [both, both, flat, flat, flat],
        u, v, p, planes, col_z, col_a, rows_z, rows_a,
    )
    far_z = swap(far, "lon", 1, 3, True)
    far_a = swap(far, "lon", 0, 3, True)
    y = jnp.concatenate([far_z, x, far_a], 0)
    near_z = swap(y, "lon", 1, 1, True)
    near_a = swap(y, "lon", 0, 1, True)
    state = (2, (2 * REACH + 3) * COLS, LANES)
    new_u, new_v, surface = call(
        substeps_kernel, [flat, flat, (COLS, LANES)], [state] * 16, y, near_a, near_z, x, star_u, star_v
    )
    return new_u.reshape(velocity_u.shape), new_v.reshape(velocity_v.shape), surface


def solution(mesh):
    return jax.shard_map(
        local,
        mesh=mesh,
        in_specs=(P(None, "lon", "lat"),) * 3 + (P("lon", "lat"),) * 5,
        out_specs=(P(None, "lon", "lat"), P(None, "lon", "lat"), P("lon", "lat")),
        check_vma=False,
    )
```

```python
import jax
import jax.numpy as jnp
import numpy as np
from jax import lax
from jax.experimental import pallas as pl
from jax.experimental.pallas import tpu as pltpu
from jax.sharding import PartitionSpec as P

SUBSTEPS = 30
LANES = 128
COLS = 8
RIM = 32
SLOTS = 4
REACH = 4
NEAR_ROWS = 9 * COLS
FAR_ROWS = 8 * COLS
PAIRS = 1
TRIOS = (((2, 0, 21), (3, 43, 22), (0, 86, 21)), ((1, 0, 21), (4, 42, 21), (5, 84, 21)))
STEP = 6.0
VMEM_BYTES = 32 * 1024 * 1024


def thickness(levels):
    index = np.arange(levels, dtype=np.float32)
    return (np.float32(1.0) + np.float32(2.0) * index / np.float32(levels)) / np.float32(levels)


def lane_index():
    return lax.broadcasted_iota(jnp.int32, (COLS, LANES), 1)


def col_index():
    return lax.broadcasted_iota(jnp.int32, (COLS, LANES), 0)


def is_even(axis):
    return lax.rem(lax.axis_index(axis), 2) == 0


def level(k):
    return pl.ds(COLS * k, COLS)


def north(own, rim):
    last = lane_index() == LANES - 1
    a, b = pltpu.roll(own, LANES - 1, 1), pltpu.roll(rim, LANES - 1, 1)
    return jnp.where(last, b, a), jnp.where(last, a, b)


def south(own, rim):
    first = lane_index() == 0
    a, b = pltpu.roll(own, 1, 1), pltpu.roll(rim, 1, 1)
    return jnp.where(first, b, a), jnp.where(first, a, b)


def pair_rims(first, second):
    lane = lax.broadcasted_iota(jnp.int32, first.shape, 1)
    return jnp.where((lane >= RIM) & (lane < LANES - RIM), pltpu.roll(second, LANES // 2, 1), first)


def shifted(own, rim, rows):
    if rows == 0:
        return own, rim
    lane = lane_index()
    wraps = lane >= LANES - rows if rows > 0 else lane < -rows
    a, b = pltpu.roll(own, -rows % LANES, 1), pltpu.roll(rim, -rows % LANES, 1)
    return jnp.where(wraps, b, a), jnp.where(wraps, a, b)


def strips(parts):
    slot = lax.broadcasted_iota(jnp.int32, parts[0].shape, 1) // RIM
    moved = [pltpu.roll(p, RIM * s, 1) if s else p for s, p in enumerate(parts)]

    def choose(order):
        first, second, third, fourth = [moved[s] for s in order]
        return jnp.where(slot < 2, jnp.where(slot == 0, first, second), jnp.where(slot == 2, third, fourth))

    return choose((1, 2, 3, 0)), choose((0, 1, 2, 3))


def pack_edges_kernel(
    u_in, v_in, b_in, land_in, bottom_in, eta_in, wx_in, wy_in,
    col_a_ref, col_z_ref, u_ref, v_ref, p_ref, plane_ref,
    b_ref, land_ref, bottom_ref, sems,
):
    levels = u_in.shape[0] // COLS
    thick = thickness(levels)
    copies = [
        pltpu.make_async_copy(src, dst, sems.at[i])
        for i, (src, dst) in enumerate(
            (
                (b_in, b_ref), (land_in, land_ref), (bottom_in, bottom_ref), (u_in, u_ref), (v_in, v_ref),
                (eta_in, plane_ref.at[level(1)]), (wx_in, plane_ref.at[level(2)]), (wy_in, plane_ref.at[level(3)]),
            )
        )
    ]
    for copy in copies:
        copy.start()
    for copy in copies[:3]:
        copy.wait()
    water = (land_ref[...] * bottom_ref[...]).astype(jnp.float32)
    plane_ref[level(0), :] = water
    p = jnp.zeros((COLS, LANES), jnp.float32)
    for k in range(levels):
        p = p + float(thick[k]) * b_ref[level(k), :]
        p_ref[level(k), :] = p
    for copy in copies[3:]:
        copy.wait()

    def edge(ref, col):
        return ref[pl.ds(col, levels, stride=COLS), :]

    def store(col, out_ref):
        first = edge(u_ref, col)
        out_ref[pl.ds(0, levels), :] = first if col else 0.05 * first - edge(p_ref, col)
        out_ref[pl.ds(levels, levels), :] = edge(v_ref, col)
        out_ref[pl.ds(2 * levels, COLS), :] = water

    even_col = is_even("lon")

    @pl.when(even_col)
    def _():
        store(COLS - 1, col_a_ref)
        store(0, col_z_ref)

    @pl.when(jnp.logical_not(even_col))
    def _():
        store(0, col_a_ref)
        store(COLS - 1, col_z_ref)


def pack_rows_kernel(u_ref, v_ref, p_ref, plane_ref, a_ref, z_ref):
    even = is_even("lat")
    groups = u_ref.shape[0] // COLS // SLOTS

    def send(at, parts):
        upper, lower = strips(parts)
        a_ref[level(at), :] = jnp.where(even, upper, lower)
        z_ref[level(at), :] = jnp.where(even, lower, upper)

    for f, ref in enumerate((u_ref, v_ref, p_ref)):
        for g in range(groups):
            send(f * groups + g, [ref[level(SLOTS * g + s), :] for s in range(SLOTS)])
    send(3 * groups, [plane_ref[level(s), :] for s in range(SLOTS)])


def pack_corners_kernel(rows_a, rows_z, col_z, col_a, a_ref, z_ref):
    even_row, even_col = is_even("lat"), is_even("lon")
    a, z = col_a[...], col_z[...]
    east, west = jnp.where(even_col, a, z), jnp.where(even_col, z, a)
    levels = (a.shape[0] - COLS) // 2
    done = rows_a.shape[0]
    a_ref[pl.ds(0, done), :] = rows_a[...]
    z_ref[pl.ds(0, done), :] = rows_z[...]

    def send(at, parts):
        upper, lower = strips(parts)
        a_ref[pl.ds(at, parts[0].shape[0]), :] = jnp.where(even_row, upper, lower)
        z_ref[pl.ds(at, parts[0].shape[0]), :] = jnp.where(even_row, lower, upper)

    send(done, [east[:levels], east[levels : 2 * levels], west[:levels], west[levels : 2 * levels]])
    send(done + levels, [east[2 * levels :]] * SLOTS)


def levels_kernel(
    u_ref, v_ref, p_ref, plane_ref, col_z, col_a, z_in, a_in,
    far_ref, x_ref, su_ref, sv_ref, east_ref, west_ref, hu_ref, hv_ref, hp_ref,
):
    levels = u_ref.shape[0] // COLS
    thick = thickness(levels)
    groups = levels // SLOTS
    even_col = is_even("lon")
    even_number = 1 - lax.rem(lax.axis_index("lat"), 2)

    def from_a(s, rows):
        slot = lax.broadcasted_iota(jnp.int32, (rows, LANES), 1) // RIM
        return jnp.where(slot == s, even_number, 1 - even_number) == 1

    masks = [from_a(s, COLS) for s in range(SLOTS)]

    def receive(at, s, rows=COLS):
        mask = masks[s] if rows == COLS else from_a(s, rows)
        both = jnp.where(mask, a_in[pl.ds(at, rows), :], z_in[pl.ds(at, rows), :])
        return pltpu.roll(both, LANES - RIM * s, 1) if s else both

    a, z = col_a[...], col_z[...]
    rows = a.shape[0]
    corners = (3 * groups + 1) * COLS
    for i, (ref, value) in enumerate(
        ((east_ref, jnp.where(even_col, a, z)), (west_ref, jnp.where(even_col, z, a)))
    ):
        ref[pl.ds(0, rows), :] = value
        ref[pl.ds(rows, levels), :] = receive(corners, 2 * i, levels)
        ref[pl.ds(rows + levels, levels), :] = receive(corners, 2 * i + 1, levels)
        ref[pl.ds(rows + 2 * levels, COLS), :] = receive(corners + levels, 0)
    for f, ref in enumerate((hu_ref, hv_ref, hp_ref)):
        for k in range(levels):
            ref[level(k), :] = receive((f * groups + k // SLOTS) * COLS, k % SLOTS)
    U, V, W = (0, rows), (levels, rows + levels), (2 * levels, rows + 2 * levels)
    col = col_index()
    top_col, bottom_col = col == COLS - 1, col == 0

    def row(ref, at):
        return jnp.broadcast_to(ref[pl.ds(at, 1), :], (COLS, LANES))

    def east(pair, places, k):
        return [
            jnp.where(top_col, row(east_ref, at + k), pltpu.roll(x, COLS - 1, 0)) for x, at in zip(pair, places)
        ]

    def west(pair, places, k):
        return [
            jnp.where(bottom_col, row(west_ref, at + k), pltpu.roll(x, 1, 0)) for x, at in zip(pair, places)
        ]

    water, eta, wx, wy = [(plane_ref[level(i), :], receive(3 * groups * COLS, i)) for i in range(SLOTS)]
    open_u = [jnp.minimum(w, e) for w, e in zip(water, east(water, W, 0))]
    open_v = [jnp.minimum(w, n) for w, n in zip(water, north(*water))]
    zero = jnp.zeros((COLS, LANES), jnp.float32)
    forcing_u, forcing_v = [zero, zero], [zero, zero]
    flow_u, flow_v = [zero, zero], [zero, zero]
    for k in range(levels):
        dz = float(thick[k])
        u, v, p = [
            (own[level(k), :], rim[level(k), :])
            for own, rim in ((u_ref, hu_ref), (v_ref, hv_ref), (p_ref, hp_ref))
        ]
        push_east = east([0.05 * u[t] - p[t] for t in range(2)], U, k)
        around_u = list(zip(west(u, U, k), north(*u), south(*u)))
        around_v = list(zip(east(v, V, k), west(v, V, k), north(*v), south(*v)))
        p_north = north(*p)
        for t in range(2):
            force_u = push_east[t] + (0.05 * (sum(around_u[t][1:], around_u[t][0]) - 4.0 * u[t]) + p[t])
            force_v = 0.05 * (sum(around_v[t][1:], around_v[t][0]) - 4.0 * v[t]) - (p_north[t] - p[t])
            if k == 0:
                force_u = force_u + wx[t] / dz
                force_v = force_v + wy[t] / dz
            wet_u, wet_v = open_u[t] > float(k), open_v[t] > float(k)
            force_u, vel_u = jnp.where(wet_u, force_u, 0.0), jnp.where(wet_u, u[t], 0.0)
            force_v, vel_v = jnp.where(wet_v, force_v, 0.0), jnp.where(wet_v, v[t], 0.0)
            forcing_u[t] = forcing_u[t] + dz * force_u
            forcing_v[t] = forcing_v[t] + dz * force_v
            flow_u[t] = flow_u[t] + dz * vel_u
            flow_v[t] = flow_v[t] + dz * vel_v
            if t == 0:
                su_ref[level(k), :] = vel_u + STEP * force_u
                sv_ref[level(k), :] = vel_v + STEP * force_v
    fields = (forcing_u, forcing_v, flow_u, flow_v, water, eta)
    for i, f in enumerate(fields):
        x_ref[level(i), :] = f[0]
        far_ref[level(i), :] = f[0]
    for i in range(3):
        x_ref[level(6 + i), :] = pair_rims(fields[2 * i][1], fields[2 * i + 1][1])
    for i, trio in enumerate(TRIOS):
        parts = [pltpu.roll(fields[f][1], at + count, 1) for f, at, count in trio]
        lane = lane_index()
        far_ref[level(6 + i), :] = jnp.where(
            lane < trio[1][1], parts[0], jnp.where(lane < trio[2][1], parts[1], parts[2])
        )


def depth_of(count, levels):
    return (count + count * (count - 1.0) * (1.0 / levels)) * (1.0 / levels)


def substeps_kernel(
    y_ref, a_in, z_in, x_ref, su_ref, sv_ref, out_u, out_v, out_eta,
    eta_ref, u_ref, v_ref, w_ref, fu_ref, fv_ref, du_ref, dv_ref, cu_ref, cv_ref, tw_ref, q_ref, t_ref,
    eta_north_ref, u_north_ref, tw_north_ref, more_ref,
):
    levels = su_ref.shape[0] // COLS
    tau = STEP / SUBSTEPS
    blocks = 2 * REACH + 1
    even = is_even("lon")
    lane = lane_index()

    def at(p, shift=0):
        return pl.ds(COLS * (p + 1) + shift, COLS)

    places = (
        ((z_in, 2), (a_in, 0)), ((y_ref, 0), (y_ref, 2)), ((a_in, 2), (z_in, 0)),
        ((z_in, 1), (a_in, 1)), ((x_ref, 0), (x_ref, 0)), ((a_in, 1), (z_in, 1)),
        ((z_in, 0), (a_in, 2)), ((y_ref, 2), (y_ref, 0)), ((a_in, 0), (z_in, 2)),
    )
    for p, (for_even, for_odd) in enumerate(places):
        def tile(i):
            def read(place):
                ref, part = place
                start = 0
                if ref is not x_ref:
                    start = (0, FAR_ROWS, FAR_ROWS + NEAR_ROWS)[part]
                return ref[pl.ds(start + COLS * i, COLS), :]

            first = read(for_even)
            return first if p == REACH else jnp.where(even, first, read(for_odd))

        targets = (fu_ref, fv_ref, u_ref, v_ref, w_ref, eta_ref)
        for i, ref in enumerate(targets):
            value = tile(i)
            ref[0, at(p), :] = tau * value if i < 2 else value
        rims = [None] * 6
        if abs(p - REACH) <= 1:
            for i in range(3):
                rims[2 * i] = tile(6 + i)
                rims[2 * i + 1] = pltpu.roll(rims[2 * i], LANES // 2, 1)
        else:
            for i, trio in enumerate(TRIOS):
                shared = tile(6 + i)
                for f, first_lane, count in trio:
                    rims[f] = pltpu.roll(shared, LANES - first_lane - count, 1)
        for i, ref in enumerate(targets):
            ref[1, at(p), :] = tau * rims[i] if i < 2 else rims[i]

    total_rows = LANES * lax.axis_size("lat")
    base = (lax.axis_index("lat") * LANES).astype(jnp.float32)
    own_row = lane.astype(jnp.float32) + base
    rim_row = jnp.where(lane < LANES // 2, lane + LANES, lane - LANES).astype(jnp.float32) + base
    spin = [
        [0.25 * tau * 0.4 * (2.0 * (r + half) * (1.0 / total_rows) - 1.0) for half in (0.5, 1.0)]
        for r in (own_row, rim_row)
    ]
    for p in range(blocks):
        water = [w_ref[t, at(p), :] for t in range(2)]
        water_north = north(*water)
        eta_north = north(eta_ref[0, at(p), :], eta_ref[1, at(p), :])
        for t in range(2):
            eta_north_ref[t, at(p), :] = eta_north[t]
            tw_north_ref[t, at(p), :] = jnp.where(water_north[t] > 0.0, tau, 0.0)
            open_u = jnp.minimum(water[t], w_ref[t, at(p, 1), :])
            open_v = jnp.minimum(water[t], water_north[t])
            du_ref[t, at(p), :] = tau * depth_of(open_u, levels)
            dv_ref[t, at(p), :] = tau * depth_of(open_v, levels)
            cu_ref[t, at(p), :] = jnp.where(open_u > 0.0, spin[t][0], 0.0)
            cv_ref[t, at(p), :] = jnp.where(open_v > 0.0, spin[t][1], 0.0)
            tw_ref[t, at(p), :] = jnp.where(water[t] > 0.0, tau, 0.0)

    flow_u, flow_v = u_ref[0, at(REACH), :], v_ref[0, at(REACH), :]
    zero = jnp.zeros((COLS, LANES), jnp.float32)

    def finish(first, last, carry, u_from, v_from):
        total_u, total_v = carry
        for p in range(first, last):
            eta = [eta_ref[t, at(p), :] for t in range(2)]
            eta_north = [eta_north_ref[t, at(p), :] for t in range(2)]
            for t in range(2):
                vbar = q_ref[t, at(p), :] + q_ref[t, at(p, 1), :]
                rise_u = eta_ref[t, at(p, 1), :] - eta[t]
                rise_v = eta_north[t] - eta[t]
                next_u = (u_from[t, at(p), :] + fu_ref[t, at(p), :]) + (
                    cu_ref[t, at(p), :] * vbar - du_ref[t, at(p), :] * rise_u
                )
                next_v = (v_from[t, at(p), :] + fv_ref[t, at(p), :]) - (
                    cv_ref[t, at(p), :] * t_ref[t, at(p), :] + dv_ref[t, at(p), :] * rise_v
                )
                u_ref[t, at(p), :] = next_u
                v_ref[t, at(p), :] = next_v
                if p == REACH and t == 0:
                    total_u, total_v = total_u + next_u, total_v + next_v
        return total_u, total_v

    def substep(first, last):
        def body(_, carry):
            for p in range(first, last):
                u = [u_ref[t, at(p), :] for t in range(2)]
                u_west = [u_ref[t, at(p, -1), :] for t in range(2)]
                v = [v_ref[t, at(p), :] for t in range(2)]
                v_south, v_north, u_north = south(*v), north(*v), north(*u)
                for t in range(2):
                    u_north_ref[t, at(p), :] = u_north[t]
                for t in range(2):
                    u_north_west = u_north_ref[t, at(p, -1), :]
                    spread = (u[t] - u_west[t]) + (v[t] - v_south[t])
                    spread_north = (u_north[t] - u_north_west) + (v_north[t] - v[t])
                    eta_ref[t, at(p), :] = eta_ref[t, at(p), :] - tw_ref[t, at(p), :] * spread
                    eta_north_ref[t, at(p), :] = (
                        eta_north_ref[t, at(p), :] - tw_north_ref[t, at(p), :] * spread_north
                    )
                    q_ref[t, at(p), :] = v[t] + v_south[t]
                    t_ref[t, at(p), :] = (u[t] + u_west[t]) + (u_north[t] + u_north_west)
            return finish(first, last, carry, u_ref, v_ref)

        return body

    names = ("u-1", "u2", "v-1", "v1", "e-1", "e0", "e1", "e2", "q1", "t-1", "t1", "U0", "U1", "V-1", "V0", "V1") + (
        "fu1", "cu1", "du1", "fv-1", "fv1", "cv-1", "cv1", "dv-1", "dv1", "tw-1", "tw2"
    )
    kept = {"u0": u_ref, "u1": u_north_ref, "v0": v_ref, "q0": q_ref, "t0": t_ref, "tw0": tw_ref, "tw1": tw_north_ref}
    kept |= {"fu0": fu_ref, "cu0": cu_ref, "du0": du_ref, "fv0": fv_ref, "cv0": cv_ref, "dv0": dv_ref}
    kept |= {name: more_ref.at[i] for i, name in enumerate(names)}

    def get(name, rows, p, t, shift=0):
        return kept[f"{name}{rows}"][t, at(p, shift), :]

    def put(name, rows, p, t, value):
        kept[f"{name}{rows}"][t, at(p), :] = value

    for p in range(PAIRS, blocks - PAIRS):
        for name, where in (
            ("fu", (1,)), ("cu", (1,)), ("du", (1,)), ("fv", (-1, 1)), ("cv", (-1, 1)), ("dv", (-1, 1)), ("tw", (-1, 2))
        ):
            here = [get(name, 0, p, t) for t in range(2)]
            for rows in where:
                for t, value in enumerate(shifted(*here, rows)):
                    put(name, rows, p, t, value)

    def pair_of_steps(first, last, carry):
        total_u, total_v = carry
        tiles = range(first, last)
        for p in tiles:
            u, v, eta = [[ref[t, at(p), :] for t in range(2)] for ref in (u_ref, v_ref, eta_ref)]
            us = {r: shifted(*u, r) for r in (0, -1, 1, 2)}
            vs = {r: shifted(*v, r) for r in (0, -1, -2, 1, 2)}
            es = {r: shifted(*eta, r) for r in (0, -1, 1, 2)}
            for t in range(2):
                for r in (-1, 1, 2):
                    put("u", r, p, t, us[r][t])
                for r in (-1, 1):
                    put("v", r, p, t, vs[r][t])
                both = {}
                for r in (-1, 0, 1, 2):
                    u_west = get("u", r, p, t, -1)
                    both[r] = us[r][t] + u_west
                    spread = (us[r][t] - u_west) + (vs[r][t] - vs[r - 1][t])
                    put("e", r, p, t, es[r][t] - get("tw", r, p, t) * spread)
                for r in (0, 1):
                    put("q", r, p, t, vs[r][t] + vs[r - 1][t])
                for r in (-1, 0, 1):
                    put("t", r, p, t, both[r] + both[r + 1])
        for p in tiles:
            for t in range(2):
                e = {r: get("e", r, p, t) for r in (-1, 0, 1, 2)}
                for r in (0, 1):
                    vbar = get("q", r, p, t) + get("q", r, p, t, 1)
                    rise = get("e", r, p, t, 1) - e[r]
                    next_u = (get("u", r, p, t) + get("fu", r, p, t)) + (
                        get("cu", r, p, t) * vbar - get("du", r, p, t) * rise
                    )
                    put("U", r, p, t, next_u)
                    if p == REACH and t == 0 and r == 0:
                        total_u = total_u + next_u
                for r in (-1, 0, 1):
                    next_v = (get("v", r, p, t) + get("fv", r, p, t)) - (
                        get("cv", r, p, t) * get("t", r, p, t) + get("dv", r, p, t) * (e[r + 1] - e[r])
                    )
                    put("V", r, p, t, next_v)
                    if p == REACH and t == 0 and r == 0:
                        total_v = total_v + next_v
        for p in tiles:
            for t in range(2):
                both = []
                for r, ref in ((0, eta_ref), (1, eta_north_ref)):
                    u, u_west = get("U", r, p, t), get("U", r, p, t, -1)
                    both.append(u + u_west)
                    spread = (u - u_west) + (get("V", r, p, t) - get("V", r - 1, p, t))
                    ref[t, at(p), :] = get("e", r, p, t) - get("tw", r, p, t) * spread
                q_ref[t, at(p), :] = get("V", 0, p, t) + get("V", -1, p, t)
                t_ref[t, at(p), :] = both[0] + both[1]
        return finish(first, last, (total_u, total_v), kept["U0"], kept["V0"])

    carry = (zero, zero)
    done = 0
    for ring in range(REACH):
        until = SUBSTEPS - COLS * (REACH - 1 - ring)
        if ring < PAIRS:
            carry = lax.fori_loop(0, until - done, substep(ring, blocks - ring), carry, unroll=until - done)
        else:
            for _ in range((until - done) // 2):
                carry = pair_of_steps(ring, blocks - ring, carry)
        done = until
    out_eta[...] = eta_ref[0, at(REACH), :]
    water = [w_ref[t, at(REACH), :] for t in range(2)]
    open_u = jnp.minimum(water[0], w_ref[0, at(REACH, 1), :])
    open_v = jnp.minimum(water[0], north(*water)[0])
    star_u = flow_u + (STEP / tau) * fu_ref[0, at(REACH), :]
    star_v = flow_v + (STEP / tau) * fv_ref[0, at(REACH), :]
    lift_u = (carry[0] / SUBSTEPS - star_u) / jnp.maximum(depth_of(open_u, levels), 0.25)
    lift_v = (carry[1] / SUBSTEPS - star_v) / jnp.maximum(depth_of(open_v, levels), 0.25)
    for k in range(levels):
        out_u[level(k), :] = su_ref[level(k), :] + jnp.where(open_u > float(k), lift_u, 0.0)
        out_v[level(k), :] = sv_ref[level(k), :] + jnp.where(open_v > float(k), lift_v, 0.0)


def call(kernel, shapes, scratch, *operands, **specs):
    return pl.pallas_call(
        kernel,
        out_shape=[jax.ShapeDtypeStruct(s, jnp.float32) for s in shapes],
        scratch_shapes=[pltpu.VMEM(s, jnp.float32) if isinstance(s, tuple) else s for s in scratch],
        compiler_params=pltpu.CompilerParams(vmem_limit_bytes=VMEM_BYTES),
        **specs,
    )(*operands)


def swap(x, axis, first, hop, wraps):
    count = lax.axis_size(axis)
    pairs = []
    for i in range(first, count, 2):
        j = i + hop
        if wraps or 0 <= j < count:
            pairs += [(i, j % count), (j % count, i)]
    return lax.ppermute(x, axis, pairs)


def local(velocity_u, velocity_v, buoyancy, wind_x, wind_y, free_surface, land_sea, bottom_level):
    levels = velocity_u.shape[0]
    flat = (levels * COLS, LANES)
    u, v, b = (a.reshape(flat) for a in (velocity_u, velocity_v, buoyancy))
    inputs = (u, v, b, land_sea, bottom_level, free_surface, wind_x, wind_y)
    edge, tile = (2 * levels + COLS, LANES), (COLS, LANES)
    whole = pltpu.VMEM(tile, jnp.int32)
    col_a, col_z, u, v, p, planes = call(
        pack_edges_kernel,
        [edge, edge, flat, flat, flat, (SLOTS * COLS, LANES)],
        [flat, whole, whole, pltpu.SemaphoreType.DMA((len(inputs),))],
        *[pltpu.with_memory_space_constraint(a, pltpu.HBM) for a in inputs],
        in_specs=[pl.BlockSpec(memory_space=pltpu.HBM)] * len(inputs),
    )
    col_z = swap(col_z, "lon", 1, 1, True)
    col_a = swap(col_a, "lon", 0, 1, True)
    rims = (3 * levels // SLOTS + 1) * COLS
    rows_a, rows_z = call(pack_rows_kernel, [(rims, LANES)] * 2, [], u, v, p, planes)
    rows_a, rows_z = call(
        pack_corners_kernel, [(rims + levels + COLS, LANES)] * 2, [], rows_a, rows_z, col_z, col_a
    )
    rows_z = swap(rows_z, "lat", 1, 1, False)
    rows_a = swap(rows_a, "lat", 0, 1, False)
    both = (2 * edge[0], LANES)
    far, x, star_u, star_v = call(
        levels_kernel, [(FAR_ROWS, LANES), (NEAR_ROWS, LANES), flat, flat], [both, both, flat, flat, flat],
        u, v, p, planes, col_z, col_a, rows_z, rows_a,
    )
    far_z = swap(far, "lon", 1, 3, True)
    far_a = swap(far, "lon", 0, 3, True)
    y = jnp.concatenate([far_z, x, far_a], 0)
    near_z = swap(y, "lon", 1, 1, True)
    near_a = swap(y, "lon", 0, 1, True)
    state = (2, (2 * REACH + 3) * COLS, LANES)
    new_u, new_v, surface = call(
        substeps_kernel, [flat, flat, (COLS, LANES)], [state] * 16 + [(27, *state)], y, near_a, near_z, x, star_u, star_v
    )
    return new_u.reshape(velocity_u.shape), new_v.reshape(velocity_v.shape), surface


def solution(mesh):
    return jax.shard_map(
        local,
        mesh=mesh,
        in_specs=(P(None, "lon", "lat"),) * 3 + (P("lon", "lat"),) * 5,
        out_specs=(P(None, "lon", "lat"), P(None, "lon", "lat"), P("lon", "lat")),
        check_vma=False,
    )
```

```python
import jax
import jax.numpy as jnp
import numpy as np
from jax import lax
from jax.experimental import pallas as pl
from jax.experimental.pallas import tpu as pltpu
from jax.sharding import PartitionSpec as P

SUBSTEPS = 30
LANES = 128
COLS = 8
RIM = 32
SLOTS = 4
REACH = 4
NEAR_ROWS = 9 * COLS
FAR_ROWS = 8 * COLS
PAIRS = 2
TRIOS = (((2, 0, 21), (3, 43, 22), (0, 86, 21)), ((1, 0, 21), (4, 42, 21), (5, 84, 21)))
STEP = 6.0
VMEM_BYTES = 32 * 1024 * 1024


def thickness(levels):
    index = np.arange(levels, dtype=np.float32)
    return (np.float32(1.0) + np.float32(2.0) * index / np.float32(levels)) / np.float32(levels)


def lane_index():
    return lax.broadcasted_iota(jnp.int32, (COLS, LANES), 1)


def col_index():
    return lax.broadcasted_iota(jnp.int32, (COLS, LANES), 0)


def is_even(axis):
    return lax.rem(lax.axis_index(axis), 2) == 0


def level(k):
    return pl.ds(COLS * k, COLS)


def north(own, rim):
    last = lane_index() == LANES - 1
    a, b = pltpu.roll(own, LANES - 1, 1), pltpu.roll(rim, LANES - 1, 1)
    return jnp.where(last, b, a), jnp.where(last, a, b)


def south(own, rim):
    first = lane_index() == 0
    a, b = pltpu.roll(own, 1, 1), pltpu.roll(rim, 1, 1)
    return jnp.where(first, b, a), jnp.where(first, a, b)


def pair_rims(first, second):
    lane = lax.broadcasted_iota(jnp.int32, first.shape, 1)
    return jnp.where((lane >= RIM) & (lane < LANES - RIM), pltpu.roll(second, LANES // 2, 1), first)


def shifted(own, rim, rows):
    if rows == 0:
        return own, rim
    lane = lane_index()
    wraps = lane >= LANES - rows if rows > 0 else lane < -rows
    a, b = pltpu.roll(own, -rows % LANES, 1), pltpu.roll(rim, -rows % LANES, 1)
    return jnp.where(wraps, b, a), jnp.where(wraps, a, b)


def strips(parts):
    slot = lax.broadcasted_iota(jnp.int32, parts[0].shape, 1) // RIM
    moved = [pltpu.roll(p, RIM * s, 1) if s else p for s, p in enumerate(parts)]

    def choose(order):
        first, second, third, fourth = [moved[s] for s in order]
        return jnp.where(slot < 2, jnp.where(slot == 0, first, second), jnp.where(slot == 2, third, fourth))

    return choose((1, 2, 3, 0)), choose((0, 1, 2, 3))


def pack_edges_kernel(
    u_in, v_in, b_in, land_in, bottom_in, eta_in, wx_in, wy_in,
    col_a_ref, col_z_ref, u_ref, v_ref, p_ref, plane_ref,
    b_ref, land_ref, bottom_ref, sems,
):
    levels = u_in.shape[0] // COLS
    thick = thickness(levels)
    copies = [
        pltpu.make_async_copy(src, dst, sems.at[i])
        for i, (src, dst) in enumerate(
            (
                (b_in, b_ref), (land_in, land_ref), (bottom_in, bottom_ref), (u_in, u_ref), (v_in, v_ref),
                (eta_in, plane_ref.at[level(1)]), (wx_in, plane_ref.at[level(2)]), (wy_in, plane_ref.at[level(3)]),
            )
        )
    ]
    for copy in copies:
        copy.start()
    for copy in copies[:3]:
        copy.wait()
    water = (land_ref[...] * bottom_ref[...]).astype(jnp.float32)
    plane_ref[level(0), :] = water
    p = jnp.zeros((COLS, LANES), jnp.float32)
    for k in range(levels):
        p = p + float(thick[k]) * b_ref[level(k), :]
        p_ref[level(k), :] = p
    for copy in copies[3:]:
        copy.wait()

    def edge(ref, col):
        return ref[pl.ds(col, levels, stride=COLS), :]

    def store(col, out_ref):
        first = edge(u_ref, col)
        out_ref[pl.ds(0, levels), :] = first if col else 0.05 * first - edge(p_ref, col)
        out_ref[pl.ds(levels, levels), :] = edge(v_ref, col)
        out_ref[pl.ds(2 * levels, COLS), :] = water

    even_col = is_even("lon")

    @pl.when(even_col)
    def _():
        store(COLS - 1, col_a_ref)
        store(0, col_z_ref)

    @pl.when(jnp.logical_not(even_col))
    def _():
        store(0, col_a_ref)
        store(COLS - 1, col_z_ref)


def pack_rows_kernel(u_ref, v_ref, p_ref, plane_ref, a_ref, z_ref):
    even = is_even("lat")
    groups = u_ref.shape[0] // COLS // SLOTS

    def send(at, parts):
        upper, lower = strips(parts)
        a_ref[level(at), :] = jnp.where(even, upper, lower)
        z_ref[level(at), :] = jnp.where(even, lower, upper)

    for f, ref in enumerate((u_ref, v_ref, p_ref)):
        for g in range(groups):
            send(f * groups + g, [ref[level(SLOTS * g + s), :] for s in range(SLOTS)])
    send(3 * groups, [plane_ref[level(s), :] for s in range(SLOTS)])


def pack_corners_kernel(rows_a, rows_z, col_z, col_a, a_ref, z_ref):
    even_row, even_col = is_even("lat"), is_even("lon")
    a, z = col_a[...], col_z[...]
    east, west = jnp.where(even_col, a, z), jnp.where(even_col, z, a)
    levels = (a.shape[0] - COLS) // 2
    done = rows_a.shape[0]
    a_ref[pl.ds(0, done), :] = rows_a[...]
    z_ref[pl.ds(0, done), :] = rows_z[...]

    def send(at, parts):
        upper, lower = strips(parts)
        a_ref[pl.ds(at, parts[0].shape[0]), :] = jnp.where(even_row, upper, lower)
        z_ref[pl.ds(at, parts[0].shape[0]), :] = jnp.where(even_row, lower, upper)

    send(done, [east[:levels], east[levels : 2 * levels], west[:levels], west[levels : 2 * levels]])
    send(done + levels, [east[2 * levels :]] * SLOTS)


def levels_kernel(
    u_ref, v_ref, p_ref, plane_ref, col_z, col_a, z_in, a_in,
    far_ref, x_ref, su_ref, sv_ref, east_ref, west_ref, hu_ref, hv_ref, hp_ref,
):
    levels = u_ref.shape[0] // COLS
    thick = thickness(levels)
    groups = levels // SLOTS
    even_col = is_even("lon")
    even_number = 1 - lax.rem(lax.axis_index("lat"), 2)

    def from_a(s, rows):
        slot = lax.broadcasted_iota(jnp.int32, (rows, LANES), 1) // RIM
        return jnp.where(slot == s, even_number, 1 - even_number) == 1

    masks = [from_a(s, COLS) for s in range(SLOTS)]

    def receive(at, s, rows=COLS):
        mask = masks[s] if rows == COLS else from_a(s, rows)
        both = jnp.where(mask, a_in[pl.ds(at, rows), :], z_in[pl.ds(at, rows), :])
        return pltpu.roll(both, LANES - RIM * s, 1) if s else both

    a, z = col_a[...], col_z[...]
    rows = a.shape[0]
    corners = (3 * groups + 1) * COLS
    for i, (ref, value) in enumerate(
        ((east_ref, jnp.where(even_col, a, z)), (west_ref, jnp.where(even_col, z, a)))
    ):
        ref[pl.ds(0, rows), :] = value
        ref[pl.ds(rows, levels), :] = receive(corners, 2 * i, levels)
        ref[pl.ds(rows + levels, levels), :] = receive(corners, 2 * i + 1, levels)
        ref[pl.ds(rows + 2 * levels, COLS), :] = receive(corners + levels, 0)
    for f, ref in enumerate((hu_ref, hv_ref, hp_ref)):
        for k in range(levels):
            ref[level(k), :] = receive((f * groups + k // SLOTS) * COLS, k % SLOTS)
    U, V, W = (0, rows), (levels, rows + levels), (2 * levels, rows + 2 * levels)
    col = col_index()
    top_col, bottom_col = col == COLS - 1, col == 0

    def row(ref, at):
        return jnp.broadcast_to(ref[pl.ds(at, 1), :], (COLS, LANES))

    def east(pair, places, k):
        return [
            jnp.where(top_col, row(east_ref, at + k), pltpu.roll(x, COLS - 1, 0)) for x, at in zip(pair, places)
        ]

    def west(pair, places, k):
        return [
            jnp.where(bottom_col, row(west_ref, at + k), pltpu.roll(x, 1, 0)) for x, at in zip(pair, places)
        ]

    water, eta, wx, wy = [(plane_ref[level(i), :], receive(3 * groups * COLS, i)) for i in range(SLOTS)]
    open_u = [jnp.minimum(w, e) for w, e in zip(water, east(water, W, 0))]
    open_v = [jnp.minimum(w, n) for w, n in zip(water, north(*water))]
    zero = jnp.zeros((COLS, LANES), jnp.float32)
    forcing_u, forcing_v = [zero, zero], [zero, zero]
    flow_u, flow_v = [zero, zero], [zero, zero]
    for k in range(levels):
        dz = float(thick[k])
        u, v, p = [
            (own[level(k), :], rim[level(k), :])
            for own, rim in ((u_ref, hu_ref), (v_ref, hv_ref), (p_ref, hp_ref))
        ]
        push_east = east([0.05 * u[t] - p[t] for t in range(2)], U, k)
        around_u = list(zip(west(u, U, k), north(*u), south(*u)))
        around_v = list(zip(east(v, V, k), west(v, V, k), north(*v), south(*v)))
        p_north = north(*p)
        for t in range(2):
            force_u = push_east[t] + (0.05 * (sum(around_u[t][1:], around_u[t][0]) - 4.0 * u[t]) + p[t])
            force_v = 0.05 * (sum(around_v[t][1:], around_v[t][0]) - 4.0 * v[t]) - (p_north[t] - p[t])
            if k == 0:
                force_u = force_u + wx[t] / dz
                force_v = force_v + wy[t] / dz
            wet_u, wet_v = open_u[t] > float(k), open_v[t] > float(k)
            force_u, vel_u = jnp.where(wet_u, force_u, 0.0), jnp.where(wet_u, u[t], 0.0)
            force_v, vel_v = jnp.where(wet_v, force_v, 0.0), jnp.where(wet_v, v[t], 0.0)
            forcing_u[t] = forcing_u[t] + dz * force_u
            forcing_v[t] = forcing_v[t] + dz * force_v
            flow_u[t] = flow_u[t] + dz * vel_u
            flow_v[t] = flow_v[t] + dz * vel_v
            if t == 0:
                su_ref[level(k), :] = vel_u + STEP * force_u
                sv_ref[level(k), :] = vel_v + STEP * force_v
    fields = (forcing_u, forcing_v, flow_u, flow_v, water, eta)
    for i, f in enumerate(fields):
        x_ref[level(i), :] = f[0]
        far_ref[level(i), :] = f[0]
    for i in range(3):
        x_ref[level(6 + i), :] = pair_rims(fields[2 * i][1], fields[2 * i + 1][1])
    for i, trio in enumerate(TRIOS):
        parts = [pltpu.roll(fields[f][1], at + count, 1) for f, at, count in trio]
        lane = lane_index()
        far_ref[level(6 + i), :] = jnp.where(
            lane < trio[1][1], parts[0], jnp.where(lane < trio[2][1], parts[1], parts[2])
        )


def depth_of(count, levels):
    return (count + count * (count - 1.0) * (1.0 / levels)) * (1.0 / levels)


def substeps_kernel(
    y_ref, a_in, z_in, x_ref, su_ref, sv_ref, out_u, out_v, out_eta,
    eta_ref, u_ref, v_ref, w_ref, fu_ref, fv_ref, du_ref, dv_ref, cu_ref, cv_ref, tw_ref, q_ref, t_ref,
    eta_north_ref, u_north_ref, tw_north_ref, more_ref,
):
    levels = su_ref.shape[0] // COLS
    tau = STEP / SUBSTEPS
    blocks = 2 * REACH + 1
    even = is_even("lon")
    lane = lane_index()

    def at(p, shift=0):
        return pl.ds(COLS * (p + 1) + shift, COLS)

    places = (
        ((z_in, 2), (a_in, 0)), ((y_ref, 0), (y_ref, 2)), ((a_in, 2), (z_in, 0)),
        ((z_in, 1), (a_in, 1)), ((x_ref, 0), (x_ref, 0)), ((a_in, 1), (z_in, 1)),
        ((z_in, 0), (a_in, 2)), ((y_ref, 2), (y_ref, 0)), ((a_in, 0), (z_in, 2)),
    )
    for p, (for_even, for_odd) in enumerate(places):
        def tile(i):
            def read(place):
                ref, part = place
                start = 0
                if ref is not x_ref:
                    start = (0, FAR_ROWS, FAR_ROWS + NEAR_ROWS)[part]
                return ref[pl.ds(start + COLS * i, COLS), :]

            first = read(for_even)
            return first if p == REACH else jnp.where(even, first, read(for_odd))

        targets = (fu_ref, fv_ref, u_ref, v_ref, w_ref, eta_ref)
        for i, ref in enumerate(targets):
            value = tile(i)
            ref[0, at(p), :] = tau * value if i < 2 else value
        rims = [None] * 6
        if abs(p - REACH) <= 1:
            for i in range(3):
                rims[2 * i] = tile(6 + i)
                rims[2 * i + 1] = pltpu.roll(rims[2 * i], LANES // 2, 1)
        else:
            for i, trio in enumerate(TRIOS):
                shared = tile(6 + i)
                for f, first_lane, count in trio:
                    rims[f] = pltpu.roll(shared, LANES - first_lane - count, 1)
        for i, ref in enumerate(targets):
            ref[1, at(p), :] = tau * rims[i] if i < 2 else rims[i]

    total_rows = LANES * lax.axis_size("lat")
    base = (lax.axis_index("lat") * LANES).astype(jnp.float32)
    own_row = lane.astype(jnp.float32) + base
    rim_row = jnp.where(lane < LANES // 2, lane + LANES, lane - LANES).astype(jnp.float32) + base
    spin = [
        [0.25 * tau * 0.4 * (2.0 * (r + half) * (1.0 / total_rows) - 1.0) for half in (0.5, 1.0)]
        for r in (own_row, rim_row)
    ]
    for p in range(blocks):
        water = [w_ref[t, at(p), :] for t in range(2)]
        water_north = north(*water)
        eta_north = north(eta_ref[0, at(p), :], eta_ref[1, at(p), :])
        for t in range(2):
            eta_north_ref[t, at(p), :] = eta_north[t]
            tw_north_ref[t, at(p), :] = jnp.where(water_north[t] > 0.0, tau, 0.0)
            open_u = jnp.minimum(water[t], w_ref[t, at(p, 1), :])
            open_v = jnp.minimum(water[t], water_north[t])
            du_ref[t, at(p), :] = tau * depth_of(open_u, levels)
            dv_ref[t, at(p), :] = tau * depth_of(open_v, levels)
            cu_ref[t, at(p), :] = jnp.where(open_u > 0.0, spin[t][0], 0.0)
            cv_ref[t, at(p), :] = jnp.where(open_v > 0.0, spin[t][1], 0.0)
            tw_ref[t, at(p), :] = jnp.where(water[t] > 0.0, tau, 0.0)

    flow_u, flow_v = u_ref[0, at(REACH), :], v_ref[0, at(REACH), :]
    zero = jnp.zeros((COLS, LANES), jnp.float32)

    def finish(first, last, carry, u_from, v_from):
        total_u, total_v = carry
        for p in range(first, last):
            eta = [eta_ref[t, at(p), :] for t in range(2)]
            eta_north = [eta_north_ref[t, at(p), :] for t in range(2)]
            for t in range(2):
                vbar = q_ref[t, at(p), :] + q_ref[t, at(p, 1), :]
                rise_u = eta_ref[t, at(p, 1), :] - eta[t]
                rise_v = eta_north[t] - eta[t]
                next_u = (u_from[t, at(p), :] + fu_ref[t, at(p), :]) + (
                    cu_ref[t, at(p), :] * vbar - du_ref[t, at(p), :] * rise_u
                )
                next_v = (v_from[t, at(p), :] + fv_ref[t, at(p), :]) - (
                    cv_ref[t, at(p), :] * t_ref[t, at(p), :] + dv_ref[t, at(p), :] * rise_v
                )
                u_ref[t, at(p), :] = next_u
                v_ref[t, at(p), :] = next_v
                if p == REACH and t == 0:
                    total_u, total_v = total_u + next_u, total_v + next_v
        return total_u, total_v

    def substep(first, last):
        def body(_, carry):
            for p in range(first, last):
                u = [u_ref[t, at(p), :] for t in range(2)]
                u_west = [u_ref[t, at(p, -1), :] for t in range(2)]
                v = [v_ref[t, at(p), :] for t in range(2)]
                v_south, v_north, u_north = south(*v), north(*v), north(*u)
                for t in range(2):
                    u_north_ref[t, at(p), :] = u_north[t]
                for t in range(2):
                    u_north_west = u_north_ref[t, at(p, -1), :]
                    spread = (u[t] - u_west[t]) + (v[t] - v_south[t])
                    spread_north = (u_north[t] - u_north_west) + (v_north[t] - v[t])
                    eta_ref[t, at(p), :] = eta_ref[t, at(p), :] - tw_ref[t, at(p), :] * spread
                    eta_north_ref[t, at(p), :] = (
                        eta_north_ref[t, at(p), :] - tw_north_ref[t, at(p), :] * spread_north
                    )
                    q_ref[t, at(p), :] = v[t] + v_south[t]
                    t_ref[t, at(p), :] = (u[t] + u_west[t]) + (u_north[t] + u_north_west)
            return finish(first, last, carry, u_ref, v_ref)

        return body

    names = ("u-1", "u2", "v-1", "v1", "e-1", "e0", "e1", "e2", "q1", "t-1", "t1", "U0", "U1", "V-1", "V0", "V1") + (
        "fu1", "cu1", "du1", "fv-1", "fv1", "cv-1", "cv1", "dv-1", "dv1", "tw-1", "tw2"
    )
    kept = {"u0": u_ref, "u1": u_north_ref, "v0": v_ref, "q0": q_ref, "t0": t_ref, "tw0": tw_ref, "tw1": tw_north_ref}
    kept |= {"fu0": fu_ref, "cu0": cu_ref, "du0": du_ref, "fv0": fv_ref, "cv0": cv_ref, "dv0": dv_ref}
    kept |= {name: more_ref.at[i] for i, name in enumerate(names)}

    def get(name, rows, p, t, shift=0):
        return kept[f"{name}{rows}"][t, at(p, shift), :]

    def put(name, rows, p, t, value):
        kept[f"{name}{rows}"][t, at(p), :] = value

    for p in range(PAIRS, blocks - PAIRS):
        for name, where in (
            ("fu", (1,)), ("cu", (1,)), ("du", (1,)), ("fv", (-1, 1)), ("cv", (-1, 1)), ("dv", (-1, 1)), ("tw", (-1, 2))
        ):
            here = [get(name, 0, p, t) for t in range(2)]
            for rows in where:
                for t, value in enumerate(shifted(*here, rows)):
                    put(name, rows, p, t, value)

    def pair_of_steps(first, last, carry):
        total_u, total_v = carry
        tiles = range(first, last)
        for p in tiles:
            u, v, eta = [[ref[t, at(p), :] for t in range(2)] for ref in (u_ref, v_ref, eta_ref)]
            us = {r: shifted(*u, r) for r in (0, -1, 1, 2)}
            vs = {r: shifted(*v, r) for r in (0, -1, -2, 1, 2)}
            es = {r: shifted(*eta, r) for r in (0, -1, 1, 2)}
            for t in range(2):
                for r in (-1, 1, 2):
                    put("u", r, p, t, us[r][t])
                for r in (-1, 1):
                    put("v", r, p, t, vs[r][t])
                both = {}
                for r in (-1, 0, 1, 2):
                    u_west = get("u", r, p, t, -1)
                    both[r] = us[r][t] + u_west
                    spread = (us[r][t] - u_west) + (vs[r][t] - vs[r - 1][t])
                    put("e", r, p, t, es[r][t] - get("tw", r, p, t) * spread)
                for r in (0, 1):
                    put("q", r, p, t, vs[r][t] + vs[r - 1][t])
                for r in (-1, 0, 1):
                    put("t", r, p, t, both[r] + both[r + 1])
        for p in tiles:
            for t in range(2):
                e = {r: get("e", r, p, t) for r in (-1, 0, 1, 2)}
                for r in (0, 1):
                    vbar = get("q", r, p, t) + get("q", r, p, t, 1)
                    rise = get("e", r, p, t, 1) - e[r]
                    next_u = (get("u", r, p, t) + get("fu", r, p, t)) + (
                        get("cu", r, p, t) * vbar - get("du", r, p, t) * rise
                    )
                    put("U", r, p, t, next_u)
                    if p == REACH and t == 0 and r == 0:
                        total_u = total_u + next_u
                for r in (-1, 0, 1):
                    next_v = (get("v", r, p, t) + get("fv", r, p, t)) - (
                        get("cv", r, p, t) * get("t", r, p, t) + get("dv", r, p, t) * (e[r + 1] - e[r])
                    )
                    put("V", r, p, t, next_v)
                    if p == REACH and t == 0 and r == 0:
                        total_v = total_v + next_v
        for p in tiles:
            for t in range(2):
                both = []
                for r, ref in ((0, eta_ref), (1, eta_north_ref)):
                    u, u_west = get("U", r, p, t), get("U", r, p, t, -1)
                    both.append(u + u_west)
                    spread = (u - u_west) + (get("V", r, p, t) - get("V", r - 1, p, t))
                    ref[t, at(p), :] = get("e", r, p, t) - get("tw", r, p, t) * spread
                q_ref[t, at(p), :] = get("V", 0, p, t) + get("V", -1, p, t)
                t_ref[t, at(p), :] = both[0] + both[1]
        return finish(first, last, (total_u, total_v), kept["U0"], kept["V0"])

    carry = (zero, zero)
    done = 0
    for ring in range(REACH):
        until = SUBSTEPS - COLS * (REACH - 1 - ring)
        if ring < PAIRS:
            carry = lax.fori_loop(0, until - done, substep(ring, blocks - ring), carry, unroll=until - done)
        else:
            for _ in range((until - done) // 2):
                carry = pair_of_steps(ring, blocks - ring, carry)
        done = until
    out_eta[...] = eta_ref[0, at(REACH), :]
    water = [w_ref[t, at(REACH), :] for t in range(2)]
    open_u = jnp.minimum(water[0], w_ref[0, at(REACH, 1), :])
    open_v = jnp.minimum(water[0], north(*water)[0])
    star_u = flow_u + (STEP / tau) * fu_ref[0, at(REACH), :]
    star_v = flow_v + (STEP / tau) * fv_ref[0, at(REACH), :]
    lift_u = (carry[0] / SUBSTEPS - star_u) / jnp.maximum(depth_of(open_u, levels), 0.25)
    lift_v = (carry[1] / SUBSTEPS - star_v) / jnp.maximum(depth_of(open_v, levels), 0.25)
    for k in range(levels):
        out_u[level(k), :] = su_ref[level(k), :] + jnp.where(open_u > float(k), lift_u, 0.0)
        out_v[level(k), :] = sv_ref[level(k), :] + jnp.where(open_v > float(k), lift_v, 0.0)


def call(kernel, shapes, scratch, *operands, **specs):
    return pl.pallas_call(
        kernel,
        out_shape=[jax.ShapeDtypeStruct(s, jnp.float32) for s in shapes],
        scratch_shapes=[pltpu.VMEM(s, jnp.float32) if isinstance(s, tuple) else s for s in scratch],
        compiler_params=pltpu.CompilerParams(vmem_limit_bytes=VMEM_BYTES),
        **specs,
    )(*operands)


def swap(x, axis, first, hop, wraps):
    count = lax.axis_size(axis)
    pairs = []
    for i in range(first, count, 2):
        j = i + hop
        if wraps or 0 <= j < count:
            pairs += [(i, j % count), (j % count, i)]
    return lax.ppermute(x, axis, pairs)


def local(velocity_u, velocity_v, buoyancy, wind_x, wind_y, free_surface, land_sea, bottom_level):
    levels = velocity_u.shape[0]
    flat = (levels * COLS, LANES)
    u, v, b = (a.reshape(flat) for a in (velocity_u, velocity_v, buoyancy))
    inputs = (u, v, b, land_sea, bottom_level, free_surface, wind_x, wind_y)
    edge, tile = (2 * levels + COLS, LANES), (COLS, LANES)
    whole = pltpu.VMEM(tile, jnp.int32)
    col_a, col_z, u, v, p, planes = call(
        pack_edges_kernel,
        [edge, edge, flat, flat, flat, (SLOTS * COLS, LANES)],
        [flat, whole, whole, pltpu.SemaphoreType.DMA((len(inputs),))],
        *[pltpu.with_memory_space_constraint(a, pltpu.HBM) for a in inputs],
        in_specs=[pl.BlockSpec(memory_space=pltpu.HBM)] * len(inputs),
    )
    col_z = swap(col_z, "lon", 1, 1, True)
    col_a = swap(col_a, "lon", 0, 1, True)
    rims = (3 * levels // SLOTS + 1) * COLS
    rows_a, rows_z = call(pack_rows_kernel, [(rims, LANES)] * 2, [], u, v, p, planes)
    rows_a, rows_z = call(
        pack_corners_kernel, [(rims + levels + COLS, LANES)] * 2, [], rows_a, rows_z, col_z, col_a
    )
    rows_z = swap(rows_z, "lat", 1, 1, False)
    rows_a = swap(rows_a, "lat", 0, 1, False)
    both = (2 * edge[0], LANES)
    far, x, star_u, star_v = call(
        levels_kernel, [(FAR_ROWS, LANES), (NEAR_ROWS, LANES), flat, flat], [both, both, flat, flat, flat],
        u, v, p, planes, col_z, col_a, rows_z, rows_a,
    )
    far_z = swap(far, "lon", 1, 3, True)
    far_a = swap(far, "lon", 0, 3, True)
    y = jnp.concatenate([far_z, x, far_a], 0)
    near_z = swap(y, "lon", 1, 1, True)
    near_a = swap(y, "lon", 0, 1, True)
    state = (2, (2 * REACH + 3) * COLS, LANES)
    new_u, new_v, surface = call(
        substeps_kernel, [flat, flat, (COLS, LANES)], [state] * 16 + [(27, *state)], y, near_a, near_z, x, star_u, star_v
    )
    return new_u.reshape(velocity_u.shape), new_v.reshape(velocity_v.shape), surface


def solution(mesh):
    return jax.shard_map(
        local,
        mesh=mesh,
        in_specs=(P(None, "lon", "lat"),) * 3 + (P("lon", "lat"),) * 5,
        out_specs=(P(None, "lon", "lat"), P(None, "lon", "lat"), P("lon", "lat")),
        check_vma=False,
    )
```
